32 devices in a mesh: dp: 4 (over z), expert: 8 (over y, x, core).
Axes of the slice: x: 2, y: 2, z: 4, core: 2. Of those that a mesh axis runs over, the one named last changes fastest.
Arguments:
- tokens: bfloat16 [16384, 512], P(('dp', 'expert')), may hold values from -6 to 6
- cotangent: bfloat16 [16384, 512], P(('dp', 'expert')), may hold values from -9 to 9
- routes: int32 [16384, 8], P(('dp', 'expert')), may hold values from 0 to 23, all different within a row; in each aligned block of 512 rows (0 to 511, 512 to 1023, ...) at most 336 rows name the same one
- group_batch: int32 [4], replicated, may hold values from 2 to 4, as said below
- seq_lengths: int32 [4, 4], replicated, may hold values from 0 to 2048, as said below
- gains: float32 [2, 512], replicated, may hold values from 0.3 to 3.5
- gains_first: float32 [2, 512], replicated, may hold values from -0.00048828125 to 0.00048828125
- gains_second: float32 [2, 512], replicated, may hold values from 4.6670895e-10 to 1.8668358e-09
- router_weight: float32 [512, 24], replicated, may hold values from -0.109375 to 0.109375
- router_first: float32 [512, 24], replicated, may hold values from -0.0024414062 to 0.0024414062
- router_second: float32 [512, 24], replicated, may hold values from 1.3275276e-08 to 5.3101104e-08
- keyval_weight: float32 [512, 128], P('dp'), may hold values from -0.25 to 0.25
- keyval_first: float32 [512, 128], P('dp'), may hold values from -0.0014648438 to 0.0014648438
- keyval_second: float32 [512, 128], P('dp'), may hold values from 5.1856546e-09 to 2.0742618e-08
- query_weight: float32 [24, 512, 64], P('expert'), may hold values from -0.25 to 0.25
- query_first: float32 [24, 512, 64], P('expert'), may hold values from -0.0004272461 to 0.0004272461
- query_second: float32 [24, 512, 64], P('expert'), may hold values from 3.7751566e-10 to 1.5100626e-09
- output_weight: float32 [24, 64, 512], P('expert'), may hold values from -12.613446 to 12.613446
- output_first: float32 [24, 64, 512], P('expert'), may hold values from -5.722046e-06 to 5.722046e-06
- output_second: float32 [24, 64, 512], P('expert'), may hold values from 8.2970475e-14 to 3.318819e-13
- up_weight: float32 [512, 2048], P('dp'), may hold values from -0.25 to 0.25
- up_first: float32 [512, 2048], P('dp'), may hold values from -0.00012207031 to 0.00012207031
- up_second: float32 [512, 2048], P('dp'), may hold values from 3.3188192e-11 to 1.3275277e-10
- down_weight: float32 [2048, 512], P(None, 'dp'), may hold values from -0.125 to 0.125
- down_first: float32 [2048, 512], P(None, 'dp'), may hold values from -0.00021362305 to 0.00021362305
- down_second: float32 [2048, 512], P(None, 'dp'), may hold values from 1.01638836e-10 to 4.0655534e-10
Outputs:
- layer_out: bfloat16 [16384, 512], P(('dp', 'expert'))
- tokens_grad: float32 [16384, 512], P(('dp', 'expert'))
- expert_counts: int32 [24], replicated
- grad_norm: float32 [], replicated
- new_gains: float32 [2, 512], replicated
- gains_moment: float32 [2, 512], replicated
- gains_power: float32 [2, 512], replicated
- new_router: float32 [512, 24], replicated
- router_moment: float32 [512, 24], replicated
- router_power: float32 [512, 24], replicated
- new_keyval: float32 [512, 128], P('dp')
- keyval_moment: float32 [512, 128], P('dp')
- keyval_power: float32 [512, 128], P('dp')
- new_query: float32 [24, 512, 64], P('expert')
- query_moment: float32 [24, 512, 64], P('expert')
- query_power: float32 [24, 512, 64], P('expert')
- new_output: float32 [24, 64, 512], P('expert')
- output_moment: float32 [24, 64, 512], P('expert')
- output_power: float32 [24, 64, 512], P('expert')
- new_up: float32 [512, 2048], P('dp')
- up_moment: float32 [512, 2048], P('dp')
- up_power: float32 [512, 2048], P('dp')
- new_down: float32 [2048, 512], P(None, 'dp')
- down_moment: float32 [2048, 512], P(None, 'dp')
- down_power: float32 [2048, 512], P(None, 'dp')
The draws below stay inside these ranges and needn't reach their ends.
Inputs may be any that keep to these rules, and one draw needn't show every extreme that they name: `routes`: within the rows of one device, no head expert is named by more than 336 rows. `group_batch`: each entry is 2 or 4; both values occur. `seq_lengths`: for a group with b sequences, entries 0 to b - 1 lie between 1 and 4096 div b and one of them equals 4096 div b; the entries from b on are 0.
All inputs are finite; a program needn't handle non-finite values.
Results may differ from the reference program's by a relative error of at most 0.018.
Values may be sent and summed in bfloat16 or wider, within the bound.
A program may use at most 192 MiB of HBM per device.

```python
import math
from functools import reduce
import jax
import jax.numpy as jnp
import numpy as np
from jax import lax

D = 512
FF = 2048
HEAD = 64
TOPK = 8
TOK_DEV = 512
ADAM_STEP = 10
EXPERTS = 24
GROUP_TOK = 4096
GROUPS = 4
TOKENS = 16384
SEQ_MAX = 2048
BATCH_MIN = 2
CAPACITY = 336


def batch_sizes(key):
    flips = jax.random.randint(jax.random.fold_in(key, 11), (GROUPS,), 0, 2)
    order = jax.random.permutation(jax.random.fold_in(key, 12), GROUPS)
    flips = flips.at[order[0]].set(1).at[order[1]].set(0)
    return (BATCH_MIN * (1 + flips)).astype(jnp.int32)


def draw_group_batch(key, part):
    return batch_sizes(key)


def draw_seq_lengths(key, part):
    seq_batch = batch_sizes(key)
    full_len = GROUP_TOK // seq_batch
    shortest = jnp.maximum(full_len // 4, 1)
    slot_ids = jnp.arange(2 * BATCH_MIN, dtype=jnp.int32)
    drawn = jax.random.randint(jax.random.fold_in(key, 13), (GROUPS, 2 * BATCH_MIN), shortest[:, None], full_len[:, None] + 1)
    chosen = jax.random.randint(jax.random.fold_in(key, 14), (GROUPS,), 0, seq_batch)
    drawn = jnp.where(slot_ids[None, :] == chosen[:, None], full_len[:, None], drawn)
    return jnp.where(slot_ids[None, :] < seq_batch[:, None], drawn, 0).astype(jnp.int32)


def draw_gains(key, part):
    ramp = jnp.arange(D, dtype=jnp.float32) / (D - 1)
    base = 0.6 * 3.0 ** ramp
    rough = jax.random.uniform(key, (2, D), jnp.float32, 0.8, 1.25)
    return base[None, :] * rough


def draw_cotangent(key, part):
    ramp = jnp.arange(D, dtype=jnp.float32) / (D - 1)
    values = jnp.clip(jax.random.normal(key, (TOKENS, D), jnp.float32), -5.0, 5.0) * (0.6 * 3.0 ** ramp)[None, :]
    return values.astype(jnp.bfloat16)


def draw_output_weight(key, part):
    ramp = 0.5 + jnp.arange(EXPERTS, dtype=jnp.float32) / (EXPERTS - 1)
    spread = (SEQ_MAX ** 0.5 / 16.0) ** 0.5
    base = jnp.clip(jax.random.normal(key, (EXPERTS, HEAD, D), jnp.float32), -5.0, 5.0)
    return base * spread * ramp[:, None, None]


def block_scale(key, extent, split, least, high):
    def one(dim, blocks):
        steps = jax.random.uniform(jax.random.fold_in(jax.random.fold_in(key, 6), dim), (blocks,), jnp.float32, least / len(split), high / len(split))
        return jnp.repeat(jnp.exp(steps), extent[dim] // blocks).reshape((-1,) + (1,) * (len(extent) - dim - 1))

    loudness = one(*split[0])
    for cut in split[1:]:
        loudness = loudness * one(*cut)
    return loudness


def routed_block(stream_key, own, number, rows, count, top, reach, skew):
    order = jax.random.permutation(stream_key, count)
    crowded, ordinary = shares(count, rows * top, reach, skew, True), shares(count, rows * top, reach, skew, False)
    places = jnp.arange(count)

    def named(sizes, turn):
        used = int((sizes > 0).sum())
        fixed = max(1, used // 4)
        moved = fixed + (places - fixed + turn * (used - fixed)) % max(1, count - fixed)
        return jnp.zeros((count,), jnp.int32).at[order[jnp.where(places < fixed, places, moved)]].set(jnp.asarray(sizes, jnp.int32))

    sizes = jnp.where(number % 4 == 0, named(crowded, number // 4), named(ordinary, number - number // 4 - 1))
    mixed = jax.random.permutation(jax.random.fold_in(own, 3), count)
    giver, taker = mixed[0:count // 2 * 2:2], mixed[1:count // 2 * 2:2]
    room = jnp.minimum(sizes[giver] - 1, reach - sizes[taker]) // 2
    room = jnp.where((giver == order[0]) | (taker == order[0]) | (sizes[taker] == 0), 0, jnp.maximum(room, 0))
    moved = jax.random.randint(jax.random.fold_in(own, 4), (count // 2,), 0, 1 << 20) % (room + 1)
    sizes = sizes.at[giver].add(-moved).at[taker].add(moved)
    members = jnp.searchsorted(jnp.cumsum(sizes), jnp.arange(rows * top), side="right").astype(jnp.int32)
    table = members.reshape(top, rows).T
    table = table[jax.random.permutation(jax.random.fold_in(own, 1), rows)]
    turn = jax.random.randint(jax.random.fold_in(own, 2), (rows, 1), 0, top)
    return jnp.take_along_axis(table, (jnp.arange(top)[None, :] + turn) % top, axis=1)


def shares(number_of, total, limit, lean, full):
    weights = [(1 << 20) // math.isqrt(grade ** lean) + 1 for grade in range(1, number_of + 1)]
    largest = limit if full else min(limit, max(-(-total // number_of), total * weights[0] // sum(weights)))
    least = 1 if total - largest >= number_of - 1 else 0
    given, rest = [largest] + [least] * (number_of - 1), total - largest - least * (number_of - 1)
    while rest > 0:
        candidates = [i for i in range(1, number_of) if given[i] < largest] or [i for i in range(1, number_of) if given[i] < limit]
        mass, budget = sum([weights[i] for i in candidates]), rest
        for i in candidates:
            addition = min(limit - given[i], max(1, budget * weights[i] // mass), rest)
            given[i] = given[i] + addition
            rest = rest - addition
    return np.array(given)


def centred(rng, extent, scale, reach, shards=(), held_as=jnp.bfloat16):
    factor_of = block_scale(rng, extent, shards, -0.22, 0.18) if shards else 1.0
    entries = jax.random.normal(rng, extent, jnp.float32) * scale * factor_of
    return jnp.minimum(jnp.maximum(entries, -reach), reach).astype(held_as)


def setup_inputs(seed: int = 0) -> dict:
    streams_of = jax.random.split(jax.random.key(seed), 27)
    tokens = centred(streams_of[0], (TOKENS, D), 1.0, 6.0, ((0, 32),))
    cotangent = draw_cotangent(jax.random.fold_in(streams_of[26], 71), 0)
    routes_keys = jax.random.split(jax.random.fold_in(streams_of[2], 1), TOKENS // TOK_DEV)
    routes_turns = jax.random.permutation(jax.random.fold_in(streams_of[2], 3), TOKENS // TOK_DEV)
    routes = jax.vmap(lambda own, number: routed_block(jax.random.fold_in(streams_of[2], 2), own, number, TOK_DEV, EXPERTS, TOPK, CAPACITY, 1))(routes_keys, routes_turns).reshape((TOKENS, TOPK))
    group_batch = draw_group_batch(jax.random.fold_in(streams_of[26], 71), 0)
    seq_lengths = draw_seq_lengths(jax.random.fold_in(streams_of[26], 71), 0)
    gains = draw_gains(jax.random.fold_in(streams_of[26], 71), 0)
    gains_first = centred(streams_of[6], (2, D), (0.1665 / (0.65 * D * FF + 1.8 * EXPERTS * D * HEAD + 59 * D * HEAD + 64 * D * EXPERTS + 8 * D) ** 0.5), 0.00048828125, (), jnp.float32)
    gains_second = jnp.clip(jnp.exp(jax.random.uniform(streams_of[7], (2, D), jnp.float32, math.log(4.667089492649268e-10), math.log(1.866835797059707e-09))), 4.667089492649268e-10, 1.866835797059707e-09)
    router_weight = centred(streams_of[8], (D, EXPERTS), (6 * D) ** -0.5, 0.109375, (), jnp.float32)
    router_first = centred(streams_of[9], (D, EXPERTS), (0.888 / (0.65 * D * FF + 1.8 * EXPERTS * D * HEAD + 59 * D * HEAD + 64 * D * EXPERTS + 8 * D) ** 0.5), 0.0024414062, (), jnp.float32)
    router_second = jnp.clip(jnp.exp(jax.random.uniform(streams_of[10], (D, EXPERTS), jnp.float32, math.log(1.3275275989599322e-08), math.log(5.310110395839729e-08))), 1.3275275989599322e-08, 5.310110395839729e-08)
    keyval_weight = centred(streams_of[11], (D, 2 * HEAD), D ** -0.5, 0.25, ((0, 4),), jnp.float32)
    keyval_first = centred(streams_of[12], (D, 2 * HEAD), (0.555 / (0.65 * D * FF + 1.8 * EXPERTS * D * HEAD + 59 * D * HEAD + 64 * D * EXPERTS + 8 * D) ** 0.5), 0.0014648438, ((0, 4),), jnp.float32)
    keyval_second = jnp.clip(jnp.exp(math.log(2.074261828965973e-08) - 1.3862944 * jax.random.uniform(streams_of[13], (D, 2 * HEAD), jnp.float32) ** block_scale(streams_of[13], (D, 2 * HEAD), ((0, 4),), -0.2, 0.2)), 5.185654572414933e-09, 2.074261828965973e-08)
    query_weight = centred(streams_of[14], (EXPERTS, D, HEAD), D ** -0.5, 0.25, ((0, 8),), jnp.float32)
    query_first = centred(streams_of[15], (EXPERTS, D, HEAD), (0.15 / (0.65 * D * FF + 1.8 * EXPERTS * D * HEAD + 59 * D * HEAD + 64 * D * EXPERTS + 8 * D) ** 0.5), 0.0004272461, ((0, 8),), jnp.float32)
    query_second = jnp.clip(jnp.exp(math.log(1.5100626304942466e-09) - 1.3862944 * jax.random.uniform(streams_of[16], (EXPERTS, D, HEAD), jnp.float32) ** block_scale(streams_of[16], (EXPERTS, D, HEAD), ((0, 8),), -0.2, 0.2)), 3.7751565762356165e-10, 1.5100626304942466e-09)
    output_weight = draw_output_weight(jax.random.fold_in(streams_of[26], 71), 0)
    output_first = centred(streams_of[18], (EXPERTS, HEAD, D), (0.00222 / (0.65 * D * FF + 1.8 * EXPERTS * D * HEAD + 59 * D * HEAD + 64 * D * EXPERTS + 8 * D) ** 0.5), 5.7220458984375e-06, ((0, 8),), jnp.float32)
    output_second = jnp.clip(jnp.exp(math.log(3.318819015180746e-13) - 1.3862944 * jax.random.uniform(streams_of[19], (EXPERTS, HEAD, D), jnp.float32) ** block_scale(streams_of[19], (EXPERTS, HEAD, D), ((0, 8),), -0.2, 0.2)), 8.297047537951865e-14, 3.318819015180746e-13)
    up_weight = centred(streams_of[20], (D, FF), D ** -0.5, 0.25, ((0, 4),), jnp.float32)
    up_first = centred(streams_of[21], (D, FF), (0.0444 / (0.65 * D * FF + 1.8 * EXPERTS * D * HEAD + 59 * D * HEAD + 64 * D * EXPERTS + 8 * D) ** 0.5), 0.00012207031, ((0, 4),), jnp.float32)
    up_second = jnp.clip(jnp.exp(math.log(1.3275276711244288e-10) - 1.3862944 * jax.random.uniform(streams_of[22], (D, FF), jnp.float32) ** block_scale(streams_of[22], (D, FF), ((0, 4),), -0.2, 0.2)), 3.318819177811072e-11, 1.3275276711244288e-10)
    down_weight = centred(streams_of[23], (FF, D), FF ** -0.5, 0.125, ((1, 4),), jnp.float32)
    down_first = centred(streams_of[24], (FF, D), (0.0777 / (0.65 * D * FF + 1.8 * EXPERTS * D * HEAD + 59 * D * HEAD + 64 * D * EXPERTS + 8 * D) ** 0.5), 0.00021362305, ((1, 4),), jnp.float32)
    down_second = jnp.clip(jnp.exp(math.log(4.0655534494504764e-10) - 1.3862944 * jax.random.uniform(streams_of[25], (FF, D), jnp.float32) ** block_scale(streams_of[25], (FF, D), ((1, 4),), -0.2, 0.2)), 1.0163883623626191e-10, 4.0655534494504764e-10)
    return dict(tokens=tokens, cotangent=cotangent, routes=routes, group_batch=group_batch, seq_lengths=seq_lengths, gains=gains, gains_first=gains_first, gains_second=gains_second, router_weight=router_weight, router_first=router_first, router_second=router_second, keyval_weight=keyval_weight, keyval_first=keyval_first, keyval_second=keyval_second, query_weight=query_weight, query_first=query_first, query_second=query_second, output_weight=output_weight, output_first=output_first, output_second=output_second, up_weight=up_weight, up_first=up_first, up_second=up_second, down_weight=down_weight, down_first=down_first, down_second=down_second)


NORM_EPS = 1e-06
BETA_FIRST = 0.9
BETA_SECOND = 0.999
ADAM_EPS = 1e-08
CLIP_LIMIT = 1.0
MASKED = -1e+30
HIGHEST = lax.Precision.HIGHEST

@jax.custom_vjp
def low(v):
    return lax.optimization_barrier(v.astype(jnp.bfloat16)).astype(jnp.float32)

@jax.custom_vjp
def low_back(v):
    return v

def low_keep(v):
    return (low(v), None)

def low_pass(kept, grad):
    return (grad,)

def back_keep(v):
    return (v, None)

def back_low(kept, grad):
    return (low(grad),)
low.defvjp(low_keep, low_pass)
low_back.defvjp(back_keep, back_low)

def rms_norm(values, gain_vec):
    inverse = lax.rsqrt(lax.optimization_barrier(jnp.mean(values * values, axis=-1, keepdims=True)) + NORM_EPS)
    return values * inverse * gain_vec

def matmul(left, right):
    return jnp.dot(left, right, preferred_element_type=jnp.float32, precision=HIGHEST)

def adam_update(weight, gradient, first_moment, second, clip_scale, step_rate, decay_rate):
    step_grad = gradient * clip_scale
    new_first = BETA_FIRST * first_moment + (1.0 - BETA_FIRST) * step_grad
    new_second = BETA_SECOND * second + (1.0 - BETA_SECOND) * step_grad * step_grad
    first_hat = new_first / (1.0 - BETA_FIRST ** ADAM_STEP)
    second_hat = new_second / (1.0 - BETA_SECOND ** ADAM_STEP)
    new_weight = weight - step_rate * (first_hat / (jnp.sqrt(second_hat) + ADAM_EPS) + decay_rate * weight)
    return (new_weight, new_first, new_second)

def reference(tokens, cotangent, routes, group_batch, seq_lengths, gains, gains_first, gains_second, router_weight, router_first, router_second, keyval_weight, keyval_first, keyval_second, query_weight, query_first, query_second, output_weight, output_first, output_second, up_weight, up_first, up_second, down_weight, down_first, down_second):
    block_rows = min(64, GROUP_TOK)
    block_count = GROUP_TOK // block_rows
    key_rows = jnp.arange(GROUP_TOK, dtype=jnp.int32)

    def forward(tokens_wide, gain_pair, router_full, keyval_full, query_full, output_full, up_full, down_full):
        normed = low(rms_norm(tokens_wide, gain_pair[0]))
        logits = low_back(matmul(normed, low(router_full)))
        gate_probs = jax.nn.softmax(jnp.take_along_axis(logits, routes, axis=1), axis=1)
        keyval = low_back(low(matmul(normed, low(keyval_full))))
        query_low = low(query_full)
        output_low = low(output_full)

        def one_group(inputs):
            normed_group, routes_group, keyval_group, seq_batch, lengths = inputs
            keys_all = keyval_group[:, :HEAD]
            values_all = keyval_group[:, HEAD:]
            key_seq = key_rows % seq_batch
            key_pos = key_rows // seq_batch

            def one_block(pieces):
                normed_block, routes_block, first_row = pieces
                query_rows = first_row + jnp.arange(block_rows, dtype=jnp.int32)
                query_seq = query_rows % seq_batch
                query_pos = query_rows // seq_batch
                row_limit = lengths[query_seq]
                visible = (key_seq[None, :] == query_seq[:, None]) & (key_pos[None, :] <= query_pos[:, None]) & (key_pos[None, :] < row_limit[:, None])
                slot_in = low_back(jnp.broadcast_to(normed_block[:, None, :], (block_rows, TOPK, D)))
                queries = low_back(low(jnp.einsum('tkd,tkdh->tkh', slot_in, query_low[routes_block], precision=HIGHEST)))
                scores = low_back(jnp.einsum('tkh,uh->tku', queries, keys_all, precision=HIGHEST) * 0.125)
                scores = jnp.where(visible[:, None, :], scores, MASKED)
                prob_rows = low(jax.nn.softmax(scores, axis=2))
                attended = low_back(low(jnp.einsum('tku,uh->tkh', prob_rows, values_all, precision=HIGHEST)))
                return low_back(low(jnp.einsum('tkh,tkhd->tkd', attended, output_low[routes_block], precision=HIGHEST)))
            starts = jnp.arange(block_count, dtype=jnp.int32) * block_rows
            branch = lax.map(jax.checkpoint(one_block), (normed_group.reshape(block_count, block_rows, D), routes_group.reshape(block_count, block_rows, TOPK), starts))
            return branch.reshape(GROUP_TOK, TOPK, D)
        branch = lax.map(one_group, (normed.reshape(GROUPS, GROUP_TOK, D), routes.reshape(GROUPS, GROUP_TOK, TOPK), keyval.reshape(GROUPS, GROUP_TOK, 2 * HEAD), group_batch, seq_lengths))
        mixed_rows = tokens_wide + jnp.einsum('tk,tkd->td', gate_probs, branch.reshape(TOKENS, TOPK, D), precision=HIGHEST)
        normed_ffn = low(rms_norm(mixed_rows, gain_pair[1]))
        up_proj = low_back(matmul(normed_ffn, low(up_full)))
        hidden = low(jax.nn.gelu(up_proj))
        return mixed_rows + matmul(hidden, low(down_full))
    tokens_wide = tokens.astype(jnp.float32)
    layer_wide, pullback = jax.vjp(forward, tokens_wide, gains, router_weight, keyval_weight, query_weight, output_weight, up_weight, down_weight)
    grads = pullback(cotangent.astype(jnp.float32))
    tokens_grad = grads[0]
    total = reduce(lambda acc, item: acc + jnp.sum(item * item), grads[1:], jnp.zeros((), jnp.float32))
    grad_norm = jnp.sqrt(total)
    clip_scale = CLIP_LIMIT / jnp.maximum(grad_norm, CLIP_LIMIT)
    row_ids = jnp.arange(TOKENS, dtype=jnp.int32)
    group_of = row_ids // GROUP_TOK
    inside = row_ids % GROUP_TOK
    batch_rows = group_batch[group_of]
    seq_rows = inside % batch_rows
    pos_rows = inside // batch_rows
    limit_rows = seq_lengths[group_of, seq_rows]
    live_rows = (pos_rows < limit_rows).astype(jnp.int32)
    onehot = (routes[:, :, None] == jnp.arange(EXPERTS, dtype=jnp.int32)[None, None, :]).astype(jnp.int32)
    expert_counts = lax.optimization_barrier(jnp.sum(onehot * live_rows[:, None, None], axis=(0, 1))).astype(jnp.int32)
    gains_out = adam_update(gains, grads[1], gains_first, gains_second, clip_scale, 0.7, 0.0)
    router_out = adam_update(router_weight, grads[2], router_first, router_second, clip_scale, 0.03, 0.1)
    keyval_out = adam_update(keyval_weight, grads[3], keyval_first, keyval_second, clip_scale, 0.06, 0.1)
    query_out = adam_update(query_weight, grads[4], query_first, query_second, clip_scale, 0.06, 0.1)
    output_out = adam_update(output_weight, grads[5], output_first, output_second, clip_scale, 2.0, 0.1)
    up_out = adam_update(up_weight, grads[6], up_first, up_second, clip_scale, 0.06, 0.1)
    down_out = adam_update(down_weight, grads[7], down_first, down_second, clip_scale, 0.03, 0.1)
    return (layer_wide.astype(jnp.bfloat16), tokens_grad, expert_counts, grad_norm, gains_out[0], gains_out[1], gains_out[2], router_out[0], router_out[1], router_out[2], keyval_out[0], keyval_out[1], keyval_out[2], query_out[0], query_out[1], query_out[2], output_out[0], output_out[1], output_out[2], up_out[0], up_out[1], up_out[2], down_out[0], down_out[1], down_out[2])
```

```python
import math

import jax
import jax.numpy as jnp
from jax import lax
from jax.experimental import pallas as pl
from jax.experimental.pallas import tpu as pltpu
from jax.sharding import PartitionSpec as P

ADAM_STEP = 10
NORM_EPS = 1e-06
BETA_FIRST = 0.9
BETA_SECOND = 0.999
ADAM_EPS = 1e-08
CLIP_LIMIT = 1.0
MASKED = -1e30
LOG2E = math.log2(math.e)
LN2 = math.log(2.0)
MESH = pl.DeviceIdType.MESH
BF = jnp.bfloat16
F32 = jnp.float32

T = 512
D = 512
FF = 2048
HD = 64
K8 = 8
NE = 24
PL = 8
LE = NE // PL
ER = LE * HD
HB = FF // 2
R = 512
NR = K8 * 128 // R


def mm(a, b):
    return jnp.dot(a, b, preferred_element_type=F32)


def mm_nt(a, b):
    return lax.dot_general(a, b, (((1,), (1,)), ((), ())), preferred_element_type=F32)


def mm_tn(a, b):
    return lax.dot_general(a, b, (((0,), (0,)), ((), ())), preferred_element_type=F32)


def expert_at(place):
    slot = place // LE
    return LE * (2 * (slot % 4) + slot // 4) + place % LE


def piece_rows(dp):
    return -(-ER // (dp * 16)) * 16


def scratch_list(dp):
    shard = D // dp
    pr = piece_rows(dp)
    return dict(
        wkvf=((D, 2 * HD), BF),
        w2=((2, D, FF), BF),
        eq=((NE * HD, D), BF),
        eo=((NE * HD, D), BF),
        kvb=((PL, 2, 256, 128), BF),
        tokx=((256, D), BF),
        cotx=((256, D), BF),
        rtx=((8, 256), jnp.int32),
        tokd=((T, D), BF),
        cotd=((T, D), BF),
        cott=((D, T), BF),
        rtd=((8, T), jnp.int32),
        nd=((T, D), BF),
        gate=((8, T), F32),
        dgate=((8, T), F32),
        big=((PL * 256, T), F32),
        at=((NE * HD, T), BF),
        qx=((4, 128, 1024), BF),
        dox=((4, 128, 1024), BF),
        att=((4, HD, 1024), F32),
        linv=((4, 8, 1024), F32),
        kx=((2, 8, 256, 128), BF),
        vx=((2, 8, 256, 128), BF),
        kt=((2, 8, HD, 256), BF),
        vt=((2, 8, HD + 16, 256), BF),
        pst=((2, 9, 256, 1024), BF),
        dkv=((2, 8, 256, 128), F32),
        mixed=((T, D), F32),
        ffn=((T, D), BF),
        ffnt=((D, T), BF),
        dmb=((T, D), BF),
        acc1=((T, D), F32),
        acc2=((T, D), F32),
        gf=((2, D, FF), BF),
        rf1=((2, D, HB), BF),
        rf2=((dp - 1, 2, shard, HB), BF),
        rs=((2, shard, HB), BF),
        rf3=((3, 2, shard, HB // 4), BF),
        f2=((2, shard, FF), BF),
        go=((NE * HD, D), BF),
        rq1=((NE * HD // 2, D), BF),
        ro1=((NE * HD // 2, D), BF),
        rq2=((3, ER, D), BF),
        ro2=((3, ER, D), BF),
        xq=((dp * pr, D), BF),
        xo=((dp * pr, D), BF),
        rq3=((dp - 1, pr, D), BF),
        ro3=((dp - 1, pr, D), BF),
        fq=((dp * pr, D), BF),
        fo=((dp * pr, D), BF),
        rk1=((4, 2, 256, 128), BF),
        rk2=((3, 2, 256, 128), BF),
        dkvd=((T, 128), BF),
        tbf=((128, 640), F32),
        tb=((128, 640), BF),
        rt1=((64, 640), BF),
        tsm=((64, 640), BF),
        rt2=((3, 16, 640), BF),
        rt3=((dp, 16, 640), BF),
        tf=((128, 640), BF),
        cnt=((32, 128), F32),
        mz=((dp, 32, 128), F32),
        mq=((PL, 32, 128), F32),
        layx=((256, D), BF),
        layr=((256, D), BF),
        tgx=((256, D), BF),
        tgr=((256, D), BF),
        gain=((8, D), F32),
        layo=((T, D), BF),
        osem=(8,),
        ssem=None,
        rsem=None,
    )


def copies_of(dp):
    return 64 + 8 * dp + 8


def layer_kernel(dp, *refs):
    shard = D // dp
    pr = piece_rows(dp)
    (tok, cot, rt, wkv, w2i, eqi, eoi, wrt, gains, info) = refs[:10]
    (lay, tg, msgo, f2o, fqo, foo, tbo) = refs[10:17]
    names = list(scratch_list(dp))
    s = type("Scratch", (), dict(zip(names, refs[17:])))

    z = lax.axis_index("dp")
    e = lax.axis_index("expert")
    c = e % 2
    q = e // 2
    qs = [q, q + 1 - 2 * (q % 2), (q + 2) % 4, 3 - q]
    sib = (z, e + 1 - 2 * c)
    chips = [None] + [(z, 2 * qs[m] + c) for m in (1, 2, 3)]
    swap = (z, 7 - e)
    zp = [None] + [((z + i) % dp, e) for i in range(1, dp)]
    zfrom = [None] + [(z + dp - i) % dp for i in range(1, dp)]
    slot = c * 4 + q
    plane = [sib] + [(z, (e + i) % PL) for i in range(1, PL)]

    count = [0]
    sends = []

    def rcopy(src, dst, peer):
        k = count[0]
        count[0] += 1
        d = pltpu.make_async_remote_copy(
            src_ref=src,
            dst_ref=dst,
            send_sem=s.ssem.at[k],
            recv_sem=s.rsem.at[k],
            device_id=peer,
            device_id_type=MESH,
        )
        d.start()
        sends.append(d)
        return (k, peer, d)

    def sent(handle):
        sends[:] = [d for d in sends if d is not handle[2]]
        handle[2].wait_send()

    def rwait(handle, dst):
        k, peer, _ = handle
        pltpu.make_async_remote_copy(
            src_ref=dst,
            dst_ref=dst,
            send_sem=s.ssem.at[k],
            recv_sem=s.rsem.at[k],
            device_id=peer,
            device_id_type=MESH,
        ).wait_recv()

    def lcopy(src, dst, k):
        d = pltpu.make_async_copy(src, dst, s.osem.at[k])
        d.start()
        return d

    bar = pltpu.get_barrier_semaphore()
    for peer in plane[1:] + zp[1:]:
        pl.semaphore_signal(bar, inc=1, device_id=peer, device_id_type=MESH)
    pl.semaphore_wait(bar, PL - 1 + dp - 1)

    def zrows(ref, i, n):
        return ref.at[pl.ds(pl.multiple_of(i * n, n), n)]

    h_wkv = [None] + [rcopy(wkv, zrows(s.wkvf, z, shard), zp[i]) for i in range(1, dp)]
    h_tok = rcopy(tok.at[pl.ds(256, 256)], s.tokx, swap)
    h_rt = rcopy(rt.at[:, pl.ds(256, 256)], s.rtx, swap)
    lo = pl.multiple_of(c * HB, HB)
    hi = pl.multiple_of((1 - c) * HB, HB)
    h_w2 = [None] + [
        rcopy(
            w2i.at[:, :, pl.ds(lo, HB)],
            s.w2.at[:, pl.ds(pl.multiple_of(z * shard, shard), shard), pl.ds(lo, HB)],
            zp[i],
        )
        for i in range(1, dp)
    ]
    h_eq = [None] + [rcopy(eqi, zrows(s.eq, slot, ER), chips[m]) for m in (1, 2, 3)]

    s.wkvf[pl.ds(pl.multiple_of(z * shard, shard), shard), :] = wkv[...]
    l_eq = lcopy(eqi, zrows(s.eq, slot, ER), 0)
    l_eo = lcopy(eoi, zrows(s.eo, slot, ER), 1)
    l_w2 = lcopy(
        w2i.at[:, :, pl.ds(lo, HB)],
        s.w2.at[:, pl.ds(pl.multiple_of(z * shard, shard), shard), pl.ds(lo, HB)],
        2,
    )

    ri = lax.broadcasted_iota(jnp.int32, (256, 256), 0)
    ci = lax.broadcasted_iota(jnp.int32, (256, 256), 1)
    split = jnp.where(ci == 2 * (ri % 128) + ri // 128, 1.0, 0.0).astype(BF)
    join = jnp.where(ri == 2 * (ci % 128) + ci // 128, 1.0, 0.0).astype(BF)
    g0 = gains[0:1, :]
    g1 = gains[1:2, :]

    def rms(x):
        inv = lax.rsqrt(jnp.mean(x * x, axis=-1, keepdims=True) + NORM_EPS)
        return x * inv, inv

    nat0 = mm(split, tok[0:256, :])
    nat1 = mm(split, tok[256:512, :])
    s.tokd[0:256, :] = nat0.astype(BF)
    n0 = (rms(nat0)[0] * g0).astype(BF)
    n1 = (rms(nat1)[0] * g0).astype(BF)
    s.nd[0:256, :] = n0
    cot0 = mm(split, cot[0:256, :])
    s.cotd[0:256, :] = cot0.astype(BF)

    for i in range(1, dp):
        rwait(h_wkv[i], zrows(s.wkvf, zfrom[i], shard))
    kv0 = mm(n0, s.wkvf[...]).astype(BF)
    kv1 = mm(n1, s.wkvf[...]).astype(BF)
    for p in range(2):
        s.kvb[slot, p, 0:128, :] = kv0[p * 128 : (p + 1) * 128]
        s.kvb[slot, p, 128:256, :] = kv1[p * 128 : (p + 1) * 128]
    h_kv = [None] + [rcopy(s.kvb.at[slot], s.kvb.at[slot], chips[m]) for m in (1, 2, 3)]
    h_cot = rcopy(cot.at[pl.ds(256, 256)], s.cotx, swap)
    h_eo = [None] + [rcopy(eoi, zrows(s.eo, slot, ER), chips[m]) for m in (1, 2, 3)]

    rwait(h_tok, s.tokx)
    rwait(h_rt, s.rtx)
    sw = mm(split, s.tokx[...])
    s.tokd[256:512, :] = sw.astype(BF)
    s.nd[256:512, :] = (rms(sw)[0] * g0).astype(BF)
    s.rtd[:, 0:256] = rt[:, 0:256]
    s.rtd[:, 256:512] = s.rtx[...]

    bm1 = info[0] - 1
    is2 = (4 - info[0]) // 2

    def seq_pos(r):
        return r & bm1, (r >> 1) * is2 + (r >> 2) * (1 - is2)

    def limit_of(index):
        out = jnp.zeros(index.shape, jnp.int32)
        for i in range(4):
            out = jnp.where(index == i, info[1 + i], out)
        return out

    block = [2 * e, 15 - 2 * e]
    lanes128 = lax.broadcasted_iota(jnp.int32, (16, 128), 1)
    row16 = lax.broadcasted_iota(jnp.int32, (16, 128), 0)
    row32 = lax.broadcasted_iota(jnp.int32, (32, 128), 0)

    logits = mm_nt(wrt[...], s.nd[...])
    row_e = lax.broadcasted_iota(jnp.int32, (32, T), 0)
    chosen = jnp.concatenate(
        [
            jnp.sum(jnp.where(row_e == s.rtd[k : k + 1, :], logits, 0.0), axis=0, keepdims=True)
            for k in range(K8)
        ],
        axis=0,
    )
    ex = jnp.exp(chosen - jnp.max(chosen, axis=0, keepdims=True))
    s.gate[...] = ex / jnp.sum(ex, axis=0, keepdims=True)

    counts = jnp.zeros((32, 128), F32)
    for g in range(4):
        b, p = g // 2, g % 2
        row = 2 * (block[b] * 128 + lanes128) + p
        seq, pos = seq_pos(row)
        live = (pos < limit_of(seq))[0:1, :].astype(F32)
        for k in range(K8):
            counts = counts + jnp.where(
                row32 == s.rtd[k : k + 1, g * 128 : (g + 1) * 128], live, 0.0
            )
        feat = jnp.where(seq == row16, 1.0, 0.0).astype(BF)
        s.qx[g, 64:80, :] = jnp.concatenate([feat] * K8, axis=1)
        s.qx[g, 80:128, :] = jnp.zeros((48, 1024), BF)
    s.cnt[...] = jnp.broadcast_to(jnp.sum(counts, axis=1, keepdims=True), (32, 128))

    for m in (1, 2, 3):
        rwait(h_eq[m], zrows(s.eq, c * 4 + qs[m], ER))
    half = NE * HD // 2
    l_eq.wait()
    h_eqs = rcopy(zrows(s.eq, c, half), zrows(s.eq, c, half), sib)
    for m in (1, 2, 3):
        rwait(h_kv[m], s.kvb.at[c * 4 + qs[m]])
    h_kvs = rcopy(s.kvb.at[pl.ds(c * 4, 4)], s.kvb.at[pl.ds(c * 4, 4)], sib)
    rwait(h_eqs, zrows(s.eq, 1 - c, half))

    def query_rows(i, _):
        rows = pl.ds(pl.multiple_of(i * 256, 256), 256)
        s.big[rows, :] = mm_nt(s.eq[rows, :], s.nd[...])
        return 0

    lax.fori_loop(0, NE * HD // 256, query_rows, 0)

    def pick(g, k):
        lanes = pl.ds(pl.multiple_of(g * 128, 128), 128)
        rk = s.rtd[k : k + 1, lanes]
        acc = jnp.zeros((HD, 128), F32)
        for place in range(NE):
            acc = jnp.where(rk == expert_at(place), s.big[place * HD : (place + 1) * HD, lanes], acc)
        return acc

    def choose(g, _):
        for k in range(K8):
            s.qx[g, 0:64, k * 128 : (k + 1) * 128] = (pick(g, k) * (0.125 * LOG2E)).astype(BF)
        return 0

    lax.fori_loop(0, 4, choose, 0)

    rwait(h_kvs, s.kvb.at[pl.ds((1 - c) * 4, 4)])
    krow = lax.broadcasted_iota(jnp.int32, (256, 128), 0)
    klane = lax.broadcasted_iota(jnp.int32, (256, 128), 1)
    for t in range(8):
        for p in range(2):
            kv = s.kvb[(t % 2) * 4 + t // 2, p].astype(F32)
            seq, pos = seq_pos(2 * (t * 256 + krow) + p)
            col = klane - 64
            shown = (seq == col) & (pos < limit_of(col))
            feat = jnp.where(shown | (col > 3), 0.0, MASKED)
            s.kx[p, t] = jnp.where(col < 0, kv, feat).astype(BF)
            s.vx[p, t] = jnp.where(col >= 0, kv, jnp.where(klane < 2, 1.0, 0.0)).astype(BF)
            kvt = kv.T
            s.kt[p, t] = kvt[0:64].astype(BF)
            s.vt[p, t, 0:64, :] = kvt[64:128].astype(BF)
            s.vt[p, t, 64:80, :] = jnp.ones((16, 256), BF)

    tiles = [e + 1, 8 - e]
    base = [0, e + 1]
    for g in range(4):
        b, p = g // 2, g % 2
        nt, first = tiles[b], base[b]
        visible = (
            lax.broadcasted_iota(jnp.int32, (256, 128), 0)
            <= lax.broadcasted_iota(jnp.int32, (256, 128), 1) + 128 * b
        )
        visible = jnp.concatenate([visible] * (R // 128), axis=1)
        for rc in range(NR):
            ls = slice(rc * R, (rc + 1) * R)

            def scores(t, peak):
                sc = mm(s.kx[p, t], s.qx[g, :, ls])
                s.big[pl.ds(pl.multiple_of(t * 256, 256), 256), :] = sc
                return jnp.maximum(peak, jnp.max(sc.reshape(32, 8, R), axis=0))

            peak = lax.fori_loop(0, nt - 1, scores, jnp.full((8, R), MASKED, F32))
            sc = jnp.where(visible, mm(s.kx[p, nt - 1], s.qx[g, :, ls]), MASKED)
            s.big[pl.ds(pl.multiple_of((nt - 1) * 256, 256), 256), :] = sc
            peak = jnp.maximum(peak, jnp.max(sc.reshape(32, 8, R), axis=0))
            peak = jnp.max(peak, axis=0, keepdims=True)

            def values(t, acc):
                pb = jnp.exp2(s.big[pl.ds(pl.multiple_of(t * 256, 256), 256), :] - peak).astype(BF)
                s.pst[p, first + t, :, ls] = pb
                return acc + mm(s.vt[p, t], pb)

            acc = lax.fori_loop(0, nt, values, jnp.zeros((HD + 16, R), F32))
            inv = 1.0 / acc[64:72]
            s.linv[g, :, ls] = inv
            s.att[g, :, ls] = acc[0:64] * inv[0:1]

    for m in (1, 2, 3):
        rwait(h_eo[m], zrows(s.eo, c * 4 + qs[m], ER))
    l_eo.wait()
    h_eos = rcopy(zrows(s.eo, c, half), zrows(s.eo, c, half), sib)
    for i in range(1, dp):
        rwait(
            h_w2[i],
            s.w2.at[:, pl.ds(pl.multiple_of(zfrom[i] * shard, shard), shard), pl.ds(lo, HB)],
        )
    l_w2.wait()
    h_w2s = rcopy(s.w2.at[:, :, pl.ds(lo, HB)], s.w2.at[:, :, pl.ds(lo, HB)], sib)

    def spread(dst, src, scale):
        def one(g, _):
            lanes = pl.ds(pl.multiple_of(g * 128, 128), 128)
            for k in range(K8):
                part = src[g, :, k * 128 : (k + 1) * 128]
                if scale is not None:
                    part = part * scale[k : k + 1, lanes]
                else:
                    part = part * 0.125
                s.acc1[k * HD : (k + 1) * HD, 0:128] = part
            for place in range(NE):
                acc = jnp.zeros((HD, 128), F32)
                for k in range(K8):
                    acc = jnp.where(
                        s.rtd[k : k + 1, lanes] == expert_at(place),
                        s.acc1[k * HD : (k + 1) * HD, 0:128],
                        acc,
                    )
                dst[place * HD : (place + 1) * HD, lanes] = acc.astype(BF)
            return 0

        lax.fori_loop(0, 4, one, 0)

    spread(s.at, s.att, s.gate)
    rwait(h_eos, zrows(s.eo, 1 - c, half))
    s.acc1[...] = s.tokd[...].astype(F32)

    def mix(i, _):
        rows = pl.ds(pl.multiple_of(i * 256, 256), 256)
        s.acc1[...] += mm_tn(s.at[rows, :], s.eo[rows, :])
        return 0

    lax.fori_loop(0, NE * HD // 256, mix, 0)
    mixed = s.acc1[...]
    s.mixed[...] = mixed
    ffn = rms(mixed)[0] * g1
    s.ffn[...] = ffn.astype(BF)
    s.ffnt[...] = ffn.T.astype(BF)
    rwait(h_cot, s.cotx)
    cot1 = mm(split, s.cotx[...])
    s.cotd[256:512, :] = cot1.astype(BF)
    s.cott[:, 0:256] = cot0.T.astype(BF)
    s.cott[:, 256:512] = cot1.T.astype(BF)
    s.acc2[...] = jnp.zeros((T, D), F32)
    rwait(h_w2s, s.w2.at[:, :, pl.ds(hi, HB)])

    FT = 256

    def feed(i, _):
        cols = pl.ds(pl.multiple_of(i * FT, FT), FT)
        up = mm(s.ffn[...], s.w2[0, :, cols])
        sq = up * up
        th = jnp.tanh(0.79788456 * up * (1.0 + 0.044715 * sq))
        hid = (0.5 * up * (1.0 + th)).astype(BF)
        slope = 0.5 * (1.0 + th) + 0.5 * up * (1.0 - th * th) * (
            0.79788456 * (1.0 + 3 * 0.044715 * sq)
        )
        s.acc1[...] += mm_nt(hid, s.w2[1, :, cols])
        dup = (mm(s.cotd[...], s.w2[1, :, cols]) * slope).astype(BF)
        s.gf[0, :, cols] = mm(s.ffnt[...], dup).astype(BF)
        s.gf[1, :, cols] = mm(s.cott[...], hid).astype(BF)
        s.acc2[...] += mm_nt(dup, s.w2[0, :, cols])
        return 0

    lax.fori_loop(0, FF // FT, feed, 0)
    h_f1 = rcopy(s.gf.at[:, :, pl.ds(hi, HB)], s.rf1, sib)

    out = s.acc1[...].astype(BF)
    s.layx[...] = mm(join, out[256:512]).astype(BF)
    h_lay = rcopy(s.layx, s.layr, swap)
    s.layo[0:256, :] = mm(join, out[0:256]).astype(BF)

    def rms_back(dn, gain, unit, inv):
        a = dn * gain
        return inv * (a - unit * jnp.mean(a * unit, axis=-1, keepdims=True)), jnp.sum(
            dn * unit, axis=0, keepdims=True
        )

    unit1, inv1 = rms(s.mixed[...])
    back, gain1 = rms_back(s.acc2[...], g1, unit1, inv1)
    s.gain[1:2, :] = gain1
    dmix = s.cotd[...].astype(F32) + back
    s.mixed[...] = dmix
    s.dmb[...] = dmix.astype(BF)

    def out_rows(i, _):
        rows = pl.ds(pl.multiple_of(i * 256, 256), 256)
        s.big[rows, :] = mm_nt(s.eo[rows, :], s.dmb[...])
        s.go[rows, :] = mm(s.at[rows, :], s.dmb[...]).astype(BF)
        return 0

    lax.fori_loop(0, NE * HD // 256, out_rows, 0)
    h_o1 = rcopy(zrows(s.go, 1 - c, half), s.ro1, sib)

    def heads_back(g, _):
        lanes = pl.ds(pl.multiple_of(g * 128, 128), 128)
        for k in range(K8):
            ks = slice(k * 128, (k + 1) * 128)
            da = pick(g, k)
            at = s.att[g, :, ks]
            s.dgate[k : k + 1, lanes] = jnp.sum(at * da, axis=0, keepdims=True)
            do = (da * (s.gate[k : k + 1, lanes] * s.linv[g, 0:1, ks])).astype(BF)
            s.dox[g, 64:128, ks] = do
            delta = -jnp.sum(do.astype(F32) * at, axis=0, keepdims=True)
            top = delta.astype(BF).astype(F32)
            s.dox[g, 0:16, ks] = jnp.where(
                row16 == 0, top, jnp.where(row16 == 1, delta - top, 0.0)
            ).astype(BF)
            s.dox[g, 16:64, ks] = jnp.zeros((48, 128), BF)
        return 0

    lax.fori_loop(0, 4, heads_back, 0)
    s.dkv[...] = jnp.zeros(s.dkv.shape, F32)

    left = lax.broadcasted_iota(jnp.int32, (256, 128), 1) < 64

    def attend_back(g):
        b, p = g // 2, g % 2
        nt, first = tiles[b], base[b]
        for rc in range(NR):
            ls = slice(rc * R, (rc + 1) * R)

            def tile(t, acc):
                prob = s.pst[p, first + t, :, ls]
                dprob = mm(s.vx[p, t], s.dox[g, :, ls])
                ds = (prob.astype(F32) * dprob).astype(BF)
                kpart = mm_nt(ds, s.qx[g, :, ls])
                vpart = mm_nt(prob, s.dox[g, :, ls])
                s.dkv[p, t] += jnp.where(left, kpart * LN2, vpart)
                return acc + mm(s.kt[p, t], ds)

            s.att[g, :, ls] = lax.fori_loop(0, nt, tile, jnp.zeros((HD, R), F32))

    def add_rows(n, step, fn):
        def one(i, _):
            fn(pl.ds(pl.multiple_of(i * step, step), step))
            return 0

        lax.fori_loop(0, n // step, one, 0)

    def both(a, b):
        return (a.astype(F32) + b.astype(F32)).astype(BF)

    attend_back(0)
    rwait(h_f1, s.rf1)

    def pair_ffn(rows):
        for w in range(2):
            s.rf1[w, rows, :] = both(s.gf[w, rows, pl.ds(lo, HB)], s.rf1[w, rows, :])

    add_rows(D, 64, pair_ffn)
    h_f2 = [None] + [
        rcopy(
            s.rf1.at[:, pl.ds(pl.multiple_of(zp[i][0] * shard, shard), shard), :],
            s.rf2.at[i - 1],
            zp[i],
        )
        for i in range(1, dp)
    ]
    rwait(h_o1, s.ro1)

    def pair_sum(own, got):
        def one(i, _):
            rows = pl.ds(pl.multiple_of(i * 64, 64), 64)
            mine = pl.ds(pl.multiple_of(c * half + i * 64, 64), 64)
            got[rows, :] = both(own[mine, :], got[rows, :])
            return 0

        lax.fori_loop(0, half // 64, one, 0)

    pair_sum(s.go, s.ro1)
    h_o2 = [None] + [rcopy(zrows(s.ro1, qs[m], ER), s.ro2.at[m - 1], chips[m]) for m in (1, 2, 3)]

    def chip_sum(dst, own, got):
        total = own[pl.ds(pl.multiple_of(q * ER, ER), ER), :].astype(F32)
        for m in (1, 2, 3):
            total = total + got[m - 1].astype(F32)
        dst[0:ER, :] = total.astype(BF)
        if dp * pr > ER:
            dst[ER:, :] = jnp.zeros((dp * pr - ER, D), BF)

    def z_scatter(own, got):
        return [None] + [rcopy(zrows(own, zp[i][0], pr), got.at[i - 1], zp[i]) for i in range(1, dp)]

    def z_sum(own, got, dst):
        total = own[pl.ds(pl.multiple_of(z * pr, pr), pr), :].astype(F32)
        for i in range(1, dp):
            total = total + got[i - 1].astype(F32)
        done = total.astype(BF)
        dst[pl.ds(pl.multiple_of(z * pr, pr), pr), :] = done
        wide = done.astype(F32)
        return [None] + [
            rcopy(zrows(dst, z, pr), zrows(dst, z, pr), zp[i]) for i in range(1, dp)
        ], wide * wide

    def fold(sq):
        sq = jnp.sum(sq, axis=0, keepdims=True)
        out = sq[:, 0:128]
        for j in range(1, sq.shape[1] // 128):
            out = out + sq[:, j * 128 : (j + 1) * 128]
        return out

    attend_back(1)
    for m in (1, 2, 3):
        rwait(h_o2[m], s.ro2.at[m - 1])
    chip_sum(s.xo, s.ro1, s.ro2)
    h_o3 = z_scatter(s.xo, s.ro3)

    attend_back(2)
    for i in range(1, dp):
        rwait(h_f2[i], s.rf2.at[i - 1])
    for w in range(2):
        total = s.rf1[w, pl.ds(pl.multiple_of(z * shard, shard), shard), :].astype(F32)
        for i in range(1, dp):
            total = total + s.rf2[i - 1, w].astype(F32)
        s.rs[w] = total.astype(BF)
    quart = HB // 4
    h_f3 = [None] + [
        rcopy(
            s.rs.at[:, :, pl.ds(pl.multiple_of(qs[m] * quart, quart), quart)],
            s.rf3.at[m - 1],
            chips[m],
        )
        for m in (1, 2, 3)
    ]
    for i in range(1, dp):
        rwait(h_o3[i], s.ro3.at[i - 1])
    h_o4, sq_o = z_sum(s.xo, s.ro3, s.fo)

    attend_back(3)
    sent(h_kvs)
    for m in (1, 2, 3):
        sent(h_kv[m])
    for dev in range(PL):
        sl = (dev % 2) * 4 + dev // 2
        for b, blk in enumerate((2 * dev, 15 - 2 * dev)):
            for p in range(2):
                s.kvb[sl, b, p * 128 : (p + 1) * 128, :] = s.dkv[p, blk // 2, (blk % 2) * 128 : (blk % 2) * 128 + 128, :].astype(BF)
    h_k1 = rcopy(s.kvb.at[pl.ds((1 - c) * 4, 4)], s.rk1, sib)
    spread(s.at, s.att, None)
    rwait(h_k1, s.rk1)
    for i in range(4):
        s.rk1[i] = both(s.kvb[c * 4 + i], s.rk1[i])
    h_k2 = [None] + [rcopy(s.rk1.at[qs[m]], s.rk2.at[m - 1], chips[m]) for m in (1, 2, 3)]

    sent(h_o1)

    def query_grad(i, _):
        rows = pl.ds(pl.multiple_of(i * 256, 256), 256)
        s.go[rows, :] = mm(s.at[rows, :], s.nd[...]).astype(BF)
        return 0

    lax.fori_loop(0, NE * HD // 256, query_grad, 0)
    h_q1 = rcopy(zrows(s.go, 1 - c, half), s.rq1, sib)
    s.acc2[...] = jnp.zeros((T, D), F32)

    def slot_sum(i, _):
        rows = pl.ds(pl.multiple_of(i * 256, 256), 256)
        s.acc2[...] += mm_tn(s.at[rows, :], s.eq[rows, :])
        return 0

    lax.fori_loop(0, NE * HD // 256, slot_sum, 0)
    gate = s.gate[...]
    dch = gate * (s.dgate[...] - jnp.sum(gate * s.dgate[...], axis=0, keepdims=True))
    dlog = jnp.zeros((32, T), F32)
    for k in range(K8):
        dlog = dlog + jnp.where(row_e == s.rtd[k : k + 1, :], dch[k : k + 1, :], 0.0)
    dlog = dlog.astype(BF)
    s.acc2[...] += mm_tn(dlog, wrt[...])
    grt = mm(dlog, s.nd[...])

    rwait(h_q1, s.rq1)
    pair_sum(s.go, s.rq1)
    for m in (1, 2, 3):
        rwait(h_k2[m], s.rk2.at[m - 1])
    for i in range(2):
        total = s.rk1[q, i].astype(F32)
        for m in (1, 2, 3):
            total = total + s.rk2[m - 1, i].astype(F32)
        s.dkvd[i * 256 : (i + 1) * 256, :] = total.astype(BF)
    dn = s.acc2[...] + mm_nt(s.dkvd[...], s.wkvf[...])
    unit0, inv0 = rms(s.tokd[...].astype(F32))
    back0, gain0 = rms_back(dn, g0, unit0, inv0)
    s.tbf[:, 0:512] = mm_tn(s.dkvd[...], s.nd[...])
    for j in range(4):
        js = slice(j * 128, (j + 1) * 128)
        s.tbf[j * 24 : (j + 1) * 24, 512:640] = grt[0:24, js]
        s.tbf[96 + j : 97 + j, 512:640] = gain0[:, js]
        s.tbf[100 + j : 101 + j, 512:640] = s.gain[1:2, js]
    s.tbf[104:128, 512:640] = jnp.zeros((24, 128), F32)
    s.tb[...] = s.tbf[...].astype(BF)
    h_t1 = rcopy(zrows(s.tb, 1 - c, 64), s.rt1, sib)
    h_q2 = [None] + [rcopy(zrows(s.rq1, qs[m], ER), s.rq2.at[m - 1], chips[m]) for m in (1, 2, 3)]

    grad = s.mixed[...] + back0
    s.tgx[...] = mm(join, grad[256:512].astype(BF)).astype(BF)
    rwait(h_t1, s.rt1)
    s.tsm[...] = both(s.tb[pl.ds(pl.multiple_of(c * 64, 64), 64), :], s.rt1[...])
    h_t2 = [None] + [rcopy(zrows(s.tsm, qs[m], 16), s.rt2.at[m - 1], chips[m]) for m in (1, 2, 3)]
    h_tg = rcopy(s.tgx, s.tgr, swap)
    top = grad[0:256].astype(BF)
    rest = (grad[0:256] - top.astype(F32)).astype(BF)
    s.acc1[0:256, :] = mm(join, top) + mm(join, rest)

    for m in (1, 2, 3):
        rwait(h_f3[m], s.rf3.at[m - 1])
    mine = pl.ds(pl.multiple_of(q * quart, quart), quart)
    sq_f = jnp.zeros((1, 128), F32)
    wide = pl.ds(pl.multiple_of(c * HB + q * quart, quart), quart)
    for w in range(2):
        total = s.rs[w, :, mine].astype(F32)
        for m in (1, 2, 3):
            total = total + s.rf3[m - 1, w].astype(F32)
        done = total.astype(BF)
        s.f2[w, :, wide] = done
        sq_f = sq_f + fold(done.astype(F32) * done.astype(F32))
    h_f4 = [None] + [
        rcopy(s.f2.at[:, :, wide], s.f2.at[:, :, wide], chips[m]) for m in (1, 2, 3)
    ]

    for m in (1, 2, 3):
        rwait(h_t2[m], s.rt2.at[m - 1])
    total = s.tsm[pl.ds(pl.multiple_of(q * 16, 16), 16), :].astype(F32)
    for m in (1, 2, 3):
        total = total + s.rt2[m - 1].astype(F32)
    s.rt3[z] = total.astype(BF)
    h_t3 = [None] + [rcopy(s.rt3.at[z], s.rt3.at[z], zp[i]) for i in range(1, dp)]
    for m in (1, 2, 3):
        rwait(h_q2[m], s.rq2.at[m - 1])
    chip_sum(s.xq, s.rq1, s.rq2)
    h_q3 = z_scatter(s.xq, s.rq3)

    for i in range(1, dp):
        rwait(h_t3[i], s.rt3.at[zfrom[i]])
    total = s.rt3[0].astype(F32)
    for i in range(1, dp):
        total = total + s.rt3[i].astype(F32)
    done = total.astype(BF)
    s.tf[pl.ds(pl.multiple_of(slot * 16, 16), 16), :] = done
    h_t4 = [None] + [
        rcopy(zrows(s.tf, slot, 16), zrows(s.tf, slot, 16), chips[m]) for m in (1, 2, 3)
    ]
    sq_t = fold(done.astype(F32) * done.astype(F32)) * (1.0 / dp)

    for i in range(1, dp):
        rwait(h_q3[i], s.rq3.at[i - 1])
    h_q4, sq_q = z_sum(s.xq, s.rq3, s.fq)

    squares = sq_f + sq_t + fold(sq_o) + fold(sq_q)
    s.mz[z] = jnp.where(row32 < 24, s.cnt[...], jnp.where(row32 == 24, squares, 0.0))
    h_m1 = [None] + [rcopy(s.mz.at[z], s.mz.at[z], zp[i]) for i in range(1, dp)]

    for m in (1, 2, 3):
        rwait(
            h_f4[m],
            s.f2.at[:, :, pl.ds(pl.multiple_of(c * HB + qs[m] * quart, quart), quart)],
        )
    h_f5 = rcopy(s.f2.at[:, :, pl.ds(lo, HB)], s.f2.at[:, :, pl.ds(lo, HB)], sib)
    for m in (1, 2, 3):
        rwait(h_t4[m], zrows(s.tf, c * 4 + qs[m], 16))
    h_t5 = rcopy(zrows(s.tf, c, 64), zrows(s.tf, c, 64), sib)

    for i in range(1, dp):
        rwait(h_m1[i], s.mz.at[zfrom[i]])
    total = s.mz[0]
    for i in range(1, dp):
        total = total + s.mz[i]
    s.mq[e] = total
    h_m2 = [None] + [rcopy(s.mq.at[e], s.mq.at[e], plane[i]) for i in range(1, PL)]

    rwait(h_lay, s.layr)
    s.layo[256:512, :] = s.layr[...]
    done = [lcopy(s.layo, lay, 0)]
    rwait(h_tg, s.tgr)
    s.acc1[256:512, :] = s.tgr[...].astype(F32)
    done.append(lcopy(s.acc1, tg, 1))
    rwait(h_f5, s.f2.at[:, :, pl.ds(hi, HB)])
    done.append(lcopy(s.f2, f2o, 2))
    rwait(h_t5, zrows(s.tf, 1 - c, 64))
    done.append(lcopy(s.tf, tbo, 3))
    for i in range(1, dp):
        rwait(h_o4[i], zrows(s.fo, zfrom[i], pr))
        rwait(h_q4[i], zrows(s.fq, zfrom[i], pr))
    done.append(lcopy(s.fo.at[pl.ds(0, ER)], foo, 4))
    done.append(lcopy(s.fq.at[pl.ds(0, ER)], fqo, 5))
    for i in range(1, PL):
        rwait(h_m2[i], s.mq.at[(e + PL - i) % PL])
    total = s.mq[0]
    for i in range(1, PL):
        total = total + s.mq[i]
    s.cnt[...] = total
    done.append(lcopy(s.cnt, msgo, 6))
    for d in done:
        d.wait()
    for d in sends:
        d.wait_send()
    assert count[0] <= copies_of(dp)


def adam_update(weight, gradient, first_moment, second, clip_scale, step_rate, decay_rate):
    step_grad = gradient * clip_scale
    new_first = BETA_FIRST * first_moment + (1.0 - BETA_FIRST) * step_grad
    new_second = BETA_SECOND * second + (1.0 - BETA_SECOND) * step_grad * step_grad
    first_hat = new_first / (1.0 - BETA_FIRST**ADAM_STEP)
    second_hat = new_second / (1.0 - BETA_SECOND**ADAM_STEP)
    new_weight = weight - step_rate * (
        first_hat / (jnp.sqrt(second_hat) + ADAM_EPS) + decay_rate * weight
    )
    return (new_weight, new_first, new_second)


def on_device(
    tokens, cotangent, routes, group_batch, seq_lengths,
    gains, gains_first, gains_second,
    router_weight, router_first, router_second,
    keyval_weight, keyval_first, keyval_second,
    query_weight, query_first, query_second,
    output_weight, output_first, output_second,
    up_weight, up_first, up_second,
    down_weight, down_first, down_second,
):
    dp = lax.axis_size("dp")
    z = lax.axis_index("dp")
    shard = D // dp
    pr = piece_rows(dp)
    batch = lax.dynamic_index_in_dim(group_batch, z, 0, keepdims=True)
    lengths = lax.dynamic_index_in_dim(seq_lengths, z, 0, keepdims=False)
    info = jnp.concatenate([batch, lengths])
    rt = routes.reshape(2, 128, 2, K8).transpose(3, 0, 2, 1).reshape(K8, T)
    w2i = jnp.stack([up_weight, down_weight.T]).astype(BF)
    eqi = query_weight.transpose(0, 2, 1).reshape(ER, D).astype(BF)
    eoi = output_weight.reshape(ER, D).astype(BF)
    wrt = jnp.pad(router_weight.T, ((0, 32 - NE), (0, 0))).astype(BF)

    scr = []
    for name, item in scratch_list(dp).items():
        if item is None:
            scr.append(pltpu.SemaphoreType.DMA((copies_of(dp),)))
        elif len(item) == 1:
            scr.append(pltpu.SemaphoreType.DMA(item))
        else:
            scr.append(pltpu.VMEM(item[0], item[1]))
    vm = pl.BlockSpec(memory_space=pltpu.VMEM)
    hbm = pl.BlockSpec(memory_space=pl.ANY)
    outs = [
        jax.ShapeDtypeStruct((T, D), BF),
        jax.ShapeDtypeStruct((T, D), F32),
        jax.ShapeDtypeStruct((32, 128), F32),
        jax.ShapeDtypeStruct((2, shard, FF), BF),
        jax.ShapeDtypeStruct((ER, D), BF),
        jax.ShapeDtypeStruct((ER, D), BF),
        jax.ShapeDtypeStruct((128, 640), BF),
    ]

    def kernel(*refs):
        layer_kernel(dp, *refs)

    lay, tg, msg, f2, fq, fo, tb = pl.pallas_call(
        kernel,
        out_shape=outs,
        in_specs=[vm] * 4 + [hbm] * 3 + [vm] * 2 + [pl.BlockSpec(memory_space=pltpu.SMEM)],
        out_specs=[hbm] * len(outs),
        scratch_shapes=scr,
        compiler_params=pltpu.CompilerParams(
            collective_id=0, has_side_effects=True, vmem_limit_bytes=64 * 2**20 - 2**17
        ),
        name="layer",
    )(tokens, cotangent, rt, keyval_weight.astype(BF), w2i, eqi, eoi, wrt, gains, info)

    counts = msg[0:NE, 0].astype(jnp.int32)
    grad_norm = jnp.sqrt(jnp.sum(msg[24]))
    clip = CLIP_LIMIT / jnp.maximum(grad_norm, CLIP_LIMIT)
    up_g = f2[0].astype(F32)
    down_g = f2[1].T.astype(F32)
    q_g = fq.reshape(LE, HD, D).transpose(0, 2, 1).astype(F32)
    o_g = fo.reshape(LE, HD, D).astype(F32)
    kv_g = lax.dynamic_slice_in_dim(tb[:, 0:512], z * shard, shard, 1).T.astype(F32)
    side = tb[:, 512:640].astype(F32)
    r_g = side[0:96].reshape(4, NE, 128).transpose(1, 0, 2).reshape(NE, D).T
    gain_g = side[96:104].reshape(2, D)
    gains_out = adam_update(gains, gain_g, gains_first, gains_second, clip, 0.7, 0.0)
    router_out = adam_update(router_weight, r_g, router_first, router_second, clip, 0.03, 0.1)
    keyval_out = adam_update(keyval_weight, kv_g, keyval_first, keyval_second, clip, 0.06, 0.1)
    query_out = adam_update(query_weight, q_g, query_first, query_second, clip, 0.06, 0.1)
    output_out = adam_update(output_weight, o_g, output_first, output_second, clip, 2.0, 0.1)
    up_out = adam_update(up_weight, up_g, up_first, up_second, clip, 0.06, 0.1)
    down_out = adam_update(down_weight, down_g, down_first, down_second, clip, 0.03, 0.1)
    return (
        lay, tg, counts, grad_norm,
        *gains_out, *router_out, *keyval_out, *query_out, *output_out, *up_out, *down_out,
    )


def solution(mesh):
    tok = P(("dp", "expert"), None)
    dp0 = P("dp", None)
    ex0 = P("expert", None, None)
    dp1 = P(None, "dp")
    return jax.shard_map(
        on_device,
        mesh=mesh,
        in_specs=(tok,) * 3 + (P(),) * 8 + (dp0,) * 3 + (ex0,) * 6 + (dp0,) * 3 + (dp1,) * 3,
        out_specs=(tok,) * 2 + (P(),) * 8 + (dp0,) * 3 + (ex0,) * 6 + (dp0,) * 3 + (dp1,) * 3,
        check_vma=False,
    )
```

```python
import math

import jax
import jax.numpy as jnp
from jax import lax
from jax.experimental import pallas as pl
from jax.experimental.pallas import tpu as pltpu
from jax.sharding import PartitionSpec as P

ADAM_STEP = 10
NORM_EPS = 1e-06
BETA_FIRST = 0.9
BETA_SECOND = 0.999
ADAM_EPS = 1e-08
CLIP_LIMIT = 1.0
MASKED = -1e30
LOG2E = math.log2(math.e)
LN2 = math.log(2.0)
MESH = pl.DeviceIdType.MESH
BF = jnp.bfloat16
F32 = jnp.float32

T = 512
D = 512
FF = 2048
HD = 64
K8 = 8
NE = 24
PL = 8
LE = NE // PL
ER = LE * HD
HB = FF // 2
R = 512
NR = K8 * 128 // R


def mm(a, b):
    return jnp.dot(a, b, preferred_element_type=F32)


def mm_nt(a, b):
    return lax.dot_general(a, b, (((1,), (1,)), ((), ())), preferred_element_type=F32)


def mm_tn(a, b):
    return lax.dot_general(a, b, (((0,), (0,)), ((), ())), preferred_element_type=F32)


def expert_at(place):
    return LE * device_at(place // LE) + place % LE


def device_at(slot):
    c, a, b = slot // 4, slot // 2 % 2, slot % 2
    qx, qy = (a, b) if c == 0 else (b, a)
    return 4 * qy + 2 * qx + c


def slot_of(dev):
    c, qx, qy = dev % 2, dev // 2 % 2, dev // 4
    return 4 * c + (2 * qx + qy if c == 0 else 2 * qy + qx)


def piece_rows(dp):
    return -(-ER // (dp * 16)) * 16


def scratch_list(dp):
    shard = D // dp
    pr = piece_rows(dp)
    return dict(
        wkvf=((D, 2 * HD), BF),
        w2=((2, D, FF), BF),
        eq=((NE * HD, D), BF),
        eo=((NE * HD, D), BF),
        kvb=((PL, 2, 256, 128), BF),
        tokx=((256, D), BF),
        cotx=((256, D), BF),
        rtx=((8, 256), jnp.int32),
        rts=((8, 256), jnp.int32),
        wrt=((32, D), F32),
        tokd=((T, D), BF),
        cotd=((T, D), BF),
        cott=((D, T), BF),
        rtd=((8, T), jnp.int32),
        nd=((T, D), BF),
        gate=((8, T), F32),
        dgate=((8, T), F32),
        big=((PL * 256, T), F32),
        at=((NE * HD, T), BF),
        qx=((4, 128, 1024), BF),
        dox=((4, 128, 1024), BF),
        att=((4, HD, 1024), F32),
        linv=((4, 8, 1024), F32),
        kx=((2, 8, 256, 128), BF),
        vx=((2, 8, 256, 128), BF),
        kt=((2, 8, HD, 256), BF),
        vt=((2, 8, HD + 16, 256), BF),
        pst=((2, 9, 256, 1024), BF),
        dkv=((2, 8, 256, 128), F32),
        mixed=((T, D), F32),
        ffn=((T, D), BF),
        ffnt=((D, T), BF),
        acc1=((T, D), F32),
        acc2=((T, D), F32),
        gfh=((2, D, HB), BF),
        gfl=((2, D, HB), BF),
        rf1=((2, D, HB), BF),
        rfa=((2, D, HB // 2), BF),
        rfb=((2, D, HB // 4), BF),
        rfc=((dp - 1, 2, shard, HB // 4), BF),
        f2=((2, shard, FF), BF),
        go=((NE * HD, D), BF),
        rq1=((NE * HD // 2, D), BF),
        ro1=((NE * HD // 2, D), BF),
        rq2=((2 * ER, D), BF),
        ro2=((2 * ER, D), BF),
        rq3=((ER, D), BF),
        ro3=((ER, D), BF),
        xq=((dp * pr, D), BF),
        xo=((dp * pr, D), BF),
        rq4=((dp - 1, pr, D), BF),
        ro4=((dp - 1, pr, D), BF),
        fq=((dp * pr, D), BF),
        fo=((dp * pr, D), BF),
        rk1=((4, 2, 256, 128), BF),
        rk2=((3, 2, 256, 128), BF),
        dkvd=((T, 128), BF),
        tbf=((128, 640), F32),
        tb=((128, 640), BF),
        rt1=((64, 640), BF),
        tsm=((64, 640), BF),
        rt2=((3, 16, 640), BF),
        rt3=((dp, 16, 640), BF),
        tf=((128, 640), BF),
        cnt=((32, 128), F32),
        mz=((dp, 32, 128), F32),
        mq=((PL, 32, 128), F32),
        layx=((256, D), BF),
        layr=((256, D), BF),
        tgr=((256, D), BF),
        gain=((8, D), F32),
        osem=(9,),
        ssem=None,
        rsem=None,
    )


def copies_of(dp):
    return 80 + 12 * dp


def layer_kernel(dp, *refs):
    shard = D // dp
    pr = piece_rows(dp)
    (tok, cot, routes, wkv, up, down, qw, ow, rw, gains, gbatch, lens) = refs[:12]
    (lay, tg, msgo, f2o, fqo, foo, sideo, kvo) = refs[12:20]
    names = list(scratch_list(dp))
    s = type("Scratch", (), dict(zip(names, refs[20:])))

    z = lax.axis_index("dp")
    e = lax.axis_index("expert")
    c = e % 2
    qx = e // 2 % 2
    qy = e // 4
    a = (1 - c) * qx + c * qy
    b = (1 - c) * qy + c * qx
    q = 2 * a + b

    def device(a_, b_):
        return (z, 4 * ((1 - c) * b_ + c * a_) + 2 * ((1 - c) * a_ + c * b_) + c)

    qs = [q, 2 * a + 1 - b, 2 * (1 - a) + b, 2 * (1 - a) + 1 - b]
    sib = (z, e + 1 - 2 * c)
    near, far = device(a, 1 - b), device(1 - a, b)
    chips = [None, near, far, device(1 - a, 1 - b)]
    swap = (z, 7 - e)
    zp = [None] + [((z + i) % dp, e) for i in range(1, dp)]
    zfrom = [None] + [(z + dp - i) % dp for i in range(1, dp)]
    slot = c * 4 + q
    plane = [sib] + [(z, (e + i) % PL) for i in range(1, PL)]

    count = [0]
    sends = []

    def rcopy(src, dst, peer):
        k = count[0]
        count[0] += 1
        d = pltpu.make_async_remote_copy(
            src_ref=src,
            dst_ref=dst,
            send_sem=s.ssem.at[k],
            recv_sem=s.rsem.at[k],
            device_id=peer,
            device_id_type=MESH,
        )
        d.start()
        sends.append(d)
        return (k, peer, d)

    def sent(handle):
        sends[:] = [d for d in sends if d is not handle[2]]
        handle[2].wait_send()

    def rwait(handle, dst):
        k, peer, _ = handle
        pltpu.make_async_remote_copy(
            src_ref=dst,
            dst_ref=dst,
            send_sem=s.ssem.at[k],
            recv_sem=s.rsem.at[k],
            device_id=peer,
            device_id_type=MESH,
        ).wait_recv()

    def lcopy(src, dst, k):
        d = pltpu.make_async_copy(src, dst, s.osem.at[k])
        d.start()
        return d

    bar = pltpu.get_barrier_semaphore()
    for peer in plane[1:] + zp[1:]:
        pl.semaphore_signal(bar, inc=1, device_id=peer, device_id_type=MESH)

    def zrows(ref, i, n):
        return ref.at[pl.ds(pl.multiple_of(i * n, n), n)]

    def turned(x):
        rows, cols = x.shape
        if cols % 128:
            x = jnp.concatenate([x, jnp.zeros((rows, 128 - cols % 128), x.dtype)], axis=1)
        return x.T[0:cols]

    lo = pl.multiple_of(c * HB, HB)
    hi = pl.multiple_of((1 - c) * HB, HB)
    ri = lax.broadcasted_iota(jnp.int32, (256, 256), 0)
    ci = lax.broadcasted_iota(jnp.int32, (256, 256), 1)
    split = jnp.where(ci == 2 * (ri % 128) + ri // 128, 1.0, 0.0).astype(BF)
    join = jnp.where(ri == 2 * (ci % 128) + ci // 128, 1.0, 0.0).astype(BF)
    own_rows = pl.ds(pl.multiple_of(z * shard, shard), shard)
    s.wkvf[own_rows, :] = wkv[...].astype(BF)
    rtt = routes[...].astype(F32).astype(BF)
    s.rtd[:, 0:256] = mm(rtt[:, 0:256], join).astype(jnp.int32)
    s.rts[...] = mm(rtt[:, 256:512], join).astype(jnp.int32)
    WD = HB // 2
    WP = (HB - WD) // 4
    part = pl.multiple_of(c * HB + WD + q * WP, WP)
    for at, n in ((lo, WD), (part, WP)):
        s.w2[0, own_rows, pl.ds(at, n)] = up[:, pl.ds(at, n)].astype(BF)
        s.w2[1, own_rows, pl.ds(at, n)] = turned(down[pl.ds(at, n), :]).astype(BF)

    def w2_rows(i, at, n):
        return s.w2.at[:, pl.ds(pl.multiple_of(i * shard, shard), shard), pl.ds(at, n)]

    def to_all_z(ref):
        return [None] + [rcopy(ref, ref, zp[i]) for i in range(1, dp)]
    pl.semaphore_wait(bar, PL - 1 + dp - 1)
    h_wkv = [None] + [
        rcopy(zrows(s.wkvf, z, shard), zrows(s.wkvf, z, shard), zp[i]) for i in range(1, dp)
    ]
    h_tok = rcopy(tok.at[pl.ds(256, 256)], s.tokx, swap)
    h_rt = rcopy(s.rts, s.rtx, swap)
    for i in range(LE):
        rows = pl.ds(pl.multiple_of(slot * ER + i * HD, HD), HD)
        s.eq[rows, :] = qw[i].astype(BF)
        s.eo[rows, :] = ow[i].astype(BF)
    own_eq = zrows(s.eq, slot, ER)
    own_eo = zrows(s.eo, slot, ER)
    h_eq1 = rcopy(own_eq, own_eq, near)
    h_wp1 = to_all_z(w2_rows(z, part, WP))
    h_wd = to_all_z(w2_rows(z, lo, WD))

    def gather_far(h, ref):
        rwait(h, zrows(ref, c * 4 + qs[1], ER))
        pair = zrows(ref, c * 2 + a, 2 * ER)
        return rcopy(pair, pair, far)

    def gather_sib(h, ref):
        rwait(h, zrows(ref, c * 2 + 1 - a, 2 * ER))
        mine = zrows(ref, c, 4 * ER)
        return rcopy(mine, mine, sib)

    def w2_cols(at, n):
        return s.w2.at[:, :, pl.ds(at, n)]

    s.wrt[0:NE, :] = rw[...]
    s.wrt[NE:32, :] = jnp.zeros((32 - NE, D), F32)

    g0 = gains[0:1, :]
    g1 = gains[1:2, :]

    def rms(x):
        inv = lax.rsqrt(jnp.mean(x * x, axis=-1, keepdims=True) + NORM_EPS)
        return x * inv, inv

    nat0 = mm(split, tok[0:256, :])
    nat1 = mm(split, tok[256:512, :])
    s.tokd[0:256, :] = nat0.astype(BF)
    n0 = (rms(nat0)[0] * g0).astype(BF)
    n1 = (rms(nat1)[0] * g0).astype(BF)
    s.nd[0:256, :] = n0
    cot0 = mm(split, cot[0:256, :])
    s.cotd[0:256, :] = cot0.astype(BF)

    for i in range(1, dp):
        rwait(h_wkv[i], zrows(s.wkvf, zfrom[i], shard))
    kv0 = mm(n0, s.wkvf[...]).astype(BF)
    kv1 = mm(n1, s.wkvf[...]).astype(BF)
    for p in range(2):
        s.kvb[slot, p, 0:128, :] = kv0[p * 128 : (p + 1) * 128]
        s.kvb[slot, p, 128:256, :] = kv1[p * 128 : (p + 1) * 128]
    h_kv = [None] + [rcopy(s.kvb.at[slot], s.kvb.at[slot], chips[m]) for m in (1, 2, 3)]
    h_eq2 = gather_far(h_eq1, s.eq)
    h_cot = rcopy(cot.at[pl.ds(256, 256)], s.cotx, swap)
    h_eo1 = rcopy(own_eo, own_eo, near)

    rwait(h_tok, s.tokx)
    rwait(h_rt, s.rtx)
    sw = mm(split, s.tokx[...])
    s.tokd[256:512, :] = sw.astype(BF)
    s.nd[256:512, :] = (rms(sw)[0] * g0).astype(BF)
    s.rtd[:, 256:512] = s.rtx[...]

    wrt = s.wrt[...].astype(BF)
    bm1 = gbatch[z] - 1
    is2 = (4 - gbatch[z]) // 2

    def seq_pos(r):
        return r & bm1, (r >> 1) * is2 + (r >> 2) * (1 - is2)

    def limit_of(index):
        out = jnp.zeros(index.shape, jnp.int32)
        for i in range(4):
            out = jnp.where(index == i, lens[z, i], out)
        return out

    block = [2 * e, 15 - 2 * e]
    lanes128 = lax.broadcasted_iota(jnp.int32, (16, 128), 1)
    row16 = lax.broadcasted_iota(jnp.int32, (16, 128), 0)
    row32 = lax.broadcasted_iota(jnp.int32, (32, 128), 0)

    logits = mm_nt(wrt, s.nd[...])
    row_e = lax.broadcasted_iota(jnp.int32, (32, T), 0)
    chosen = jnp.concatenate(
        [
            jnp.sum(jnp.where(row_e == s.rtd[k : k + 1, :], logits, 0.0), axis=0, keepdims=True)
            for k in range(K8)
        ],
        axis=0,
    )
    ex = jnp.exp(chosen - jnp.max(chosen, axis=0, keepdims=True))
    s.gate[...] = ex / jnp.sum(ex, axis=0, keepdims=True)

    counts = jnp.zeros((32, 128), F32)
    for g in range(4):
        blk, p = g // 2, g % 2
        row = 2 * (block[blk] * 128 + lanes128) + p
        seq, pos = seq_pos(row)
        live = (pos < limit_of(seq))[0:1, :].astype(F32)
        for k in range(K8):
            counts = counts + jnp.where(
                row32 == s.rtd[k : k + 1, g * 128 : (g + 1) * 128], live, 0.0
            )
        feat = jnp.where(seq == row16, 1.0, 0.0).astype(BF)
        s.qx[g, 64:80, :] = jnp.concatenate([feat] * K8, axis=1)
        s.qx[g, 80:128, :] = jnp.zeros((48, 1024), BF)
    s.cnt[...] = jnp.broadcast_to(jnp.sum(counts, axis=1, keepdims=True), (32, 128))

    half = NE * HD // 2
    h_eqs = gather_sib(h_eq2, s.eq)
    for m in (1, 2, 3):
        rwait(h_kv[m], s.kvb.at[c * 4 + qs[m]])
    h_kvs = rcopy(s.kvb.at[pl.ds(c * 4, 4)], s.kvb.at[pl.ds(c * 4, 4)], sib)
    rwait(h_eqs, zrows(s.eq, 1 - c, half))

    def query_rows(i, _):
        rows = pl.ds(pl.multiple_of(i * 256, 256), 256)
        s.big[rows, :] = mm_nt(s.eq[rows, :], s.nd[...])
        return 0

    lax.fori_loop(0, NE * HD // 256, query_rows, 0)

    def pick(g, k):
        lanes = pl.ds(pl.multiple_of(g * 128, 128), 128)
        rk = s.rtd[k : k + 1, lanes]
        acc = jnp.zeros((HD, 128), F32)
        for place in range(NE):
            acc = jnp.where(rk == expert_at(place), s.big[place * HD : (place + 1) * HD, lanes], acc)
        return acc

    def choose(g, _):
        for k in range(K8):
            s.qx[g, 0:64, k * 128 : (k + 1) * 128] = (pick(g, k) * (0.125 * LOG2E)).astype(BF)
        return 0

    lax.fori_loop(0, 4, choose, 0)

    for i in range(1, dp):
        rwait(h_wp1[i], w2_rows(zfrom[i], part, WP))
    h_wp2 = rcopy(w2_cols(part, WP), w2_cols(part, WP), near)
    h_eo2 = gather_far(h_eo1, s.eo)
    rwait(h_kvs, s.kvb.at[pl.ds((1 - c) * 4, 4)])
    krow = lax.broadcasted_iota(jnp.int32, (256, 128), 0)
    klane = lax.broadcasted_iota(jnp.int32, (256, 128), 1)
    for t in range(8):
        for p in range(2):
            kv = s.kvb[slot_of(t), p].astype(F32)
            seq, pos = seq_pos(2 * (t * 256 + krow) + p)
            col = klane - 64
            shown = (seq == col) & (pos < limit_of(col))
            feat = jnp.where(shown | (col > 3), 0.0, MASKED)
            s.kx[p, t] = jnp.where(col < 0, kv, feat).astype(BF)
            s.vx[p, t] = jnp.where(col >= 0, kv, jnp.where(klane < 2, 1.0, 0.0)).astype(BF)
            kvt = kv.T
            s.kt[p, t] = kvt[0:64].astype(BF)
            s.vt[p, t, 0:64, :] = kvt[64:128].astype(BF)
            s.vt[p, t, 64:80, :] = jnp.ones((16, 256), BF)

    tiles = [e + 1, 8 - e]
    base = [0, e + 1]

    def attend(g, rc):
        blk, p = g // 2, g % 2
        nt, first = tiles[blk], base[blk]
        visible = (
            lax.broadcasted_iota(jnp.int32, (256, 128), 0)
            <= lax.broadcasted_iota(jnp.int32, (256, 128), 1) + 128 * blk
        )
        visible = jnp.concatenate([visible] * (R // 128), axis=1)
        ls = slice(rc * R, (rc + 1) * R)

        def scores(t, peak):
            sc = mm(s.kx[p, t], s.qx[g, :, ls])
            s.big[pl.ds(pl.multiple_of(t * 256, 256), 256), :] = sc
            return jnp.maximum(peak, jnp.max(sc.reshape(32, 8, R), axis=0))

        peak = lax.fori_loop(0, nt - 1, scores, jnp.full((8, R), MASKED, F32))
        sc = jnp.where(visible, mm(s.kx[p, nt - 1], s.qx[g, :, ls]), MASKED)
        s.big[pl.ds(pl.multiple_of((nt - 1) * 256, 256), 256), :] = sc
        peak = jnp.maximum(peak, jnp.max(sc.reshape(32, 8, R), axis=0))
        peak = jnp.max(peak, axis=0, keepdims=True)

        def values(t, acc):
            pb = jnp.exp2(s.big[pl.ds(pl.multiple_of(t * 256, 256), 256), :] - peak).astype(BF)
            s.pst[p, first + t, :, ls] = pb
            return acc + mm(s.vt[p, t], pb)

        acc = lax.fori_loop(0, nt, values, jnp.zeros((HD + 16, R), F32))
        inv = 1.0 / acc[64:72]
        s.linv[g, :, ls] = inv
        s.att[g, :, ls] = acc[0:64] * inv[0:1]

    pieces = [(p + 2 * blk, rc) for p in range(2) for rc in range(NR) for blk in range(2)]
    for piece in pieces[0:2]:
        attend(*piece)
    rwait(h_wp2, w2_cols(c * HB + WD + qs[1] * WP, WP))
    both_parts = pl.multiple_of(c * HB + WD + a * 2 * WP, 2 * WP)
    h_wp3 = rcopy(w2_cols(both_parts, 2 * WP), w2_cols(both_parts, 2 * WP), far)
    for piece in pieces[2:4]:
        attend(*piece)
    h_eos = gather_sib(h_eo2, s.eo)
    for piece in pieces[4:6]:
        attend(*piece)
    rwait(h_wp3, w2_cols(pl.multiple_of(c * HB + WD + (1 - a) * 2 * WP, 2 * WP), 2 * WP))
    for piece in pieces[6:8]:
        attend(*piece)
    for i in range(1, dp):
        rwait(h_wd[i], w2_rows(zfrom[i], lo, WD))
    h_w2s = rcopy(w2_cols(lo, HB), w2_cols(lo, HB), sib)

    def spread(dst, src, scale):
        def one(g, _):
            lanes = pl.ds(pl.multiple_of(g * 128, 128), 128)
            for k in range(K8):
                part = src[g, :, k * 128 : (k + 1) * 128]
                if scale is not None:
                    part = part * scale[k : k + 1, lanes]
                else:
                    part = part * 0.125
                s.acc1[k * HD : (k + 1) * HD, 0:128] = part
            for place in range(NE):
                acc = jnp.zeros((HD, 128), F32)
                for k in range(K8):
                    acc = jnp.where(
                        s.rtd[k : k + 1, lanes] == expert_at(place),
                        s.acc1[k * HD : (k + 1) * HD, 0:128],
                        acc,
                    )
                dst[place * HD : (place + 1) * HD, lanes] = acc.astype(BF)
            return 0

        lax.fori_loop(0, 4, one, 0)

    spread(s.at, s.att, s.gate)
    rwait(h_eos, zrows(s.eo, 1 - c, half))
    s.acc1[...] = s.tokd[...].astype(F32)

    def mix(i, _):
        rows = pl.ds(pl.multiple_of(i * 256, 256), 256)
        s.acc1[...] += mm_tn(s.at[rows, :], s.eo[rows, :])
        return 0

    lax.fori_loop(0, NE * HD // 256, mix, 0)
    mixed = s.acc1[...]
    s.mixed[...] = mixed
    ffn = rms(mixed)[0] * g1
    s.ffn[...] = ffn.astype(BF)
    s.ffnt[...] = ffn.T.astype(BF)
    rwait(h_cot, s.cotx)
    cot1 = mm(split, s.cotx[...])
    s.cotd[256:512, :] = cot1.astype(BF)
    s.cott[:, 0:256] = cot0.T.astype(BF)
    s.cott[:, 256:512] = cot1.T.astype(BF)
    s.acc2[...] = jnp.zeros((T, D), F32)
    rwait(h_w2s, s.w2.at[:, :, pl.ds(hi, HB)])

    FT = 256

    def feed(i, base_, keep):
        cols = pl.ds(pl.multiple_of(base_ + i * FT, FT), FT)
        part_cols = pl.ds(pl.multiple_of(i * FT, FT), FT)
        up = mm(s.ffn[...], s.w2[0, :, cols])
        sq = up * up
        th = jnp.tanh(0.79788456 * up * (1.0 + 0.044715 * sq))
        hid = (0.5 * up * (1.0 + th)).astype(BF)
        slope = 0.5 * (1.0 + th) + 0.5 * up * (1.0 - th * th) * (
            0.79788456 * (1.0 + 3 * 0.044715 * sq)
        )
        s.acc1[...] += mm_nt(hid, s.w2[1, :, cols])
        dup = (mm(s.cotd[...], s.w2[1, :, cols]) * slope).astype(BF)
        keep[0, :, part_cols] = mm(s.ffnt[...], dup).astype(BF)
        keep[1, :, part_cols] = mm(s.cott[...], hid).astype(BF)
        s.acc2[...] += mm_nt(dup, s.w2[0, :, cols])
        return 0

    lax.fori_loop(0, HB // FT, lambda i, _: feed(i, hi, s.gfh), 0)
    h_f1 = [rcopy(s.gfh.at[w], s.rf1.at[w], sib) for w in range(2)]
    lax.fori_loop(0, HB // FT, lambda i, _: feed(i, lo, s.gfl), 0)

    def both(x, y):
        return (x.astype(F32) + y.astype(F32)).astype(BF)

    def fold(sq):
        sq = jnp.sum(sq, axis=0, keepdims=True)
        out = sq[:, 0:128]
        for j in range(1, sq.shape[1] // 128):
            out = out + sq[:, j * 128 : (j + 1) * 128]
        return out

    done, squares = [], []
    quart = HB // 4
    keep2 = pl.multiple_of(a * 2 * quart, 2 * quart)
    give2 = pl.multiple_of((1 - a) * 2 * quart, 2 * quart)
    keep1 = pl.multiple_of(q * quart, quart)
    give1 = pl.multiple_of(qs[1] * quart, quart)
    place1 = pl.multiple_of(c * HB + keep1, quart)

    def feed_grad(w):
        own, total, one, two, three, out = (
            s.gfl.at[w], s.rf1.at[w], s.rfa.at[w], s.rfb.at[w], s.rfc, s.f2.at[w],
        )

        def pair(at, n):
            total[:, pl.ds(at, n)] = both(own[:, pl.ds(at, n)], total[:, pl.ds(at, n)])

        rwait(h_f1[w], total)
        pair(give2, 2 * quart)
        h = rcopy(total.at[:, pl.ds(give2, 2 * quart)], one, far)
        pair(keep2, 2 * quart)
        yield
        rwait(h, one)
        for at in (give1, keep1):
            inner = pl.multiple_of(at - keep2, quart)
            total[:, pl.ds(at, quart)] = both(
                total[:, pl.ds(at, quart)], one[:, pl.ds(inner, quart)]
            )
            if at is give1:
                h = rcopy(total.at[:, pl.ds(give1, quart)], two, near)
        yield
        rwait(h, two)
        total[:, pl.ds(keep1, quart)] = both(total[:, pl.ds(keep1, quart)], two[...])

        def zpart(i):
            return total.at[pl.ds(pl.multiple_of(i * shard, shard), shard), pl.ds(keep1, quart)]

        hz = [rcopy(zpart(zp[i][0]), three.at[i - 1, w], zp[i]) for i in range(1, dp)]
        yield
        acc = zpart(z)[...].astype(F32)
        for i in range(1, dp):
            rwait(hz[i - 1], three.at[i - 1, w])
            acc = acc + three[i - 1, w].astype(F32)
        acc = acc.astype(BF)
        out[:, pl.ds(place1, quart)] = acc
        acc = acc.astype(F32)
        squares.append(fold(acc * acc))
        h = rcopy(out.at[:, pl.ds(place1, quart)], out.at[:, pl.ds(place1, quart)], near)
        yield
        rwait(h, out.at[:, pl.ds(pl.multiple_of(c * HB + give1, quart), quart)])
        wide = out.at[:, pl.ds(pl.multiple_of(c * HB + keep2, 2 * quart), 2 * quart)]
        h = rcopy(wide, wide, far)
        yield
        rwait(h, out.at[:, pl.ds(pl.multiple_of(c * HB + give2, 2 * quart), 2 * quart)])
        h = rcopy(out.at[:, pl.ds(lo, HB)], out.at[:, pl.ds(lo, HB)], sib)
        yield
        rwait(h, out.at[:, pl.ds(hi, HB)])
        done.append(lcopy(out, f2o.at[w], 2 + w))
        yield

    def head_grad(src, total, one, two, full, part_, final, dst, sem):
        h = rcopy(zrows(src, 1 - c, half), total, sib)
        s.half_sent = h
        yield
        rwait(h, total)

        def pair(which):
            rows = pl.ds(pl.multiple_of(which * 2 * ER, 128), 2 * ER)
            wide = pl.ds(pl.multiple_of(c * half + which * 2 * ER, 128), 2 * ER)
            total[rows, :] = both(src[wide, :], total[rows, :])

        pair(1 - a)
        h = rcopy(zrows(total, 1 - a, 2 * ER), one, far)
        pair(a)
        yield
        rwait(h, one)
        for which in (1 - b, b):
            rows = pl.ds(pl.multiple_of((2 * a + which) * ER, ER), ER)
            total[rows, :] = both(total[rows, :], one[pl.ds(pl.multiple_of(which * ER, ER), ER), :])
            if which is not b:
                h = rcopy(zrows(total, qs[1], ER), two, near)
        yield
        rwait(h, two)
        full[0:ER, :] = both(total[pl.ds(pl.multiple_of(q * ER, ER), ER), :], two[...])
        if dp * pr > ER:
            full[ER:, :] = jnp.zeros((dp * pr - ER, D), BF)
        hz = [rcopy(zrows(full, zp[i][0], pr), part_.at[i - 1], zp[i]) for i in range(1, dp)]
        yield
        mine = pl.ds(pl.multiple_of(z * pr, pr), pr)
        acc = full[mine, :].astype(F32)
        for i in range(1, dp):
            rwait(hz[i - 1], part_.at[i - 1])
            acc = acc + part_[i - 1].astype(F32)
        acc = acc.astype(BF)
        final[mine, :] = acc
        acc = acc.astype(F32)
        squares.append(fold(acc * acc))
        hz = to_all_z(zrows(final, z, pr))
        yield
        for i in range(1, dp):
            rwait(hz[i], zrows(final, zfrom[i], pr))
        done.append(lcopy(final.at[pl.ds(0, ER)], dst, sem))
        yield

    chain = [feed_grad(0), feed_grad(1)]

    out = s.acc1[...].astype(BF)
    s.layx[...] = mm(join, out[256:512]).astype(BF)
    h_lay = rcopy(s.layx, s.layr, swap)
    s.ffn[0:256, :] = mm(join, out[0:256]).astype(BF)

    def rms_back(dn, gain, unit, inv):
        a = dn * gain
        return inv * (a - unit * jnp.mean(a * unit, axis=-1, keepdims=True)), jnp.sum(
            dn * unit, axis=0, keepdims=True
        )

    unit1, inv1 = rms(s.mixed[...])
    back, gain1 = rms_back(s.acc2[...], g1, unit1, inv1)
    s.gain[1:2, :] = gain1
    dmix = s.cotd[...].astype(F32) + back
    s.mixed[...] = dmix
    s.cott[...] = dmix.astype(BF)

    def out_rows(i, _):
        rows = pl.ds(pl.multiple_of(i * 256, 256), 256)
        s.big[rows, :] = mm_nt(s.eo[rows, :], s.cott[...])
        s.go[rows, :] = mm(s.at[rows, :], s.cott[...]).astype(BF)
        return 0

    lax.fori_loop(0, NE * HD // 256, out_rows, 0)
    chain.append(head_grad(s.go, s.ro1, s.ro2, s.ro3, s.xo, s.ro4, s.fo, foo, 4))
    next(chain[2])
    sent_o = s.half_sent
    next(chain[0])

    def heads_back(g, _):
        lanes = pl.ds(pl.multiple_of(g * 128, 128), 128)
        for k in range(K8):
            ks = slice(k * 128, (k + 1) * 128)
            da = pick(g, k)
            at = s.att[g, :, ks]
            s.dgate[k : k + 1, lanes] = jnp.sum(at * da, axis=0, keepdims=True)
            do = (da * (s.gate[k : k + 1, lanes] * s.linv[g, 0:1, ks])).astype(BF)
            s.dox[g, 64:128, ks] = do
            delta = -jnp.sum(do.astype(F32) * at, axis=0, keepdims=True)
            top = delta.astype(BF).astype(F32)
            s.dox[g, 0:16, ks] = jnp.where(
                row16 == 0, top, jnp.where(row16 == 1, delta - top, 0.0)
            ).astype(BF)
            s.dox[g, 16:64, ks] = jnp.zeros((48, 128), BF)
        return 0

    lax.fori_loop(0, 4, heads_back, 0)
    s.dkv[...] = jnp.zeros(s.dkv.shape, F32)

    left = lax.broadcasted_iota(jnp.int32, (256, 128), 1) < 64

    def attend_back(g, rc):
        blk, p = g // 2, g % 2
        nt, first = tiles[blk], base[blk]
        ls = slice(rc * R, (rc + 1) * R)

        def tile(t, acc):
            prob = s.pst[p, first + t, :, ls]
            dprob = mm(s.vx[p, t], s.dox[g, :, ls])
            ds = (prob.astype(F32) * dprob).astype(BF)
            kpart = mm_nt(ds, s.qx[g, :, ls])
            vpart = mm_nt(prob, s.dox[g, :, ls])
            s.dkv[p, t] += jnp.where(left, kpart * LN2, vpart)
            return acc + mm(s.kt[p, t], ds)

        s.att[g, :, ls] = lax.fori_loop(0, nt, tile, jnp.zeros((HD, R), F32))

    next(chain[1])
    next(chain[2])
    for piece in pieces[0:2]:
        attend_back(*piece)
    next(chain[0])
    for piece in pieces[2:4]:
        attend_back(*piece)
    next(chain[1])
    next(chain[2])
    for piece in pieces[4:6]:
        attend_back(*piece)
    next(chain[0])
    next(chain[2])
    for piece in pieces[6:8]:
        attend_back(*piece)
    next(chain[1])
    next(chain[2])
    sent(h_kvs)
    for m in (1, 2, 3):
        sent(h_kv[m])
    for dev in range(PL):
        sl = slot_of(dev)
        for side_, blk in enumerate((2 * dev, 15 - 2 * dev)):
            for p in range(2):
                s.kvb[sl, side_, p * 128 : (p + 1) * 128, :] = s.dkv[p, blk // 2, (blk % 2) * 128 : (blk % 2) * 128 + 128, :].astype(BF)
    h_k1 = rcopy(s.kvb.at[pl.ds((1 - c) * 4, 4)], s.rk1, sib)
    spread(s.at, s.att, None)
    rwait(h_k1, s.rk1)
    for i in range(4):
        s.rk1[i] = both(s.kvb[c * 4 + i], s.rk1[i])
    h_k2 = [None] + [rcopy(s.rk1.at[qs[m]], s.rk2.at[m - 1], chips[m]) for m in (1, 2, 3)]

    sent(sent_o)
    next(chain[0])

    def query_grad(i, _):
        rows = pl.ds(pl.multiple_of(i * 256, 256), 256)
        s.go[rows, :] = mm(s.at[rows, :], s.nd[...]).astype(BF)
        return 0

    lax.fori_loop(0, NE * HD // 256, query_grad, 0)
    chain.append(head_grad(s.go, s.rq1, s.rq2, s.rq3, s.xq, s.rq4, s.fq, fqo, 5))
    next(chain[3])
    next(chain[1])
    s.acc2[...] = jnp.zeros((T, D), F32)

    def slot_sum(i, _):
        rows = pl.ds(pl.multiple_of(i * 256, 256), 256)
        s.acc2[...] += mm_tn(s.at[rows, :], s.eq[rows, :])
        return 0

    lax.fori_loop(0, NE * HD // 256, slot_sum, 0)
    gate = s.gate[...]
    dch = gate * (s.dgate[...] - jnp.sum(gate * s.dgate[...], axis=0, keepdims=True))
    dlog = jnp.zeros((32, T), F32)
    for k in range(K8):
        dlog = dlog + jnp.where(row_e == s.rtd[k : k + 1, :], dch[k : k + 1, :], 0.0)
    dlog = dlog.astype(BF)
    s.acc2[...] += mm_tn(dlog, wrt)
    grt = mm(dlog, s.nd[...])

    next(chain[3])
    next(chain[0])
    for m in (1, 2, 3):
        rwait(h_k2[m], s.rk2.at[m - 1])
    for i in range(2):
        total = s.rk1[q, i].astype(F32)
        for m in (1, 2, 3):
            total = total + s.rk2[m - 1, i].astype(F32)
        s.dkvd[i * 256 : (i + 1) * 256, :] = total.astype(BF)
    dn = s.acc2[...] + mm_nt(s.dkvd[...], s.wkvf[...])
    unit0, inv0 = rms(s.tokd[...].astype(F32))
    back0, gain0 = rms_back(dn, g0, unit0, inv0)
    s.tbf[:, 0:512] = mm_tn(s.dkvd[...], s.nd[...])
    for j in range(4):
        js = slice(j * 128, (j + 1) * 128)
        s.tbf[j * 24 : (j + 1) * 24, 512:640] = grt[0:24, js]
        s.tbf[96 + j : 97 + j, 512:640] = gain0[:, js]
        s.tbf[100 + j : 101 + j, 512:640] = s.gain[1:2, js]
    s.tbf[104:128, 512:640] = jnp.zeros((24, 128), F32)
    s.tb[...] = s.tbf[...].astype(BF)
    h_t1 = rcopy(zrows(s.tb, 1 - c, 64), s.rt1, sib)
    next(chain[3])
    next(chain[1])

    grad = s.mixed[...] + back0
    sent(h_lay)
    s.layx[...] = mm(join, grad[256:512].astype(BF)).astype(BF)
    rwait(h_t1, s.rt1)
    s.tsm[...] = both(s.tb[pl.ds(pl.multiple_of(c * 64, 64), 64), :], s.rt1[...])
    h_t2 = [None] + [rcopy(zrows(s.tsm, qs[m], 16), s.rt2.at[m - 1], chips[m]) for m in (1, 2, 3)]
    h_tg = rcopy(s.layx, s.tgr, swap)
    top = grad[0:256].astype(BF)
    rest = (grad[0:256] - top.astype(F32)).astype(BF)
    s.acc1[0:256, :] = mm(join, top) + mm(join, rest)

    next(chain[3])
    next(chain[0])
    for m in (1, 2, 3):
        rwait(h_t2[m], s.rt2.at[m - 1])
    total = s.tsm[pl.ds(pl.multiple_of(q * 16, 16), 16), :].astype(F32)
    for m in (1, 2, 3):
        total = total + s.rt2[m - 1].astype(F32)
    s.rt3[z] = total.astype(BF)
    h_t3 = [None] + [rcopy(s.rt3.at[z], s.rt3.at[z], zp[i]) for i in range(1, dp)]
    next(chain[3])
    next(chain[1])
    for i in range(1, dp):
        rwait(h_t3[i], s.rt3.at[zfrom[i]])
    total = s.rt3[0].astype(F32)
    for i in range(1, dp):
        total = total + s.rt3[i].astype(F32)
    tail = total.astype(BF)
    s.tf[pl.ds(pl.multiple_of(slot * 16, 16), 16), :] = tail
    h_t4 = [None] + [
        rcopy(zrows(s.tf, slot, 16), zrows(s.tf, slot, 16), chips[m]) for m in (1, 2, 3)
    ]
    sq_t = fold(tail.astype(F32) * tail.astype(F32)) * (1.0 / dp)

    total = squares[0]
    for sq in squares[1:] + [sq_t]:
        total = total + sq
    squares = jnp.sum(total, axis=1, keepdims=True)
    s.mz[z] = jnp.where(row32 < 24, s.cnt[...], jnp.where(row32 == 24, squares, 0.0))
    h_m1 = [None] + [rcopy(s.mz.at[z], s.mz.at[z], zp[i]) for i in range(1, dp)]

    for m in (1, 2, 3):
        rwait(h_t4[m], zrows(s.tf, c * 4 + qs[m], 16))
    h_t5 = rcopy(zrows(s.tf, c, 64), zrows(s.tf, c, 64), sib)

    for i in range(1, dp):
        rwait(h_m1[i], s.mz.at[zfrom[i]])
    total = s.mz[0]
    for i in range(1, dp):
        total = total + s.mz[i]
    s.mq[e] = total
    h_m2 = [None] + [rcopy(s.mq.at[e], s.mq.at[e], plane[i]) for i in range(1, PL)]

    rwait(h_lay, s.layr)
    s.ffn[256:512, :] = s.layr[...]
    done.append(lcopy(s.ffn, lay, 0))
    rwait(h_tg, s.tgr)
    s.acc1[256:512, :] = s.tgr[...].astype(F32)
    done.append(lcopy(s.acc1, tg, 1))
    next(chain[0])
    next(chain[1])
    rwait(h_t5, zrows(s.tf, 1 - c, 64))
    s.acc2[:, 0:128] = s.tf[:, 0:512].astype(F32).T
    done.append(lcopy(s.tf.at[:, pl.ds(512, 128)], sideo, 8))
    done.append(lcopy(s.acc2.at[own_rows, pl.ds(0, 128)], kvo, 7))
    next(chain[2])
    next(chain[3])
    for i in range(1, PL):
        rwait(h_m2[i], s.mq.at[(e + PL - i) % PL])
    total = s.mq[0]
    for i in range(1, PL):
        total = total + s.mq[i]
    s.cnt[...] = total
    done.append(lcopy(s.cnt, msgo, 6))
    for d in done:
        d.wait()
    for d in sends:
        d.wait_send()
    assert count[0] <= copies_of(dp)


def adam_kernel(steps, *refs):
    (lay, tg, msg, upg, downg, qg, og, side, kvg) = refs[:9]
    params = [refs[9 + 3 * i : 12 + 3 * i] for i in range(7)]
    layo, tgo, counts, norm = refs[30:34]
    outs = [refs[34 + 3 * i : 37 + 3 * i] for i in range(7)]
    step = pl.program_id(0)
    total = jnp.sqrt(jnp.full((8, 128), msg[24, 0], F32))
    clip = (CLIP_LIMIT / jnp.maximum(total, CLIP_LIMIT))[0:1, 0:1]

    def update(k, g, rate, decay, at=Ellipsis):
        w, m, v = [r[at] for r in params[k]]
        g = g * clip
        m = BETA_FIRST * m + (1.0 - BETA_FIRST) * g
        v = BETA_SECOND * v + (1.0 - BETA_SECOND) * g * g
        mh = m * (1.0 / (1.0 - BETA_FIRST**ADAM_STEP))
        vh = v * (1.0 / (1.0 - BETA_SECOND**ADAM_STEP))
        outs[k][0][at] = w - rate * (mh / (jnp.sqrt(vh) + ADAM_EPS) + decay * w)
        outs[k][1][at] = m
        outs[k][2][at] = v

    @pl.when(step == 0)
    def _():
        norm[...] = total[0:1, 0:1]
        for i in range(NE):
            counts[i] = msg[i, 0].astype(jnp.int32)
        sd = side[...].astype(F32)
        for row in range(2):
            g = jnp.concatenate([sd[96 + 4 * row + j : 97 + 4 * row + j] for j in range(4)], axis=1)
            update(0, g, 0.7, 0.0, pl.ds(row, 1))
        g = jnp.concatenate([sd[j * NE : (j + 1) * NE] for j in range(4)], axis=1)
        update(1, g, 0.03, 0.1)

    layo[...] = lay[...]
    tgo[...] = tg[...]
    update(2, kvg[...], 0.06, 0.1)
    update(3, qg[...].astype(F32), 0.06, 0.1)
    update(4, og[...].astype(F32), 2.0, 0.1)
    update(5, upg[0].astype(F32), 0.06, 0.1)
    update(6, downg[0].astype(F32).T, 0.03, 0.1)


def on_device(tokens, cotangent, routes, group_batch, seq_lengths, *state):
    dp = lax.axis_size("dp")
    shard = D // dp
    state = list(state)
    for i in range(3):
        state[3 + i] = state[3 + i].T
        state[9 + i] = state[9 + i].transpose(0, 2, 1)
    gains, router, keyval, query, output, up, down = [state[3 * i] for i in range(7)]

    scr = []
    for item in scratch_list(dp).values():
        if item is None:
            scr.append(pltpu.SemaphoreType.DMA((copies_of(dp),)))
        elif len(item) == 1:
            scr.append(pltpu.SemaphoreType.DMA(item))
        else:
            scr.append(pltpu.VMEM(item[0], item[1]))
    routes_cols = routes.T
    vm = pl.BlockSpec(memory_space=pltpu.VMEM)
    sm = pl.BlockSpec(memory_space=pltpu.SMEM)
    hbm = pl.BlockSpec(memory_space=pl.ANY)
    outs = [
        jax.ShapeDtypeStruct((T, D), BF),
        jax.ShapeDtypeStruct((T, D), F32),
        jax.ShapeDtypeStruct((32, 128), F32),
        jax.ShapeDtypeStruct((2, shard, FF), BF),
        jax.ShapeDtypeStruct((ER, D), BF),
        jax.ShapeDtypeStruct((ER, D), BF),
        jax.ShapeDtypeStruct((128, 128), BF),
        jax.ShapeDtypeStruct((shard, 128), F32),
    ]

    def kernel(*refs):
        layer_kernel(dp, *refs)

    lay, tg, msg, f2, fq, fo, side, kvg = pl.pallas_call(
        kernel,
        out_shape=outs,
        in_specs=[vm] * 10 + [sm] * 2,
        out_specs=[hbm] * len(outs),
        scratch_shapes=scr,
        compiler_params=pltpu.CompilerParams(
            collective_id=0, has_side_effects=True, vmem_limit_bytes=64 * 2**20 - 2**17
        ),
        name="layer",
    )(
        tokens, cotangent, routes_cols, keyval, up, down, query, output, router, gains,
        group_batch, seq_lengths,
    )

    steps = min(4, shard // 16)
    rows = lambda i: (i, 0)
    middle = lambda i: (0, i, 0)
    blocks = [
        pl.BlockSpec((2, D), lambda i: (0, 0)),
        pl.BlockSpec((NE, D), lambda i: (0, 0)),
        pl.BlockSpec((shard // steps, 2 * HD), rows),
        pl.BlockSpec((LE, HD // steps, D), middle),
        pl.BlockSpec((LE, HD // steps, D), middle),
        pl.BlockSpec((shard // steps, FF), rows),
        pl.BlockSpec((FF // steps, shard), rows),
    ]
    each = [b for b in blocks for _ in range(3)]

    def update(*refs):
        adam_kernel(steps, *refs)

    result = list(pl.pallas_call(
        update,
        grid=(steps,),
        out_shape=[
            jax.ShapeDtypeStruct((T, D), BF),
            jax.ShapeDtypeStruct((T, D), F32),
            jax.ShapeDtypeStruct((NE,), jnp.int32),
            jax.ShapeDtypeStruct((1, 1), F32),
        ]
        + [jax.ShapeDtypeStruct(x.shape, F32) for x in state],
        in_specs=[
            pl.BlockSpec((T // steps, D), rows),
            pl.BlockSpec((T // steps, D), rows),
            sm,
            pl.BlockSpec((1, shard // steps, FF), middle),
            pl.BlockSpec((1, shard, FF // steps), lambda i: (1, 0, i)),
            pl.BlockSpec((LE, HD // steps, D), middle),
            pl.BlockSpec((LE, HD // steps, D), middle),
            pl.BlockSpec((128, 128), lambda i: (0, 0)),
            pl.BlockSpec((shard // steps, 2 * HD), rows),
        ]
        + each,
        out_specs=[pl.BlockSpec((T // steps, D), rows), pl.BlockSpec((T // steps, D), rows), sm, pl.BlockSpec((1, 1), lambda i: (0, 0))] + each,
        compiler_params=pltpu.CompilerParams(vmem_limit_bytes=63 * 2**20),
        name="adamw",
    )(lay, tg, msg, f2, f2, fq.reshape(LE, HD, D), fo.reshape(LE, HD, D), side, kvg, *state))
    result[3] = result[3].reshape(())
    for i in range(3):
        result[7 + i] = result[7 + i].T
        result[13 + i] = result[13 + i].transpose(0, 2, 1)
    return tuple(result)


def solution(mesh):
    tok = P(("dp", "expert"), None)
    dp0 = P("dp", None)
    ex0 = P("expert", None, None)
    dp1 = P(None, "dp")
    return jax.shard_map(
        on_device,
        mesh=mesh,
        in_specs=(tok,) * 3 + (P(),) * 8 + (dp0,) * 3 + (ex0,) * 6 + (dp0,) * 3 + (dp1,) * 3,
        out_specs=(tok,) * 2 + (P(),) * 8 + (dp0,) * 3 + (ex0,) * 6 + (dp0,) * 3 + (dp1,) * 3,
        check_vma=False,
    )
```

```python
import math

import jax
import jax.numpy as jnp
from jax import lax
from jax.experimental import pallas as pl
from jax.experimental.pallas import tpu as pltpu
from jax.sharding import PartitionSpec as P

ADAM_STEP = 10
NORM_EPS = 1e-06
BETA_FIRST = 0.9
BETA_SECOND = 0.999
ADAM_EPS = 1e-08
CLIP_LIMIT = 1.0
MASKED = -1e30
LOG2E = math.log2(math.e)
LN2 = math.log(2.0)
MESH = pl.DeviceIdType.MESH
BF = jnp.bfloat16
F32 = jnp.float32

T = 512
D = 512
FF = 2048
HD = 64
K8 = 8
NE = 24
PL = 8
LE = NE // PL
ER = LE * HD
HB = FF // 2


def mm(a, b):
    return jnp.dot(a, b, preferred_element_type=F32)


def mm_nt(a, b):
    return lax.dot_general(a, b, (((1,), (1,)), ((), ())), preferred_element_type=F32)


def mm_tn(a, b):
    return lax.dot_general(a, b, (((0,), (0,)), ((), ())), preferred_element_type=F32)


def expert_at(place):
    return LE * device_at(place // LE) + place % LE


def device_at(slot):
    c, a, b = slot // 4, slot // 2 % 2, slot % 2
    qx, qy = (a, b) if c == 0 else (b, a)
    return 4 * qy + 2 * qx + c


def slot_of(dev):
    c, qx, qy = dev % 2, dev // 2 % 2, dev // 4
    return 4 * c + (2 * qx + qy if c == 0 else 2 * qy + qx)


def piece_rows(dp):
    return -(-ER // (dp * 16)) * 16


def scratch_list(dp):
    shard = D // dp
    pr = piece_rows(dp)
    return dict(
        wkvf=((D, 2 * HD), BF),
        w2=((2, D, FF), BF),
        eq=((NE * HD, D), BF),
        eo=((NE * HD, D), BF),
        kvb=((PL, 2, 256, 128), BF),
        tokx=((256, D), BF),
        cotx=((256, D), BF),
        rtx=((8, 256), jnp.int32),
        rts=((8, 256), jnp.int32),
        wrt=((32, D), F32),
        tokd=((T, D), BF),
        cotd=((T, D), BF),
        cott=((D, T), BF),
        rtd=((8, T), jnp.int32),
        nd=((T, D), BF),
        gate=((8, T), F32),
        dgate=((8, T), F32),
        big=((NE * HD, T), F32),
        peak=((2, 9, 8, 1024), F32),
        at=((NE * HD, T), BF),
        qx=((4, 128, 1024), BF),
        dox=((4, 128, 1024), BF),
        att=((4, HD + 16, 1024), F32),
        top=((4, 8, 1024), F32),
        linv=((4, 8, 1024), F32),
        kx=((2, 8, 256, 128), BF),
        vx=((2, 8, 256, 128), BF),
        kt=((2, 8, HD, 256), BF),
        vt=((2, 8, HD + 16, 256), BF),
        pst=((2, 9, 256, 1024), BF),
        dkv=((2, 8, 256, 128), F32),
        mixed=((T, D), F32),
        ffn=((T, D), BF),
        ffnt=((D, T), BF),
        acc1=((T, D), F32),
        acc2=((T, D), F32),
        gfh=((2, D, HB), BF),
        gfl=((2, D, HB), BF),
        rf1=((2, D, HB), BF),
        rfa=((2, D, HB // 2), BF),
        rfb=((2, D, HB // 4), BF),
        rfc=((dp - 1, 2, shard, HB // 4), BF),
        f2=((2, shard, FF), BF),
        go=((NE * HD, D), BF),
        rq1=((NE * HD // 2, D), BF),
        ro1=((NE * HD // 2, D), BF),
        rq2=((2 * ER, D), BF),
        ro2=((2 * ER, D), BF),
        rq3=((ER, D), BF),
        ro3=((ER, D), BF),
        xq=((dp * pr, D), BF),
        xo=((dp * pr, D), BF),
        rq4=((dp - 1, pr, D), BF),
        ro4=((dp - 1, pr, D), BF),
        fq=((dp * pr, D), BF),
        fo=((dp * pr, D), BF),
        rk1=((4, 2, 256, 128), BF),
        rk2=((3, 2, 256, 128), BF),
        dkvd=((T, 128), BF),
        tbf=((128, 640), F32),
        tb=((128, 640), BF),
        rt1=((64, 640), BF),
        tsm=((64, 640), BF),
        rt2=((3, 16, 640), BF),
        rt3=((dp, 16, 640), BF),
        tf=((128, 640), BF),
        cnt=((32, 128), F32),
        mz=((dp, 32, 128), F32),
        mq=((PL, 32, 128), F32),
        layx=((256, D), BF),
        layr=((256, D), BF),
        tgr=((256, D), BF),
        gain=((8, D), F32),
        osem=(9,),
        ssem=None,
        rsem=None,
    )


def copies_of(dp):
    return 80 + 12 * dp


def layer_kernel(dp, *refs):
    shard = D // dp
    pr = piece_rows(dp)
    (tok, cot, routes, wkv, up, down, qw, ow, rw, gains, gbatch, lens) = refs[:12]
    (lay, tg, msgo, f2o, fqo, foo, sideo, kvo) = refs[12:20]
    names = list(scratch_list(dp))
    s = type("Scratch", (), dict(zip(names, refs[20:])))

    z = lax.axis_index("dp")
    e = lax.axis_index("expert")
    c = e % 2
    qx = e // 2 % 2
    qy = e // 4
    a = (1 - c) * qx + c * qy
    b = (1 - c) * qy + c * qx
    q = 2 * a + b

    def device(a_, b_):
        return (z, 4 * ((1 - c) * b_ + c * a_) + 2 * ((1 - c) * a_ + c * b_) + c)

    qs = [q, 2 * a + 1 - b, 2 * (1 - a) + b, 2 * (1 - a) + 1 - b]
    sib = (z, e + 1 - 2 * c)
    near, far = device(a, 1 - b), device(1 - a, b)
    chips = [None, near, far, device(1 - a, 1 - b)]
    swap = (z, 7 - e)
    zp = [None] + [((z + i) % dp, e) for i in range(1, dp)]
    zfrom = [None] + [(z + dp - i) % dp for i in range(1, dp)]
    slot = c * 4 + q
    plane = [sib] + [(z, (e + i) % PL) for i in range(1, PL)]

    count = [0]
    sends = []

    def rcopy(src, dst, peer):
        k = count[0]
        count[0] += 1
        d = pltpu.make_async_remote_copy(
            src_ref=src,
            dst_ref=dst,
            send_sem=s.ssem.at[k],
            recv_sem=s.rsem.at[k],
            device_id=peer,
            device_id_type=MESH,
        )
        d.start()
        sends.append(d)
        return (k, peer, d)

    def sent(handle):
        sends[:] = [d for d in sends if d is not handle[2]]
        handle[2].wait_send()

    def rwait(handle, dst):
        k, peer, _ = handle
        pltpu.make_async_remote_copy(
            src_ref=dst,
            dst_ref=dst,
            send_sem=s.ssem.at[k],
            recv_sem=s.rsem.at[k],
            device_id=peer,
            device_id_type=MESH,
        ).wait_recv()

    def lcopy(src, dst, k):
        d = pltpu.make_async_copy(src, dst, s.osem.at[k])
        d.start()
        return d

    bar = pltpu.get_barrier_semaphore()
    for peer in plane[1:] + zp[1:]:
        pl.semaphore_signal(bar, inc=1, device_id=peer, device_id_type=MESH)

    def zrows(ref, i, n):
        return ref.at[pl.ds(pl.multiple_of(i * n, n), n)]

    def turned(x):
        rows, cols = x.shape
        if cols % 128:
            x = jnp.concatenate([x, jnp.zeros((rows, 128 - cols % 128), x.dtype)], axis=1)
        return x.T[0:cols]

    lo = pl.multiple_of(c * HB, HB)
    hi = pl.multiple_of((1 - c) * HB, HB)
    ri = lax.broadcasted_iota(jnp.int32, (256, 256), 0)
    ci = lax.broadcasted_iota(jnp.int32, (256, 256), 1)
    split = jnp.where(ci == 2 * (ri % 128) + ri // 128, 1.0, 0.0).astype(BF)
    join = jnp.where(ri == 2 * (ci % 128) + ci // 128, 1.0, 0.0).astype(BF)
    own_rows = pl.ds(pl.multiple_of(z * shard, shard), shard)
    s.wkvf[own_rows, :] = wkv[...].astype(BF)
    rtt = routes[...].astype(F32).astype(BF)
    s.rtd[:, 0:256] = mm(rtt[:, 0:256], join).astype(jnp.int32)
    s.rts[...] = mm(rtt[:, 256:512], join).astype(jnp.int32)
    WD = HB // 2
    WP = (HB - WD) // 4
    part = pl.multiple_of(c * HB + WD + q * WP, WP)
    for at, n in ((lo, WD), (part, WP)):
        s.w2[0, own_rows, pl.ds(at, n)] = up[:, pl.ds(at, n)].astype(BF)
        s.w2[1, own_rows, pl.ds(at, n)] = turned(down[pl.ds(at, n), :]).astype(BF)

    def w2_rows(i, at, n):
        return s.w2.at[:, pl.ds(pl.multiple_of(i * shard, shard), shard), pl.ds(at, n)]

    def to_all_z(ref):
        return [None] + [rcopy(ref, ref, zp[i]) for i in range(1, dp)]
    pl.semaphore_wait(bar, PL - 1 + dp - 1)
    h_wkv = [None] + [
        rcopy(zrows(s.wkvf, z, shard), zrows(s.wkvf, z, shard), zp[i]) for i in range(1, dp)
    ]
    h_tok = rcopy(tok.at[pl.ds(256, 256)], s.tokx, swap)
    h_rt = rcopy(s.rts, s.rtx, swap)
    for i in range(LE):
        rows = pl.ds(pl.multiple_of(slot * ER + i * HD, HD), HD)
        s.eq[rows, :] = qw[i].astype(BF)
        s.eo[rows, :] = ow[i].astype(BF)
    own_eq = zrows(s.eq, slot, ER)
    own_eo = zrows(s.eo, slot, ER)
    h_eq1 = rcopy(own_eq, own_eq, near)
    h_wp1 = to_all_z(w2_rows(z, part, WP))
    h_wd = to_all_z(w2_rows(z, lo, WD))

    def gather_far(h, ref):
        rwait(h, zrows(ref, c * 4 + qs[1], ER))
        pair = zrows(ref, c * 2 + a, 2 * ER)
        return rcopy(pair, pair, far)

    def gather_sib(h, ref):
        rwait(h, zrows(ref, c * 2 + 1 - a, 2 * ER))
        mine = zrows(ref, c, 4 * ER)
        return rcopy(mine, mine, sib)

    def w2_cols(at, n):
        return s.w2.at[:, :, pl.ds(at, n)]

    s.wrt[0:NE, :] = rw[...]
    s.wrt[NE:32, :] = jnp.zeros((32 - NE, D), F32)

    g0 = gains[0:1, :]
    g1 = gains[1:2, :]

    def rms(x):
        inv = lax.rsqrt(jnp.mean(x * x, axis=-1, keepdims=True) + NORM_EPS)
        return x * inv, inv

    nat0 = mm(split, tok[0:256, :])
    nat1 = mm(split, tok[256:512, :])
    s.tokd[0:256, :] = nat0.astype(BF)
    n0 = (rms(nat0)[0] * g0).astype(BF)
    n1 = (rms(nat1)[0] * g0).astype(BF)
    s.nd[0:256, :] = n0
    cot0 = mm(split, cot[0:256, :])
    s.cotd[0:256, :] = cot0.astype(BF)

    for i in range(1, dp):
        rwait(h_wkv[i], zrows(s.wkvf, zfrom[i], shard))
    kv0 = mm(n0, s.wkvf[...]).astype(BF)
    kv1 = mm(n1, s.wkvf[...]).astype(BF)
    for p in range(2):
        s.kvb[slot, p, 0:128, :] = kv0[p * 128 : (p + 1) * 128]
        s.kvb[slot, p, 128:256, :] = kv1[p * 128 : (p + 1) * 128]
    h_kv = [None] + [rcopy(s.kvb.at[slot], s.kvb.at[slot], chips[m]) for m in (1, 2, 3)]
    h_eq2 = gather_far(h_eq1, s.eq)

    rwait(h_tok, s.tokx)
    rwait(h_rt, s.rtx)
    sw = mm(split, s.tokx[...])
    s.tokd[256:512, :] = sw.astype(BF)
    s.nd[256:512, :] = (rms(sw)[0] * g0).astype(BF)
    s.rtd[:, 256:512] = s.rtx[...]

    wrt = s.wrt[...].astype(BF)
    bm1 = gbatch[z] - 1
    is2 = (4 - gbatch[z]) // 2

    def seq_pos(r):
        return r & bm1, (r >> 1) * is2 + (r >> 2) * (1 - is2)

    def limit_of(index):
        out = jnp.zeros(index.shape, jnp.int32)
        for i in range(4):
            out = jnp.where(index == i, lens[z, i], out)
        return out

    block = [2 * e, 15 - 2 * e]
    lanes128 = lax.broadcasted_iota(jnp.int32, (16, 128), 1)
    row16 = lax.broadcasted_iota(jnp.int32, (16, 128), 0)
    row32 = lax.broadcasted_iota(jnp.int32, (32, 128), 0)

    logits = mm_nt(wrt, s.nd[...])
    row_e = lax.broadcasted_iota(jnp.int32, (32, T), 0)
    chosen = jnp.concatenate(
        [
            jnp.sum(jnp.where(row_e == s.rtd[k : k + 1, :], logits, 0.0), axis=0, keepdims=True)
            for k in range(K8)
        ],
        axis=0,
    )
    ex = jnp.exp(chosen - jnp.max(chosen, axis=0, keepdims=True))
    s.gate[...] = ex / jnp.sum(ex, axis=0, keepdims=True)

    counts = jnp.zeros((32, 128), F32)
    for g in range(4):
        blk, p = g // 2, g % 2
        row = 2 * (block[blk] * 128 + lanes128) + p
        seq, pos = seq_pos(row)
        live = (pos < limit_of(seq))[0:1, :].astype(F32)
        for k in range(K8):
            counts = counts + jnp.where(
                row32 == s.rtd[k : k + 1, g * 128 : (g + 1) * 128], live, 0.0
            )
        feat = jnp.where(seq == row16, 1.0, 0.0).astype(BF)
        s.qx[g, 64:80, :] = jnp.concatenate([feat] * K8, axis=1)
        s.qx[g, 80:128, :] = jnp.zeros((48, 1024), BF)
    s.cnt[...] = jnp.broadcast_to(jnp.sum(counts, axis=1, keepdims=True), (32, 128))

    half = NE * HD // 2
    h_eqs = gather_sib(h_eq2, s.eq)
    for m in (1, 2, 3):
        rwait(h_kv[m], s.kvb.at[c * 4 + qs[m]])
    h_kvs = rcopy(s.kvb.at[pl.ds(c * 4, 4)], s.kvb.at[pl.ds(c * 4, 4)], sib)
    rwait(h_eqs, zrows(s.eq, 1 - c, half))

    def query_rows(i, _):
        rows = pl.ds(pl.multiple_of(i * 256, 256), 256)
        s.big[rows, :] = mm_nt(s.eq[rows, :], s.nd[...])
        return 0

    lax.fori_loop(0, NE * HD // 256, query_rows, 0)

    def pick(g, k):
        lanes = pl.ds(pl.multiple_of(g * 128, 128), 128)
        rk = s.rtd[k : k + 1, lanes]
        acc = jnp.zeros((HD, 128), F32)
        for place in range(NE):
            acc = jnp.where(rk == expert_at(place), s.big[place * HD : (place + 1) * HD, lanes], acc)
        return acc

    def choose(g, _):
        for k in range(K8):
            s.qx[g, 0:64, k * 128 : (k + 1) * 128] = (pick(g, k) * (0.125 * LOG2E)).astype(BF)
        return 0

    lax.fori_loop(0, 4, choose, 0)

    h_eo1 = rcopy(own_eo, own_eo, near)
    rwait(h_kvs, s.kvb.at[pl.ds((1 - c) * 4, 4)])
    krow = lax.broadcasted_iota(jnp.int32, (256, 128), 0)
    klane = lax.broadcasted_iota(jnp.int32, (256, 128), 1)
    for t in range(8):
        for p in range(2):
            kv = s.kvb[slot_of(t), p].astype(F32)
            seq, pos = seq_pos(2 * (t * 256 + krow) + p)
            col = klane - 64
            shown = (seq == col) & (pos < limit_of(col))
            feat = jnp.where(shown | (col > 3), 0.0, MASKED)
            s.kx[p, t] = jnp.where(col < 0, kv, feat).astype(BF)
            s.vx[p, t] = jnp.where(col >= 0, kv, jnp.where(klane < 2, 1.0, 0.0)).astype(BF)
            kvt = kv.T
            s.kt[p, t] = kvt[0:64].astype(BF)
            s.vt[p, t, 0:64, :] = kvt[64:128].astype(BF)
            s.vt[p, t, 64:80, :] = jnp.ones((16, 256), BF)

    turn = e + 1
    below = lax.broadcasted_iota(jnp.int32, (256, 128), 0) - lax.broadcasted_iota(
        jnp.int32, (256, 128), 1
    )
    s.att[...] = jnp.zeros(s.att.shape, F32)
    s.top[...] = jnp.full(s.top.shape, MASKED, F32)

    def place_of(i):
        blk = jnp.where(i >= turn, 1, 0)
        return blk * 2, i - blk * turn

    def attend(i, _):
        g0_, t = place_of(i)
        visible = below <= jnp.where(i == turn - 1, 0, jnp.where(i == 8, 128, 256))
        visible = jnp.concatenate([visible] * K8, axis=1)
        both_p = range(2)
        scs = [jnp.where(visible, mm(s.kx[p, t], s.qx[g0_ + p]), MASKED) for p in both_p]
        tops = [jnp.max(jnp.max(x.reshape(32, 8, 1024), axis=0), axis=0, keepdims=True) for x in scs]
        olds = [s.top[g0_ + p, 0:1, :] for p in both_p]
        news = [jnp.maximum(old, jnp.ceil(x)) for old, x in zip(olds, tops)]
        pbs = [jnp.exp2(sc - new).astype(BF) for sc, new in zip(scs, news)]
        outs = [mm(s.vt[p, t], pbs[p]) for p in both_p]
        for p in both_p:
            s.att[g0_ + p] = s.att[g0_ + p] * jnp.exp2(olds[p] - news[p]) + outs[p]
            s.pst[p, i] = pbs[p]
            s.peak[p, i] = jnp.broadcast_to(news[p], (8, 1024))
            s.top[g0_ + p] = jnp.broadcast_to(news[p], (8, 1024))
        return 0

    lax.fori_loop(0, 3, attend, 0)
    h_eo2 = gather_far(h_eo1, s.eo)
    for i in range(1, dp):
        rwait(h_wp1[i], w2_rows(zfrom[i], part, WP))
    h_wp2 = rcopy(w2_cols(part, WP), w2_cols(part, WP), near)
    lax.fori_loop(3, 5, attend, 0)
    rwait(h_wp2, w2_cols(c * HB + WD + qs[1] * WP, WP))
    both_parts = pl.multiple_of(c * HB + WD + a * 2 * WP, 2 * WP)
    h_wp3 = rcopy(w2_cols(both_parts, 2 * WP), w2_cols(both_parts, 2 * WP), far)
    h_cot = rcopy(cot.at[pl.ds(256, 256)], s.cotx, swap)
    lax.fori_loop(5, 7, attend, 0)
    h_eos = gather_sib(h_eo2, s.eo)
    lax.fori_loop(7, 9, attend, 0)
    for g in range(4):
        inv = 1.0 / s.att[g, 64:72, :]
        s.linv[g] = inv
        s.att[g, 0:64, :] = s.att[g, 0:64, :] * inv[0:1]
    for i in range(1, dp):
        rwait(h_wd[i], w2_rows(zfrom[i], lo, WD))
    h_w2s = [rcopy(w2_cols(lo, WD), w2_cols(lo, WD), sib)]
    rwait(h_wp3, w2_cols(pl.multiple_of(c * HB + WD + (1 - a) * 2 * WP, 2 * WP), 2 * WP))
    rest = pl.multiple_of(lo + WD, WD)
    h_w2s.append(rcopy(w2_cols(rest, HB - WD), w2_cols(rest, HB - WD), sib))
    def spread(dst, src, scale):
        def one(g, _):
            lanes = pl.ds(pl.multiple_of(g * 128, 128), 128)
            for k in range(K8):
                part = src[g, 0:HD, k * 128 : (k + 1) * 128]
                if scale is not None:
                    part = part * scale[k : k + 1, lanes]
                else:
                    part = part * 0.125
                s.acc1[k * HD : (k + 1) * HD, 0:128] = part
            for place in range(NE):
                acc = jnp.zeros((HD, 128), F32)
                for k in range(K8):
                    acc = jnp.where(
                        s.rtd[k : k + 1, lanes] == expert_at(place),
                        s.acc1[k * HD : (k + 1) * HD, 0:128],
                        acc,
                    )
                dst[place * HD : (place + 1) * HD, lanes] = acc.astype(BF)
            return 0

        lax.fori_loop(0, 4, one, 0)

    spread(s.at, s.att, s.gate)
    rwait(h_eos, zrows(s.eo, 1 - c, half))
    s.acc1[...] = s.tokd[...].astype(F32)

    def mix(i, _):
        rows = pl.ds(pl.multiple_of(i * 256, 256), 256)
        s.acc1[...] += mm_tn(s.at[rows, :], s.eo[rows, :])
        return 0

    lax.fori_loop(0, NE * HD // 256, mix, 0)
    mixed = s.acc1[...]
    s.mixed[...] = mixed
    ffn = rms(mixed)[0] * g1
    s.ffn[...] = ffn.astype(BF)
    s.ffnt[...] = ffn.T.astype(BF)
    rwait(h_cot, s.cotx)
    cot1 = mm(split, s.cotx[...])
    s.cotd[256:512, :] = cot1.astype(BF)
    s.cott[:, 0:256] = cot0.T.astype(BF)
    s.cott[:, 256:512] = cot1.T.astype(BF)
    s.acc2[...] = jnp.zeros((T, D), F32)
    rwait(h_w2s[0], w2_cols(hi, WD))
    rwait(h_w2s[1], w2_cols(pl.multiple_of(hi + WD, WD), HB - WD))

    FT = 256

    def feed(i, base_, keep):
        cols = pl.ds(pl.multiple_of(base_ + i * FT, FT), FT)
        part_cols = pl.ds(pl.multiple_of(i * FT, FT), FT)
        up = mm(s.ffn[...], s.w2[0, :, cols])
        sq = up * up
        th = jnp.tanh(0.79788456 * up * (1.0 + 0.044715 * sq))
        hid = (0.5 * up * (1.0 + th)).astype(BF)
        slope = 0.5 * (1.0 + th) + 0.5 * up * (1.0 - th * th) * (
            0.79788456 * (1.0 + 3 * 0.044715 * sq)
        )
        s.acc1[...] += mm_nt(hid, s.w2[1, :, cols])
        dup = (mm(s.cotd[...], s.w2[1, :, cols]) * slope).astype(BF)
        keep[0, :, part_cols] = mm(s.ffnt[...], dup).astype(BF)
        keep[1, :, part_cols] = mm(s.cott[...], hid).astype(BF)
        s.acc2[...] += mm_nt(dup, s.w2[0, :, cols])
        return 0

    lax.fori_loop(0, HB // FT, lambda i, _: feed(i, hi, s.gfh), 0)
    h_f1 = [rcopy(s.gfh.at[w], s.rf1.at[w], sib) for w in range(2)]
    lax.fori_loop(0, HB // FT, lambda i, _: feed(i, lo, s.gfl), 0)

    def both(x, y):
        return (x.astype(F32) + y.astype(F32)).astype(BF)

    def fold(sq):
        sq = jnp.sum(sq, axis=0, keepdims=True)
        out = sq[:, 0:128]
        for j in range(1, sq.shape[1] // 128):
            out = out + sq[:, j * 128 : (j + 1) * 128]
        return out

    done, squares = [], []
    quart = HB // 4
    keep2 = pl.multiple_of(a * 2 * quart, 2 * quart)
    give2 = pl.multiple_of((1 - a) * 2 * quart, 2 * quart)
    keep1 = pl.multiple_of(q * quart, quart)
    give1 = pl.multiple_of(qs[1] * quart, quart)
    place1 = pl.multiple_of(c * HB + keep1, quart)

    def feed_grad(w):
        own, total, one, two, three, out = (
            s.gfl.at[w], s.rf1.at[w], s.rfa.at[w], s.rfb.at[w], s.rfc, s.f2.at[w],
        )

        def pair(at, n):
            total[:, pl.ds(at, n)] = both(own[:, pl.ds(at, n)], total[:, pl.ds(at, n)])

        rwait(h_f1[w], total)
        pair(give2, 2 * quart)
        h = rcopy(total.at[:, pl.ds(give2, 2 * quart)], one, far)
        pair(keep2, 2 * quart)
        yield
        rwait(h, one)
        for at in (give1, keep1):
            inner = pl.multiple_of(at - keep2, quart)
            total[:, pl.ds(at, quart)] = both(
                total[:, pl.ds(at, quart)], one[:, pl.ds(inner, quart)]
            )
            if at is give1:
                h = rcopy(total.at[:, pl.ds(give1, quart)], two, near)
        yield
        rwait(h, two)
        total[:, pl.ds(keep1, quart)] = both(total[:, pl.ds(keep1, quart)], two[...])

        def zpart(i):
            return total.at[pl.ds(pl.multiple_of(i * shard, shard), shard), pl.ds(keep1, quart)]

        hz = [rcopy(zpart(zp[i][0]), three.at[i - 1, w], zp[i]) for i in range(1, dp)]
        yield
        acc = zpart(z)[...].astype(F32)
        for i in range(1, dp):
            rwait(hz[i - 1], three.at[i - 1, w])
            acc = acc + three[i - 1, w].astype(F32)
        acc = acc.astype(BF)
        out[:, pl.ds(place1, quart)] = acc
        acc = acc.astype(F32)
        squares.append(fold(acc * acc))
        h = rcopy(out.at[:, pl.ds(place1, quart)], out.at[:, pl.ds(place1, quart)], near)
        yield
        rwait(h, out.at[:, pl.ds(pl.multiple_of(c * HB + give1, quart), quart)])
        wide = out.at[:, pl.ds(pl.multiple_of(c * HB + keep2, 2 * quart), 2 * quart)]
        h = rcopy(wide, wide, far)
        yield
        rwait(h, out.at[:, pl.ds(pl.multiple_of(c * HB + give2, 2 * quart), 2 * quart)])
        h = rcopy(out.at[:, pl.ds(lo, HB)], out.at[:, pl.ds(lo, HB)], sib)
        yield
        rwait(h, out.at[:, pl.ds(hi, HB)])
        done.append(lcopy(out, f2o.at[w], 2 + w))
        yield

    def head_grad(src, total, one, two, full, part_, final, dst, sem):
        h = rcopy(zrows(src, 1 - c, half), total, sib)
        s.half_sent = h
        yield
        rwait(h, total)

        def pair(which):
            rows = pl.ds(pl.multiple_of(which * 2 * ER, 128), 2 * ER)
            wide = pl.ds(pl.multiple_of(c * half + which * 2 * ER, 128), 2 * ER)
            total[rows, :] = both(src[wide, :], total[rows, :])

        pair(1 - a)
        h = rcopy(zrows(total, 1 - a, 2 * ER), one, far)
        pair(a)
        yield
        rwait(h, one)
        for which in (1 - b, b):
            rows = pl.ds(pl.multiple_of((2 * a + which) * ER, ER), ER)
            total[rows, :] = both(total[rows, :], one[pl.ds(pl.multiple_of(which * ER, ER), ER), :])
            if which is not b:
                h = rcopy(zrows(total, qs[1], ER), two, near)
        yield
        rwait(h, two)
        full[0:ER, :] = both(total[pl.ds(pl.multiple_of(q * ER, ER), ER), :], two[...])
        if dp * pr > ER:
            full[ER:, :] = jnp.zeros((dp * pr - ER, D), BF)
        hz = [rcopy(zrows(full, zp[i][0], pr), part_.at[i - 1], zp[i]) for i in range(1, dp)]
        yield
        mine = pl.ds(pl.multiple_of(z * pr, pr), pr)
        acc = full[mine, :].astype(F32)
        for i in range(1, dp):
            rwait(hz[i - 1], part_.at[i - 1])
            acc = acc + part_[i - 1].astype(F32)
        acc = acc.astype(BF)
        final[mine, :] = acc
        acc = acc.astype(F32)
        squares.append(fold(acc * acc))
        hz = to_all_z(zrows(final, z, pr))
        yield
        for i in range(1, dp):
            rwait(hz[i], zrows(final, zfrom[i], pr))
        done.append(lcopy(final.at[pl.ds(0, ER)], dst, sem))
        yield

    chain = [feed_grad(0), feed_grad(1)]
    next(chain[0])
    next(chain[1])

    out = s.acc1[...].astype(BF)
    s.layx[...] = mm(join, out[256:512]).astype(BF)
    s.ffn[0:256, :] = mm(join, out[0:256]).astype(BF)

    def rms_back(dn, gain, unit, inv):
        a = dn * gain
        return inv * (a - unit * jnp.mean(a * unit, axis=-1, keepdims=True)), jnp.sum(
            dn * unit, axis=0, keepdims=True
        )

    unit1, inv1 = rms(s.mixed[...])
    back, gain1 = rms_back(s.acc2[...], g1, unit1, inv1)
    s.gain[1:2, :] = gain1
    dmix = s.cotd[...].astype(F32) + back
    s.mixed[...] = dmix
    s.cott[...] = dmix.astype(BF)

    def out_rows(i, _):
        rows = pl.ds(pl.multiple_of(i * 256, 256), 256)
        s.big[rows, :] = mm_nt(s.eo[rows, :], s.cott[...])
        s.go[rows, :] = mm(s.at[rows, :], s.cott[...]).astype(BF)
        return 0

    lax.fori_loop(0, NE * HD // 256, out_rows, 0)
    chain.append(head_grad(s.go, s.ro1, s.ro2, s.ro3, s.xo, s.ro4, s.fo, foo, 4))
    next(chain[2])
    sent_o = s.half_sent

    def heads_back(g, _):
        lanes = pl.ds(pl.multiple_of(g * 128, 128), 128)
        for k in range(K8):
            ks = slice(k * 128, (k + 1) * 128)
            da = pick(g, k)
            at = s.att[g, 0:HD, ks]
            s.dgate[k : k + 1, lanes] = jnp.sum(at * da, axis=0, keepdims=True)
            do = (da * (s.gate[k : k + 1, lanes] * s.linv[g, 0:1, ks])).astype(BF)
            s.dox[g, 64:128, ks] = do
            delta = -jnp.sum(do.astype(F32) * at, axis=0, keepdims=True)
            top = delta.astype(BF).astype(F32)
            s.dox[g, 0:16, ks] = jnp.where(
                row16 == 0, top, jnp.where(row16 == 1, delta - top, 0.0)
            ).astype(BF)
            s.dox[g, 16:64, ks] = jnp.zeros((48, 128), BF)
        return 0

    lax.fori_loop(0, 4, heads_back, 0)
    s.dkv[...] = jnp.zeros(s.dkv.shape, F32)

    left = lax.broadcasted_iota(jnp.int32, (256, 128), 1) < 64

    s.att[...] = jnp.zeros(s.att.shape, F32)

    def attend_back(i, _):
        g0_, t = place_of(i)
        both_p = range(2)
        scales = [jnp.exp2(s.peak[p, i, 0:1, :] - s.top[g0_ + p, 0:1, :]) for p in both_p]
        doxs = [(s.dox[g0_ + p].astype(F32) * scales[p]).astype(BF) for p in both_p]
        dprobs = [mm(s.vx[p, t], doxs[p]) for p in both_p]
        vparts = [mm_nt(s.pst[p, i], doxs[p]) for p in both_p]
        dss = [(s.pst[p, i].astype(F32) * dprobs[p]).astype(BF) for p in both_p]
        kparts = [mm_nt(dss[p], s.qx[g0_ + p]) for p in both_p]
        dqs = [mm(s.kt[p, t], dss[p]) for p in both_p]
        for p in both_p:
            s.dkv[p, t] += jnp.where(left, kparts[p] * LN2, vparts[p])
            s.att[g0_ + p, 0:HD, :] += dqs[p]
        return 0

    next(chain[2])
    lax.fori_loop(0, 3, attend_back, 0)
    next(chain[0])
    lax.fori_loop(3, 5, attend_back, 0)
    next(chain[1])
    lax.fori_loop(5, 7, attend_back, 0)
    next(chain[2])
    next(chain[0])
    lax.fori_loop(7, 9, attend_back, 0)
    next(chain[1])
    h_lay = rcopy(s.layx, s.layr, swap)
    sent(h_kvs)
    for m in (1, 2, 3):
        sent(h_kv[m])
    for dev in range(PL):
        sl = slot_of(dev)
        for side_, blk in enumerate((2 * dev, 15 - 2 * dev)):
            for p in range(2):
                s.kvb[sl, side_, p * 128 : (p + 1) * 128, :] = s.dkv[p, blk // 2, (blk % 2) * 128 : (blk % 2) * 128 + 128, :].astype(BF)
    h_k1 = rcopy(s.kvb.at[pl.ds((1 - c) * 4, 4)], s.rk1, sib)
    spread(s.at, s.att, None)
    next(chain[0])
    rwait(h_k1, s.rk1)
    for i in range(4):
        s.rk1[i] = both(s.kvb[c * 4 + i], s.rk1[i])
    h_k2 = [None] + [rcopy(s.rk1.at[qs[m]], s.rk2.at[m - 1], chips[m]) for m in (1, 2, 3)]

    next(chain[2])
    sent(sent_o)

    def query_grad(i, start):
        rows = pl.ds(pl.multiple_of(start + i * 256, 256), 256)
        s.go[rows, :] = mm(s.at[rows, :], s.nd[...]).astype(BF)
        return start

    lax.fori_loop(0, half // 256, query_grad, (1 - c) * half)
    chain.append(head_grad(s.go, s.rq1, s.rq2, s.rq3, s.xq, s.rq4, s.fq, fqo, 5))
    next(chain[3])
    lax.fori_loop(0, half // 256, lambda i, _: query_grad(i, c * half) * 0, 0)
    s.acc2[...] = jnp.zeros((T, D), F32)

    def slot_sum(i, _):
        rows = pl.ds(pl.multiple_of(i * 256, 256), 256)
        s.acc2[...] += mm_tn(s.at[rows, :], s.eq[rows, :])
        return 0

    lax.fori_loop(0, NE * HD // 256, slot_sum, 0)
    gate = s.gate[...]
    dch = gate * (s.dgate[...] - jnp.sum(gate * s.dgate[...], axis=0, keepdims=True))
    dlog = jnp.zeros((32, T), F32)
    for k in range(K8):
        dlog = dlog + jnp.where(row_e == s.rtd[k : k + 1, :], dch[k : k + 1, :], 0.0)
    dlog = dlog.astype(BF)
    s.acc2[...] += mm_tn(dlog, wrt)
    grt = mm(dlog, s.nd[...])

    next(chain[3])
    next(chain[0])
    next(chain[1])
    for m in (1, 2, 3):
        rwait(h_k2[m], s.rk2.at[m - 1])
    for i in range(2):
        total = s.rk1[q, i].astype(F32)
        for m in (1, 2, 3):
            total = total + s.rk2[m - 1, i].astype(F32)
        s.dkvd[i * 256 : (i + 1) * 256, :] = total.astype(BF)
    dn = s.acc2[...] + mm_nt(s.dkvd[...], s.wkvf[...])
    unit0, inv0 = rms(s.tokd[...].astype(F32))
    back0, gain0 = rms_back(dn, g0, unit0, inv0)
    s.tbf[:, 0:512] = mm_tn(s.dkvd[...], s.nd[...])
    for j in range(4):
        js = slice(j * 128, (j + 1) * 128)
        s.tbf[j * 24 : (j + 1) * 24, 512:640] = grt[0:24, js]
        s.tbf[96 + j : 97 + j, 512:640] = gain0[:, js]
        s.tbf[100 + j : 101 + j, 512:640] = s.gain[1:2, js]
    s.tbf[104:128, 512:640] = jnp.zeros((24, 128), F32)
    s.tb[...] = s.tbf[...].astype(BF)
    h_t1 = rcopy(zrows(s.tb, 1 - c, 64), s.rt1, sib)
    next(chain[0])
    next(chain[2])
    next(chain[3])
    rwait(h_t1, s.rt1)
    s.tsm[...] = both(s.tb[pl.ds(pl.multiple_of(c * 64, 64), 64), :], s.rt1[...])
    h_t2 = [None] + [rcopy(zrows(s.tsm, qs[m], 16), s.rt2.at[m - 1], chips[m]) for m in (1, 2, 3)]
    grad = s.mixed[...] + back0
    sent(h_lay)
    s.layx[...] = mm(join, grad[256:512].astype(BF)).astype(BF)
    top = grad[0:256].astype(BF)
    rest = (grad[0:256] - top.astype(F32)).astype(BF)
    s.acc1[0:256, :] = mm(join, top) + mm(join, rest)
    next(chain[1])
    next(chain[3])
    for m in (1, 2, 3):
        rwait(h_t2[m], s.rt2.at[m - 1])
    total = s.tsm[pl.ds(pl.multiple_of(q * 16, 16), 16), :].astype(F32)
    for m in (1, 2, 3):
        total = total + s.rt2[m - 1].astype(F32)
    s.rt3[z] = total.astype(BF)
    h_t3 = [None] + [rcopy(s.rt3.at[z], s.rt3.at[z], zp[i]) for i in range(1, dp)]
    h_tg = rcopy(s.layx, s.tgr, swap)
    next(chain[1])
    for i in range(1, dp):
        rwait(h_t3[i], s.rt3.at[zfrom[i]])
    total = s.rt3[0].astype(F32)
    for i in range(1, dp):
        total = total + s.rt3[i].astype(F32)
    tail = total.astype(BF)
    s.tf[pl.ds(pl.multiple_of(slot * 16, 16), 16), :] = tail
    h_t4 = [None] + [
        rcopy(zrows(s.tf, slot, 16), zrows(s.tf, slot, 16), chips[m]) for m in (1, 2, 3)
    ]
    next(chain[3])
    sq_t = fold(tail.astype(F32) * tail.astype(F32)) * (1.0 / dp)

    total = squares[0]
    for sq in squares[1:] + [sq_t]:
        total = total + sq
    squares = jnp.sum(total, axis=1, keepdims=True)
    s.mz[z] = jnp.where(row32 < 24, s.cnt[...], jnp.where(row32 == 24, squares, 0.0))
    h_m1 = [None] + [rcopy(s.mz.at[z], s.mz.at[z], zp[i]) for i in range(1, dp)]

    for m in (1, 2, 3):
        rwait(h_t4[m], zrows(s.tf, c * 4 + qs[m], 16))
    h_t5 = rcopy(zrows(s.tf, c, 64), zrows(s.tf, c, 64), sib)

    for i in range(1, dp):
        rwait(h_m1[i], s.mz.at[zfrom[i]])
    total = s.mz[0]
    for i in range(1, dp):
        total = total + s.mz[i]
    s.mq[e] = total
    h_m2 = [None] + [rcopy(s.mq.at[e], s.mq.at[e], plane[i]) for i in range(1, PL)]

    rwait(h_lay, s.layr)
    s.ffn[256:512, :] = s.layr[...]
    done.append(lcopy(s.ffn, lay, 0))
    rwait(h_tg, s.tgr)
    s.acc1[256:512, :] = s.tgr[...].astype(F32)
    done.append(lcopy(s.acc1, tg, 1))
    next(chain[0])
    next(chain[1])
    rwait(h_t5, zrows(s.tf, 1 - c, 64))
    s.acc2[:, 0:128] = s.tf[:, 0:512].astype(F32).T
    done.append(lcopy(s.tf.at[:, pl.ds(512, 128)], sideo, 8))
    done.append(lcopy(s.acc2.at[own_rows, pl.ds(0, 128)], kvo, 7))
    next(chain[2])
    next(chain[3])
    for i in range(1, PL):
        rwait(h_m2[i], s.mq.at[(e + PL - i) % PL])
    total = s.mq[0]
    for i in range(1, PL):
        total = total + s.mq[i]
    s.cnt[...] = total
    done.append(lcopy(s.cnt, msgo, 6))
    for d in done:
        d.wait()
    for d in sends:
        d.wait_send()
    assert count[0] <= copies_of(dp)


def adam_kernel(steps, *refs):
    (lay, tg, msg, upg, downg, qg, og, side, kvg) = refs[:9]
    params = [refs[9 + 3 * i : 12 + 3 * i] for i in range(7)]
    layo, tgo, counts, norm = refs[30:34]
    outs = [refs[34 + 3 * i : 37 + 3 * i] for i in range(7)]
    step = pl.program_id(0)
    total = jnp.sqrt(jnp.full((8, 128), msg[24, 0], F32))
    clip = (CLIP_LIMIT / jnp.maximum(total, CLIP_LIMIT))[0:1, 0:1]

    def update(k, g, rate, decay, at=Ellipsis):
        w, m, v = [r[at] for r in params[k]]
        g = g * clip
        m = BETA_FIRST * m + (1.0 - BETA_FIRST) * g
        v = BETA_SECOND * v + (1.0 - BETA_SECOND) * g * g
        mh = m * (1.0 / (1.0 - BETA_FIRST**ADAM_STEP))
        vh = v * (1.0 / (1.0 - BETA_SECOND**ADAM_STEP))
        outs[k][0][at] = w - rate * (mh / (jnp.sqrt(vh) + ADAM_EPS) + decay * w)
        outs[k][1][at] = m
        outs[k][2][at] = v

    @pl.when(step == 0)
    def _():
        norm[...] = total[0:1, 0:1]
        for i in range(NE):
            counts[i] = msg[i, 0].astype(jnp.int32)
        sd = side[...].astype(F32)
        for row in range(2):
            g = jnp.concatenate([sd[96 + 4 * row + j : 97 + 4 * row + j] for j in range(4)], axis=1)
            update(0, g, 0.7, 0.0, pl.ds(row, 1))
        g = jnp.concatenate([sd[j * NE : (j + 1) * NE] for j in range(4)], axis=1)
        update(1, g, 0.03, 0.1)

    layo[...] = lay[...]
    tgo[...] = tg[...]
    update(2, kvg[...], 0.06, 0.1)
    update(3, qg[...].astype(F32), 0.06, 0.1)
    update(4, og[...].astype(F32), 2.0, 0.1)
    update(5, upg[0].astype(F32), 0.06, 0.1)
    update(6, downg[0].astype(F32).T, 0.03, 0.1)


def on_device(tokens, cotangent, routes, group_batch, seq_lengths, *state):
    dp = lax.axis_size("dp")
    shard = D // dp
    state = list(state)
    for i in range(3):
        state[3 + i] = state[3 + i].T
        state[9 + i] = state[9 + i].transpose(0, 2, 1)
    gains, router, keyval, query, output, up, down = [state[3 * i] for i in range(7)]

    scr = []
    for item in scratch_list(dp).values():
        if item is None:
            scr.append(pltpu.SemaphoreType.DMA((copies_of(dp),)))
        elif len(item) == 1:
            scr.append(pltpu.SemaphoreType.DMA(item))
        else:
            scr.append(pltpu.VMEM(item[0], item[1]))
    routes_cols = routes.T
    vm = pl.BlockSpec(memory_space=pltpu.VMEM)
    sm = pl.BlockSpec(memory_space=pltpu.SMEM)
    hbm = pl.BlockSpec(memory_space=pl.ANY)
    outs = [
        jax.ShapeDtypeStruct((T, D), BF),
        jax.ShapeDtypeStruct((T, D), F32),
        jax.ShapeDtypeStruct((32, 128), F32),
        jax.ShapeDtypeStruct((2, shard, FF), BF),
        jax.ShapeDtypeStruct((ER, D), BF),
        jax.ShapeDtypeStruct((ER, D), BF),
        jax.ShapeDtypeStruct((128, 128), BF),
        jax.ShapeDtypeStruct((shard, 128), F32),
    ]

    def kernel(*refs):
        layer_kernel(dp, *refs)

    lay, tg, msg, f2, fq, fo, side, kvg = pl.pallas_call(
        kernel,
        out_shape=outs,
        in_specs=[vm] * 10 + [sm] * 2,
        out_specs=[hbm] * len(outs),
        scratch_shapes=scr,
        compiler_params=pltpu.CompilerParams(
            collective_id=0, has_side_effects=True, vmem_limit_bytes=64 * 2**20 - 2**17
        ),
        name="layer",
    )(
        tokens, cotangent, routes_cols, keyval, up, down, query, output, router, gains,
        group_batch, seq_lengths,
    )

    steps = min(4, shard // 16)
    rows = lambda i: (i, 0)
    middle = lambda i: (0, i, 0)
    blocks = [
        pl.BlockSpec((2, D), lambda i: (0, 0)),
        pl.BlockSpec((NE, D), lambda i: (0, 0)),
        pl.BlockSpec((shard // steps, 2 * HD), rows),
        pl.BlockSpec((LE, HD // steps, D), middle),
        pl.BlockSpec((LE, HD // steps, D), middle),
        pl.BlockSpec((shard // steps, FF), rows),
        pl.BlockSpec((FF // steps, shard), rows),
    ]
    each = [b for b in blocks for _ in range(3)]

    def update(*refs):
        adam_kernel(steps, *refs)

    result = list(pl.pallas_call(
        update,
        grid=(steps,),
        out_shape=[
            jax.ShapeDtypeStruct((T, D), BF),
            jax.ShapeDtypeStruct((T, D), F32),
            jax.ShapeDtypeStruct((NE,), jnp.int32),
            jax.ShapeDtypeStruct((1, 1), F32),
        ]
        + [jax.ShapeDtypeStruct(x.shape, F32) for x in state],
        in_specs=[
            pl.BlockSpec((T // steps, D), rows),
            pl.BlockSpec((T // steps, D), rows),
            sm,
            pl.BlockSpec((1, shard // steps, FF), middle),
            pl.BlockSpec((1, shard, FF // steps), lambda i: (1, 0, i)),
            pl.BlockSpec((LE, HD // steps, D), middle),
            pl.BlockSpec((LE, HD // steps, D), middle),
            pl.BlockSpec((128, 128), lambda i: (0, 0)),
            pl.BlockSpec((shard // steps, 2 * HD), rows),
        ]
        + each,
        out_specs=[pl.BlockSpec((T // steps, D), rows), pl.BlockSpec((T // steps, D), rows), sm, pl.BlockSpec((1, 1), lambda i: (0, 0))] + each,
        compiler_params=pltpu.CompilerParams(vmem_limit_bytes=63 * 2**20),
        name="adamw",
    )(lay, tg, msg, f2, f2, fq.reshape(LE, HD, D), fo.reshape(LE, HD, D), side, kvg, *state))
    result[3] = result[3].reshape(())
    for i in range(3):
        result[7 + i] = result[7 + i].T
        result[13 + i] = result[13 + i].transpose(0, 2, 1)
    return tuple(result)


def solution(mesh):
    tok = P(("dp", "expert"), None)
    dp0 = P("dp", None)
    ex0 = P("expert", None, None)
    dp1 = P(None, "dp")
    return jax.shard_map(
        on_device,
        mesh=mesh,
        in_specs=(tok,) * 3 + (P(),) * 8 + (dp0,) * 3 + (ex0,) * 6 + (dp0,) * 3 + (dp1,) * 3,
        out_specs=(tok,) * 2 + (P(),) * 8 + (dp0,) * 3 + (ex0,) * 6 + (dp0,) * 3 + (dp1,) * 3,
        check_vma=False,
    )
```

```python
import math

import jax
import jax.numpy as jnp
from jax import lax
from jax.experimental import pallas as pl
from jax.experimental.pallas import tpu as pltpu
from jax.sharding import PartitionSpec as P

ADAM_STEP = 10
NORM_EPS = 1e-06
BETA_FIRST = 0.9
BETA_SECOND = 0.999
ADAM_EPS = 1e-08
CLIP_LIMIT = 1.0
MASKED = -1e30
LOG2E = math.log2(math.e)
LN2 = math.log(2.0)
MESH = pl.DeviceIdType.MESH
BF = jnp.bfloat16
F32 = jnp.float32

T = 512
D = 512
FF = 2048
HD = 64
K8 = 8
NE = 24
PL = 8
LE = NE // PL
ER = LE * HD
HB = FF // 2


def mm(a, b):
    return jnp.dot(a, b, preferred_element_type=F32)


def mm_nt(a, b):
    return lax.dot_general(a, b, (((1,), (1,)), ((), ())), preferred_element_type=F32)


def mm_tn(a, b):
    return lax.dot_general(a, b, (((0,), (0,)), ((), ())), preferred_element_type=F32)


def expert_at(place):
    return LE * device_at(place // LE) + place % LE


def device_at(slot):
    c, a, b = slot // 4, slot // 2 % 2, slot % 2
    qx, qy = (a, b) if c == 0 else (b, a)
    return 4 * qy + 2 * qx + c


def slot_of(dev):
    c, qx, qy = dev % 2, dev // 2 % 2, dev // 4
    return 4 * c + (2 * qx + qy if c == 0 else 2 * qy + qx)


def piece_rows(dp):
    return -(-ER // (dp * 16)) * 16


def scratch_list(dp):
    shard = D // dp
    pr = piece_rows(dp)
    return dict(
        wkvf=((D, 2 * HD), BF),
        w2=((2, D, FF), BF),
        eq=((NE * HD, D), BF),
        eo=((NE * HD, D), BF),
        kvb=((PL, 2, 256, 128), BF),
        tokx=((256, D), BF),
        cotx=((256, D), BF),
        rtx=((8, 256), jnp.int32),
        rts=((8, 256), jnp.int32),
        wrt=((32, D), F32),
        tokd=((T, D), BF),
        cotd=((T, D), BF),
        cott=((D, T), BF),
        rtd=((8, T), jnp.int32),
        nd=((T, D), BF),
        gate=((8, T), F32),
        dgate=((8, T), F32),
        big=((NE * HD, T), F32),
        peak=((2, 9, 8, 1024), F32),
        at=((NE * HD, T), BF),
        qx=((4, 128, 1024), BF),
        dox=((4, 128, 1024), BF),
        att=((4, HD + 16, 1024), F32),
        top=((4, 8, 1024), F32),
        linv=((4, 8, 1024), F32),
        kx=((2, 8, 256, 128), BF),
        vx=((2, 8, 256, 128), BF),
        kt=((2, 8, HD, 256), BF),
        vt=((2, 8, HD + 16, 256), BF),
        pst=((2, 9, 256, 1024), BF),
        dkv=((2, 8, 256, 128), F32),
        mixed=((T, D), F32),
        ffn=((T, D), BF),
        ffnt=((D, T), BF),
        acc1=((T, D), F32),
        acc2=((T, D), F32),
        gfh=((2, D, HB), BF),
        gfl=((2, D, HB), BF),
        rf1=((2, D, HB), BF),
        rfa=((D, HB // 2), BF),
        rfb=((D, HB // 4), BF),
        rfc=((dp - 1, shard, HB // 4), BF),
        rga=((shard, HB // 2), BF),
        rgb=((shard, HB // 4), BF),
        rgc=((dp - 1, shard, HB), BF),
        rgs=((shard, HB), BF),
        f2=((2, shard, FF), BF),
        go=((NE * HD, D), BF),
        rq1=((NE * HD // 2, D), BF),
        ro1=((NE * HD // 2, D), BF),
        rq2=((2 * ER, D), BF),
        ro2=((2 * ER, D), BF),
        rq3=((ER, D), BF),
        ro3=((ER, D), BF),
        xq=((dp * pr, D), BF),
        xo=((dp * pr, D), BF),
        rq4=((dp - 1, pr, D), BF),
        ro4=((dp - 1, pr, D), BF),
        fq=((dp * pr, D), BF),
        fo=((dp * pr, D), BF),
        rk1=((4, 2, 256, 128), BF),
        rk2=((3, 2, 256, 128), BF),
        dkvd=((T, 128), BF),
        tb=((128, 640), BF),
        rt1=((64, 640), BF),
        tsm=((64, 640), BF),
        rt2=((3, 16, 640), BF),
        rt3=((dp, 16, 640), BF),
        tf=((128, 640), BF),
        cnt=((32, 128), F32),
        mz=((dp, 32, 128), F32),
        mq=((PL, 32, 128), F32),
        layx=((256, D), BF),
        layr=((256, D), BF),
        tgr=((256, D), BF),
        gain=((8, D), F32),
        i_cot=((T, D), BF),
        i_up=((shard, FF), F32),
        i_down=((FF, shard), F32),
        i_qw=((LE, HD, D), F32),
        i_ow=((LE, HD, D), F32),
        osem=(10,),
        ssem=None,
        rsem=None,
    )


def copies_of(dp):
    return 80 + 16 * dp


def layer_kernel(dp, *refs):
    shard = D // dp
    pr = piece_rows(dp)
    (tok, cot_, routes, wkv, up_, down_, qw_, ow_, rw, gains, gbatch, lens) = refs[:12]
    (lay, tg, msgo, f2o, fqo, foo, sideo, kvo) = refs[12:20]
    names = list(scratch_list(dp))
    s = type("Scratch", (), dict(zip(names, refs[20:])))

    z = lax.axis_index("dp")
    e = lax.axis_index("expert")
    c = e % 2
    qx = e // 2 % 2
    qy = e // 4
    a = (1 - c) * qx + c * qy
    b = (1 - c) * qy + c * qx
    q = 2 * a + b

    def device(a_, b_):
        return (z, 4 * ((1 - c) * b_ + c * a_) + 2 * ((1 - c) * a_ + c * b_) + c)

    qs = [q, 2 * a + 1 - b, 2 * (1 - a) + b, 2 * (1 - a) + 1 - b]
    sib = (z, e + 1 - 2 * c)
    near, far = device(a, 1 - b), device(1 - a, b)
    chips = [None, near, far, device(1 - a, 1 - b)]
    swap = (z, 7 - e)
    zp = [None] + [((z + i) % dp, e) for i in range(1, dp)]
    zfrom = [None] + [(z + dp - i) % dp for i in range(1, dp)]
    slot = c * 4 + q
    plane = [sib] + [(z, (e + i) % PL) for i in range(1, PL)]

    count = [0]
    sends = []

    def rcopy(src, dst, peer):
        k = count[0]
        count[0] += 1
        d = pltpu.make_async_remote_copy(
            src_ref=src,
            dst_ref=dst,
            send_sem=s.ssem.at[k],
            recv_sem=s.rsem.at[k],
            device_id=peer,
            device_id_type=MESH,
        )
        d.start()
        sends.append(d)
        return (k, peer, d)

    def sent(handle):
        sends[:] = [d for d in sends if d is not handle[2]]
        handle[2].wait_send()

    def rwait(handle, dst):
        k, peer, _ = handle
        pltpu.make_async_remote_copy(
            src_ref=dst,
            dst_ref=dst,
            send_sem=s.ssem.at[k],
            recv_sem=s.rsem.at[k],
            device_id=peer,
            device_id_type=MESH,
        ).wait_recv()

    def lcopy(src, dst, k):
        d = pltpu.make_async_copy(src, dst, s.osem.at[k])
        d.start()
        return d

    cot, up, down, qw, ow = s.i_cot, s.i_up, s.i_down, s.i_qw, s.i_ow
    loads = [
        lcopy(x, y, k)
        for k, (x, y) in enumerate(
            ((up_, up), (down_, down), (qw_, qw), (ow_, ow), (cot_, cot))
        )
    ]
    bar = pltpu.get_barrier_semaphore()
    for peer in plane[1:] + zp[1:]:
        pl.semaphore_signal(bar, inc=1, device_id=peer, device_id_type=MESH)

    def zrows(ref, i, n):
        return ref.at[pl.ds(pl.multiple_of(i * n, n), n)]

    def turned(x):
        rows, cols = x.shape
        if cols % 128:
            x = jnp.concatenate([x, jnp.zeros((rows, 128 - cols % 128), x.dtype)], axis=1)
        return x.T[0:cols]

    lo = pl.multiple_of(c * HB, HB)
    hi = pl.multiple_of((1 - c) * HB, HB)
    ri = lax.broadcasted_iota(jnp.int32, (256, 256), 0)
    ci = lax.broadcasted_iota(jnp.int32, (256, 256), 1)
    split = jnp.where(ci == 2 * (ri % 128) + ri // 128, 1.0, 0.0).astype(BF)
    join = jnp.where(ri == 2 * (ci % 128) + ci // 128, 1.0, 0.0).astype(BF)
    own_rows = pl.ds(pl.multiple_of(z * shard, shard), shard)
    s.wkvf[own_rows, :] = wkv[...].astype(BF)
    rtt = routes[...].astype(F32).astype(BF)
    s.rtd[:, 0:256] = mm(rtt[:, 0:256], join).astype(jnp.int32)
    s.rts[...] = mm(rtt[:, 256:512], join).astype(jnp.int32)
    WD = HB // 2
    WP = (HB - WD) // 4
    part = pl.multiple_of(c * HB + WD + q * WP, WP)
    def w2_rows(w, i, at, n):
        return s.w2.at[w, pl.ds(pl.multiple_of(i * shard, shard), shard), pl.ds(at, n)]

    def to_all_z(ref):
        return [None] + [rcopy(ref, ref, zp[i]) for i in range(1, dp)]
    pl.semaphore_wait(bar, PL - 1 + dp - 1)
    h_wkv = [None] + [
        rcopy(zrows(s.wkvf, z, shard), zrows(s.wkvf, z, shard), zp[i]) for i in range(1, dp)
    ]
    h_tok = rcopy(tok.at[pl.ds(256, 256)], s.tokx, swap)
    h_rt = rcopy(s.rts, s.rtx, swap)
    loads[2].wait()
    loads[3].wait()
    for i in range(LE):
        rows = pl.ds(pl.multiple_of(slot * ER + i * HD, HD), HD)
        s.eq[rows, :] = qw[i].astype(BF)
        s.eo[rows, :] = ow[i].astype(BF)
    own_eq = zrows(s.eq, slot, ER)
    own_eo = zrows(s.eo, slot, ER)
    h_eq1 = rcopy(own_eq, own_eq, near)
    loads[0].wait()
    loads[1].wait()
    for at, n in ((lo, WD), (part, WP)):
        s.w2[0, own_rows, pl.ds(at, n)] = up[:, pl.ds(at, n)].astype(BF)
    s.w2[1, own_rows, pl.ds(lo, HB)] = turned(down[pl.ds(lo, HB), :]).astype(BF)

    h_wp1 = to_all_z(w2_rows(0, z, part, WP))
    h_wu = to_all_z(w2_rows(0, z, lo, WD))
    h_wd = to_all_z(w2_rows(1, z, lo, HB))

    def gather_far(h, ref):
        rwait(h, zrows(ref, c * 4 + qs[1], ER))
        pair = zrows(ref, c * 2 + a, 2 * ER)
        return rcopy(pair, pair, far)

    def gather_sib(h, ref):
        rwait(h, zrows(ref, c * 2 + 1 - a, 2 * ER))
        mine = zrows(ref, c, 4 * ER)
        return rcopy(mine, mine, sib)

    def w2_cols(w, at, n):
        return s.w2.at[w, :, pl.ds(at, n)]

    s.wrt[0:NE, :] = rw[...]
    s.wrt[NE:32, :] = jnp.zeros((32 - NE, D), F32)

    g0 = gains[0:1, :]
    g1 = gains[1:2, :]

    def rms(x):
        inv = lax.rsqrt(jnp.mean(x * x, axis=-1, keepdims=True) + NORM_EPS)
        return x * inv, inv

    nat0 = mm(split, tok[0:256, :])
    nat1 = mm(split, tok[256:512, :])
    s.tokd[0:256, :] = nat0.astype(BF)
    n0 = (rms(nat0)[0] * g0).astype(BF)
    n1 = (rms(nat1)[0] * g0).astype(BF)
    s.nd[0:256, :] = n0
    loads[4].wait()
    cot0 = mm(split, cot[0:256, :])
    s.cotd[0:256, :] = cot0.astype(BF)

    for i in range(1, dp):
        rwait(h_wkv[i], zrows(s.wkvf, zfrom[i], shard))
    kv0 = mm(n0, s.wkvf[...]).astype(BF)
    kv1 = mm(n1, s.wkvf[...]).astype(BF)
    for p in range(2):
        s.kvb[slot, p, 0:128, :] = kv0[p * 128 : (p + 1) * 128]
        s.kvb[slot, p, 128:256, :] = kv1[p * 128 : (p + 1) * 128]
    h_kv1 = rcopy(s.kvb.at[slot], s.kvb.at[slot], near)
    h_eq2 = gather_far(h_eq1, s.eq)

    rwait(h_tok, s.tokx)
    rwait(h_rt, s.rtx)
    sw = mm(split, s.tokx[...])
    s.tokd[256:512, :] = sw.astype(BF)
    s.nd[256:512, :] = (rms(sw)[0] * g0).astype(BF)
    s.rtd[:, 256:512] = s.rtx[...]

    wrt = s.wrt[...].astype(BF)
    bm1 = gbatch[z] - 1
    is2 = (4 - gbatch[z]) // 2

    def seq_pos(r):
        return r & bm1, (r >> 1) * is2 + (r >> 2) * (1 - is2)

    def limit_of(index):
        out = jnp.zeros(index.shape, jnp.int32)
        for i in range(4):
            out = jnp.where(index == i, lens[z, i], out)
        return out

    block = [2 * e, 15 - 2 * e]
    lanes128 = lax.broadcasted_iota(jnp.int32, (16, 128), 1)
    row16 = lax.broadcasted_iota(jnp.int32, (16, 128), 0)
    row32 = lax.broadcasted_iota(jnp.int32, (32, 128), 0)

    logits = mm_nt(wrt, s.nd[...])
    row_e = lax.broadcasted_iota(jnp.int32, (32, T), 0)
    chosen = jnp.concatenate(
        [
            jnp.sum(jnp.where(row_e == s.rtd[k : k + 1, :], logits, 0.0), axis=0, keepdims=True)
            for k in range(K8)
        ],
        axis=0,
    )
    ex = jnp.exp(chosen - jnp.max(chosen, axis=0, keepdims=True))
    s.gate[...] = ex / jnp.sum(ex, axis=0, keepdims=True)

    counts = jnp.zeros((32, 128), F32)
    for g in range(4):
        blk, p = g // 2, g % 2
        row = 2 * (block[blk] * 128 + lanes128) + p
        seq, pos = seq_pos(row)
        live = (pos < limit_of(seq))[0:1, :].astype(F32)
        for k in range(K8):
            counts = counts + jnp.where(
                row32 == s.rtd[k : k + 1, g * 128 : (g + 1) * 128], live, 0.0
            )
        feat = jnp.where(seq == row16, 1.0, 0.0).astype(BF)
        s.qx[g, 64:80, :] = jnp.concatenate([feat] * K8, axis=1)
        s.qx[g, 80:128, :] = jnp.zeros((48, 1024), BF)
    s.cnt[...] = jnp.broadcast_to(jnp.sum(counts, axis=1, keepdims=True), (32, 128))

    half = NE * HD // 2
    rwait(h_kv1, s.kvb.at[c * 4 + qs[1]])
    kv_pair = s.kvb.at[pl.ds(c * 4 + a * 2, 2)]
    h_kv2 = rcopy(kv_pair, kv_pair, far)
    h_eqs = gather_sib(h_eq2, s.eq)
    rwait(h_kv2, s.kvb.at[pl.ds(c * 4 + (1 - a) * 2, 2)])
    h_eo1 = rcopy(own_eo, own_eo, near)
    h_kvs = rcopy(s.kvb.at[pl.ds(c * 4, 4)], s.kvb.at[pl.ds(c * 4, 4)], sib)
    rwait(h_eqs, zrows(s.eq, 1 - c, half))

    def query_rows(i, _):
        rows = pl.ds(pl.multiple_of(i * 256, 256), 256)
        s.big[rows, :] = mm_nt(s.eq[rows, :], s.nd[...])
        return 0

    lax.fori_loop(0, NE * HD // 256, query_rows, 0)

    def pick(g, k):
        lanes = pl.ds(pl.multiple_of(g * 128, 128), 128)
        rk = s.rtd[k : k + 1, lanes]
        acc = jnp.zeros((HD, 128), F32)
        for place in range(NE):
            acc = jnp.where(rk == expert_at(place), s.big[place * HD : (place + 1) * HD, lanes], acc)
        return acc

    def choose(g, _):
        for k in range(K8):
            s.qx[g, 0:64, k * 128 : (k + 1) * 128] = (pick(g, k) * (0.125 * LOG2E)).astype(BF)
        return 0

    lax.fori_loop(0, 4, choose, 0)

    rwait(h_kvs, s.kvb.at[pl.ds((1 - c) * 4, 4)])
    krow = lax.broadcasted_iota(jnp.int32, (256, 128), 0)
    klane = lax.broadcasted_iota(jnp.int32, (256, 128), 1)
    for t in range(8):
        for p in range(2):
            kv = s.kvb[slot_of(t), p].astype(F32)
            seq, pos = seq_pos(2 * (t * 256 + krow) + p)
            col = klane - 64
            shown = (seq == col) & (pos < limit_of(col))
            feat = jnp.where(shown | (col > 3), 0.0, MASKED)
            s.kx[p, t] = jnp.where(col < 0, kv, feat).astype(BF)
            s.vx[p, t] = jnp.where(col >= 0, kv, jnp.where(klane < 2, 1.0, 0.0)).astype(BF)
            kvt = kv.T
            s.kt[p, t] = kvt[0:64].astype(BF)
            s.vt[p, t, 0:64, :] = kvt[64:128].astype(BF)
            s.vt[p, t, 64:80, :] = jnp.ones((16, 256), BF)

    turn = e + 1
    below = lax.broadcasted_iota(jnp.int32, (256, 128), 0) - lax.broadcasted_iota(
        jnp.int32, (256, 128), 1
    )
    s.att[...] = jnp.zeros(s.att.shape, F32)
    s.top[...] = jnp.full(s.top.shape, MASKED, F32)

    def place_of(i):
        blk = jnp.where(i >= turn, 1, 0)
        return blk * 2, i - blk * turn

    def attend(i, _):
        g0_, t = place_of(i)
        visible = below <= jnp.where(i == turn - 1, 0, jnp.where(i == 8, 128, 256))
        visible = jnp.concatenate([visible] * K8, axis=1)
        both_p = range(2)
        scs = [jnp.where(visible, mm(s.kx[p, t], s.qx[g0_ + p]), MASKED) for p in both_p]
        tops = [jnp.max(jnp.max(x.reshape(32, 8, 1024), axis=0), axis=0, keepdims=True) for x in scs]
        olds = [s.top[g0_ + p, 0:1, :] for p in both_p]
        news = [jnp.maximum(old, jnp.ceil(x)) for old, x in zip(olds, tops)]
        pbs = [jnp.exp2(sc - new).astype(BF) for sc, new in zip(scs, news)]
        outs = [mm(s.vt[p, t], pbs[p]) for p in both_p]
        for p in both_p:
            s.att[g0_ + p] = s.att[g0_ + p] * jnp.exp2(olds[p] - news[p]) + outs[p]
            s.pst[p, i] = pbs[p]
            s.peak[p, i] = jnp.broadcast_to(news[p], (8, 1024))
            s.top[g0_ + p] = jnp.broadcast_to(news[p], (8, 1024))
        return 0

    h_eo2 = gather_far(h_eo1, s.eo)
    lax.fori_loop(0, 3, attend, 0)
    for i in range(1, dp):
        rwait(h_wp1[i], w2_rows(0, zfrom[i], part, WP))
    h_wp2 = rcopy(w2_cols(0, part, WP), w2_cols(0, part, WP), near)
    h_cot = rcopy(cot.at[pl.ds(256, 256)], s.cotx, swap)
    lax.fori_loop(3, 5, attend, 0)
    rwait(h_wp2, w2_cols(0, c * HB + WD + qs[1] * WP, WP))
    both_parts = pl.multiple_of(c * HB + WD + a * 2 * WP, 2 * WP)
    h_wp3 = rcopy(w2_cols(0, both_parts, 2 * WP), w2_cols(0, both_parts, 2 * WP), far)
    lax.fori_loop(5, 7, attend, 0)
    h_eos = gather_sib(h_eo2, s.eo)
    lax.fori_loop(7, 9, attend, 0)
    for g in range(4):
        inv = 1.0 / s.att[g, 64:72, :]
        s.linv[g] = inv
        s.att[g, 0:64, :] = s.att[g, 0:64, :] * inv[0:1]
    rwait(h_wp3, w2_cols(0, pl.multiple_of(c * HB + WD + (1 - a) * 2 * WP, 2 * WP), 2 * WP))
    for i in range(1, dp):
        rwait(h_wu[i], w2_rows(0, zfrom[i], lo, WD))
    h_w2s = [rcopy(w2_cols(0, lo, HB), w2_cols(0, lo, HB), sib)]
    def spread(dst, src, scale):
        def one(g, _):
            lanes = pl.ds(pl.multiple_of(g * 128, 128), 128)
            for k in range(K8):
                part = src[g, 0:HD, k * 128 : (k + 1) * 128]
                if scale is not None:
                    part = part * scale[k : k + 1, lanes]
                else:
                    part = part * 0.125
                s.acc1[k * HD : (k + 1) * HD, 0:128] = part
            for place in range(NE):
                acc = jnp.zeros((HD, 128), F32)
                for k in range(K8):
                    acc = jnp.where(
                        s.rtd[k : k + 1, lanes] == expert_at(place),
                        s.acc1[k * HD : (k + 1) * HD, 0:128],
                        acc,
                    )
                dst[place * HD : (place + 1) * HD, lanes] = acc.astype(BF)
            return 0

        lax.fori_loop(0, 4, one, 0)

    spread(s.at, s.att, s.gate)
    for i in range(1, dp):
        rwait(h_wd[i], w2_rows(1, zfrom[i], lo, HB))
    h_w2s.append(rcopy(w2_cols(1, lo, HB), w2_cols(1, lo, HB), sib))
    rwait(h_eos, zrows(s.eo, 1 - c, half))
    s.acc1[...] = s.tokd[...].astype(F32)

    def mix(i, _):
        rows = pl.ds(pl.multiple_of(i * 256, 256), 256)
        s.acc1[...] += mm_tn(s.at[rows, :], s.eo[rows, :])
        return 0

    lax.fori_loop(0, NE * HD // 256, mix, 0)
    mixed = s.acc1[...]
    s.mixed[...] = mixed
    ffn = rms(mixed)[0] * g1
    s.ffn[...] = ffn.astype(BF)
    s.ffnt[...] = ffn.T.astype(BF)
    rwait(h_cot, s.cotx)
    cot1 = mm(split, s.cotx[...])
    s.cotd[256:512, :] = cot1.astype(BF)
    s.cott[:, 0:256] = cot0.T.astype(BF)
    s.cott[:, 256:512] = cot1.T.astype(BF)
    s.acc2[...] = jnp.zeros((T, D), F32)
    for w in range(2):
        rwait(h_w2s[w], w2_cols(w, hi, HB))

    FT = 256

    def feed(i, base_, at, keep):
        cols = pl.ds(pl.multiple_of(base_ + at + i * FT, FT), FT)
        part_cols = pl.ds(pl.multiple_of(at + i * FT, FT), FT)
        up = mm(s.ffn[...], s.w2[0, :, cols])
        sq = up * up
        th = jnp.tanh(0.79788456 * up * (1.0 + 0.044715 * sq))
        hid = (0.5 * up * (1.0 + th)).astype(BF)
        slope = 0.5 * (1.0 + th) + 0.5 * up * (1.0 - th * th) * (
            0.79788456 * (1.0 + 3 * 0.044715 * sq)
        )
        s.acc1[...] += mm_nt(hid, s.w2[1, :, cols])
        dup = (mm(s.cotd[...], s.w2[1, :, cols]) * slope).astype(BF)
        keep[0, :, part_cols] = mm(s.ffnt[...], dup).astype(BF)
        keep[1, :, part_cols] = mm(s.cott[...], hid).astype(BF)
        s.acc2[...] += mm_nt(dup, s.w2[0, :, cols])
        return 0

    def both(x, y):
        return (x.astype(F32) + y.astype(F32)).astype(BF)

    def fold(sq):
        sq = jnp.sum(sq, axis=0, keepdims=True)
        out = sq[:, 0:128]
        for j in range(1, sq.shape[1] // 128):
            out = out + sq[:, j * 128 : (j + 1) * 128]
        return out

    done, squares = [], []
    quart = HB // 4
    keep2 = pl.multiple_of(a * 2 * quart, 2 * quart)
    give2 = pl.multiple_of((1 - a) * 2 * quart, 2 * quart)
    keep1 = pl.multiple_of(q * quart, quart)
    give1 = pl.multiple_of(qs[1] * quart, quart)
    place1 = pl.multiple_of(c * HB + keep1, quart)

    def feed_grad(w):
        own, total, one, two, three = s.gfl.at[w], s.rf1.at[w], s.rfa, s.rfb, s.rfc

        def pair(j, at):
            cols = pl.ds(at, 2 * quart)
            rwait(h_f1[j][w], total.at[:, cols])
            total[:, cols] = both(own[:, cols], total[:, cols])

        pair(0, give2)
        h = rcopy(total.at[:, pl.ds(give2, 2 * quart)], one, far)
        yield
        pair(1, keep2)
        yield
        rwait(h, one)
        for at in (give1, keep1):
            inner = pl.multiple_of(at - keep2, quart)
            total[:, pl.ds(at, quart)] = both(
                total[:, pl.ds(at, quart)], one[:, pl.ds(inner, quart)]
            )
            if at is give1:
                h = rcopy(total.at[:, pl.ds(give1, quart)], two, near)
        yield
        rwait(h, two)
        total[:, pl.ds(keep1, quart)] = both(total[:, pl.ds(keep1, quart)], two[...])

        def zpart(i):
            return total.at[pl.ds(pl.multiple_of(i * shard, shard), shard), pl.ds(keep1, quart)]

        hz = [rcopy(zpart(zp[i][0]), three.at[i - 1], zp[i]) for i in range(1, dp)]
        yield
        acc = zpart(z)[...].astype(F32)
        for i in range(1, dp):
            rwait(hz[i - 1], three.at[i - 1])
            acc = acc + three[i - 1].astype(F32)
        yield from spread_grad(w, acc)

    def spread_grad(w, acc):
        out = s.f2.at[w]
        acc = acc.astype(BF)
        out[:, pl.ds(place1, quart)] = acc
        acc = acc.astype(F32)
        squares.append(fold(acc * acc))
        h = rcopy(out.at[:, pl.ds(place1, quart)], out.at[:, pl.ds(place1, quart)], near)
        yield
        rwait(h, out.at[:, pl.ds(pl.multiple_of(c * HB + give1, quart), quart)])
        wide = out.at[:, pl.ds(pl.multiple_of(c * HB + keep2, 2 * quart), 2 * quart)]
        h = rcopy(wide, wide, far)
        yield
        rwait(h, out.at[:, pl.ds(pl.multiple_of(c * HB + give2, 2 * quart), 2 * quart)])
        h = rcopy(out.at[:, pl.ds(lo, HB)], out.at[:, pl.ds(lo, HB)], sib)
        yield
        rwait(h, out.at[:, pl.ds(hi, HB)])
        done.append(lcopy(out, f2o.at[w], 2 + w))
        yield

    def dp_first_grad(w):
        own, total, one, two, three = s.gfl.at[w], s.rf1.at[w], s.rga, s.rgb, s.rgc
        hz = []
        for j, at in ((0, give2), (1, keep2)):
            cols = pl.ds(at, 2 * quart)
            rwait(h_f1[j][w], total.at[:, cols])
            total[:, cols] = both(own[:, cols], total[:, cols])
            for i in range(1, dp):
                mine = pl.ds(pl.multiple_of(zp[i][0] * shard, shard), shard)
                hz.append((rcopy(total.at[mine, cols], three.at[i - 1, :, cols], zp[i]), i, cols))
            yield
        for h, i, cols in hz:
            rwait(h, three.at[i - 1, :, cols])
        acc = total[own_rows, :].astype(F32)
        for i in range(1, dp):
            acc = acc + three[i - 1].astype(F32)
        s.rgs[...] = acc.astype(BF)
        h = rcopy(s.rgs.at[:, pl.ds(give2, 2 * quart)], one, far)
        yield
        rwait(h, one)
        s.rgs[:, pl.ds(keep2, 2 * quart)] = both(s.rgs[:, pl.ds(keep2, 2 * quart)], one[...])
        h = rcopy(s.rgs.at[:, pl.ds(give1, quart)], two, near)
        yield
        rwait(h, two)
        acc = s.rgs[:, pl.ds(keep1, quart)].astype(F32) + two[...].astype(F32)
        yield from spread_grad(w, acc)

    def head_grad(src, total, one, two, full, part_, final, dst, sem):
        h = rcopy(zrows(src, 1 - c, half), total, sib)
        s.half_sent = h
        yield
        rwait(h, total)

        def pair(which):
            rows = pl.ds(pl.multiple_of(which * 2 * ER, 128), 2 * ER)
            wide = pl.ds(pl.multiple_of(c * half + which * 2 * ER, 128), 2 * ER)
            total[rows, :] = both(src[wide, :], total[rows, :])

        pair(1 - a)
        h = rcopy(zrows(total, 1 - a, 2 * ER), one, far)
        pair(a)
        yield
        rwait(h, one)
        for which in (1 - b, b):
            rows = pl.ds(pl.multiple_of((2 * a + which) * ER, ER), ER)
            total[rows, :] = both(total[rows, :], one[pl.ds(pl.multiple_of(which * ER, ER), ER), :])
            if which is not b:
                h = rcopy(zrows(total, qs[1], ER), two, near)
        yield
        rwait(h, two)
        full[0:ER, :] = both(total[pl.ds(pl.multiple_of(q * ER, ER), ER), :], two[...])
        if dp * pr > ER:
            full[ER:, :] = jnp.zeros((dp * pr - ER, full.shape[1]), BF)
        hz = [rcopy(zrows(full, zp[i][0], pr), part_.at[i - 1], zp[i]) for i in range(1, dp)]
        yield
        mine = pl.ds(pl.multiple_of(z * pr, pr), pr)
        acc = full[mine, :].astype(F32)
        for i in range(1, dp):
            rwait(hz[i - 1], part_.at[i - 1])
            acc = acc + part_[i - 1].astype(F32)
        acc = acc.astype(BF)
        final[mine, :] = acc
        acc = acc.astype(F32)
        squares.append(fold(acc * acc))
        hz = to_all_z(zrows(final, z, pr))
        yield
        for i in range(1, dp):
            rwait(hz[i], zrows(final, zfrom[i], pr))
        done.append(lcopy(final.at[pl.ds(0, ER)], dst, sem))
        yield

    def feed_tiles(base_, at, keep):
        lax.fori_loop(0, HB // FT // 2, lambda i, _: feed(i, base_, at, keep), 0)

    def to_sibling(at):
        cols = pl.ds(at, 2 * quart)
        return [rcopy(s.gfh.at[w, :, cols], s.rf1.at[w, :, cols], sib) for w in range(2)]

    sib_give2 = pl.multiple_of((1 - b) * 2 * quart, 2 * quart)
    sib_keep2 = pl.multiple_of(b * 2 * quart, 2 * quart)
    feed_tiles(hi, sib_give2, s.gfh)
    h_f1 = [to_sibling(sib_give2)]
    feed_tiles(lo, give2, s.gfl)
    chain = [feed_grad(0), dp_first_grad(1)]
    next(chain[0])
    next(chain[1])
    feed_tiles(hi, sib_keep2, s.gfh)
    h_f1.append(to_sibling(sib_keep2))
    feed_tiles(lo, keep2, s.gfl)
    next(chain[0])
    next(chain[1])

    out = s.acc1[...].astype(BF)
    s.layx[...] = mm(join, out[256:512]).astype(BF)
    s.ffn[0:256, :] = mm(join, out[0:256]).astype(BF)

    def rms_back(dn, gain, unit, inv):
        a = dn * gain
        return inv * (a - unit * jnp.mean(a * unit, axis=-1, keepdims=True)), jnp.sum(
            dn * unit, axis=0, keepdims=True
        )

    unit1, inv1 = rms(s.mixed[...])
    back, gain1 = rms_back(s.acc2[...], g1, unit1, inv1)
    s.gain[1:2, :] = gain1
    dmix = s.cotd[...].astype(F32) + back
    s.mixed[...] = dmix
    s.cott[...] = dmix.astype(BF)

    def out_rows(i, _):
        rows = pl.ds(pl.multiple_of(i * 256, 256), 256)
        s.big[rows, :] = mm_nt(s.eo[rows, :], s.cott[...])
        s.go[rows, :] = mm(s.at[rows, :], s.cott[...]).astype(BF)
        return 0

    lax.fori_loop(0, NE * HD // 256, out_rows, 0)
    chain.append(head_grad(s.go, s.ro1, s.ro2, s.ro3, s.xo, s.ro4, s.fo, foo, 4))
    next(chain[2])
    sent_o = s.half_sent

    def heads_back(g, _):
        lanes = pl.ds(pl.multiple_of(g * 128, 128), 128)
        for k in range(K8):
            ks = slice(k * 128, (k + 1) * 128)
            da = pick(g, k)
            at = s.att[g, 0:HD, ks]
            s.dgate[k : k + 1, lanes] = jnp.sum(at * da, axis=0, keepdims=True)
            do = (da * (s.gate[k : k + 1, lanes] * s.linv[g, 0:1, ks])).astype(BF)
            s.dox[g, 64:128, ks] = do
            delta = -jnp.sum(do.astype(F32) * at, axis=0, keepdims=True)
            top = delta.astype(BF).astype(F32)
            s.dox[g, 0:16, ks] = jnp.where(
                row16 == 0, top, jnp.where(row16 == 1, delta - top, 0.0)
            ).astype(BF)
            s.dox[g, 16:64, ks] = jnp.zeros((48, 128), BF)
        return 0

    lax.fori_loop(0, 4, heads_back, 0)
    s.dkv[...] = jnp.zeros(s.dkv.shape, F32)

    left = lax.broadcasted_iota(jnp.int32, (256, 128), 1) < 64

    s.att[...] = jnp.zeros(s.att.shape, F32)

    def attend_back(i, _):
        g0_, t = place_of(i)
        both_p = range(2)
        scales = [jnp.exp2(s.peak[p, i, 0:1, :] - s.top[g0_ + p, 0:1, :]) for p in both_p]
        doxs = [(s.dox[g0_ + p].astype(F32) * scales[p]).astype(BF) for p in both_p]
        dprobs = [mm(s.vx[p, t], doxs[p]) for p in both_p]
        vparts = [mm_nt(s.pst[p, i], doxs[p]) for p in both_p]
        dss = [(s.pst[p, i].astype(F32) * dprobs[p]).astype(BF) for p in both_p]
        kparts = [mm_nt(dss[p], s.qx[g0_ + p]) for p in both_p]
        dqs = [mm(s.kt[p, t], dss[p]) for p in both_p]
        for p in both_p:
            s.dkv[p, t] += jnp.where(left, kparts[p] * LN2, vparts[p])
            s.att[g0_ + p, 0:HD, :] += dqs[p]
        return 0

    next(chain[2])
    lax.fori_loop(0, 3, attend_back, 0)
    next(chain[0])
    lax.fori_loop(3, 5, attend_back, 0)
    next(chain[2])
    lax.fori_loop(5, 7, attend_back, 0)
    next(chain[0])
    lax.fori_loop(7, 9, attend_back, 0)
    next(chain[2])
    h_lay = rcopy(s.layx, s.layr, swap)
    for h in (h_kv1, h_kv2, h_kvs):
        sent(h)
    for dev in range(PL):
        sl = slot_of(dev)
        for side_, blk in enumerate((2 * dev, 15 - 2 * dev)):
            for p in range(2):
                s.kvb[sl, side_, p * 128 : (p + 1) * 128, :] = s.dkv[p, blk // 2, (blk % 2) * 128 : (blk % 2) * 128 + 128, :].astype(BF)
    h_k1 = rcopy(s.kvb.at[pl.ds((1 - c) * 4, 4)], s.rk1, sib)
    spread(s.at, s.att, None)
    sent(sent_o)

    def query_grad(i, cols):
        rows = pl.ds(pl.multiple_of(i * 256, 256), 256)
        s.go[rows, cols] = mm(s.at[rows, :], s.nd[:, cols]).astype(BF)
        return 0

    for j in range(2):
        cols = pl.ds(j * 256, 256)
        lax.fori_loop(0, NE * HD // 256, lambda i, _: query_grad(i, cols), 0)
        chain.append(
            head_grad(
                *[x.at[:, cols] for x in (s.go, s.rq1, s.rq2, s.rq3, s.xq)],
                s.rq4.at[:, :, cols], s.fq.at[:, cols], fqo.at[:, cols], 5 + 4 * j,
            )
        )
        next(chain[3 + j])
        if j == 0:
            rwait(h_k1, s.rk1)
            for i in range(4):
                s.rk1[i] = both(s.kvb[c * 4 + i], s.rk1[i])
            h_k2 = [None] + [
                rcopy(s.rk1.at[qs[m]], s.rk2.at[m - 1], chips[m]) for m in (1, 2, 3)
            ]
    s.acc2[...] = jnp.zeros((T, D), F32)

    def slot_sum(i, _):
        rows = pl.ds(pl.multiple_of(i * 256, 256), 256)
        s.acc2[...] += mm_tn(s.at[rows, :], s.eq[rows, :])
        return 0

    lax.fori_loop(0, NE * HD // 256, slot_sum, 0)
    gate = s.gate[...]
    dch = gate * (s.dgate[...] - jnp.sum(gate * s.dgate[...], axis=0, keepdims=True))
    dlog = jnp.zeros((32, T), F32)
    for k in range(K8):
        dlog = dlog + jnp.where(row_e == s.rtd[k : k + 1, :], dch[k : k + 1, :], 0.0)
    dlog = dlog.astype(BF)
    s.acc2[...] += mm_tn(dlog, wrt)
    grt = mm(dlog, s.nd[...])

    next(chain[3])
    next(chain[4])
    next(chain[1])
    next(chain[0])
    for m in (1, 2, 3):
        rwait(h_k2[m], s.rk2.at[m - 1])
    for i in range(2):
        total = s.rk1[q, i].astype(F32)
        for m in (1, 2, 3):
            total = total + s.rk2[m - 1, i].astype(F32)
        s.dkvd[i * 256 : (i + 1) * 256, :] = total.astype(BF)
    dn = s.acc2[...] + mm_nt(s.dkvd[...], s.wkvf[...])
    unit0, inv0 = rms(s.tokd[...].astype(F32))
    back0, gain0 = rms_back(dn, g0, unit0, inv0)
    s.tb[:, 0:512] = mm_tn(s.dkvd[...], s.nd[...]).astype(BF)
    side = s.acc1.at[pl.ds(0, 128), pl.ds(0, 128)]
    for j in range(4):
        js = slice(j * 128, (j + 1) * 128)
        side[j * 24 : (j + 1) * 24, :] = grt[0:24, js]
        side[96 + j : 97 + j, :] = gain0[:, js]
        side[100 + j : 101 + j, :] = s.gain[1:2, js]
    side[104:128, :] = jnp.zeros((24, 128), F32)
    s.tb[:, 512:640] = side[...].astype(BF)
    h_t1 = rcopy(zrows(s.tb, 1 - c, 64), s.rt1, sib)
    next(chain[1])
    next(chain[0])
    next(chain[2])
    next(chain[3])
    next(chain[4])
    rwait(h_t1, s.rt1)
    s.tsm[...] = both(s.tb[pl.ds(pl.multiple_of(c * 64, 64), 64), :], s.rt1[...])
    h_t2 = [None] + [rcopy(zrows(s.tsm, qs[m], 16), s.rt2.at[m - 1], chips[m]) for m in (1, 2, 3)]
    grad = s.mixed[...] + back0
    sent(h_lay)
    s.layx[...] = mm(join, grad[256:512].astype(BF)).astype(BF)
    top = grad[0:256].astype(BF)
    rest = (grad[0:256] - top.astype(F32)).astype(BF)
    s.acc1[0:256, :] = mm(join, top) + mm(join, rest)
    next(chain[1])
    next(chain[3])
    next(chain[4])
    next(chain[0])
    for m in (1, 2, 3):
        rwait(h_t2[m], s.rt2.at[m - 1])
    total = s.tsm[pl.ds(pl.multiple_of(q * 16, 16), 16), :].astype(F32)
    for m in (1, 2, 3):
        total = total + s.rt2[m - 1].astype(F32)
    s.rt3[z] = total.astype(BF)
    h_t3 = [None] + [rcopy(s.rt3.at[z], s.rt3.at[z], zp[i]) for i in range(1, dp)]
    h_tg = rcopy(s.layx, s.tgr, swap)
    next(chain[1])
    for i in range(1, dp):
        rwait(h_t3[i], s.rt3.at[zfrom[i]])
    total = s.rt3[0].astype(F32)
    for i in range(1, dp):
        total = total + s.rt3[i].astype(F32)
    tail = total.astype(BF)
    s.tf[pl.ds(pl.multiple_of(slot * 16, 16), 16), :] = tail
    h_t4 = [None] + [
        rcopy(zrows(s.tf, slot, 16), zrows(s.tf, slot, 16), chips[m]) for m in (1, 2, 3)
    ]
    next(chain[3])
    next(chain[4])
    sq_t = fold(tail.astype(F32) * tail.astype(F32)) * (1.0 / dp)

    total = squares[0]
    for sq in squares[1:] + [sq_t]:
        total = total + sq
    squares = jnp.sum(total, axis=1, keepdims=True)
    s.mz[z] = jnp.where(row32 < 24, s.cnt[...], jnp.where(row32 == 24, squares, 0.0))
    h_m1 = [None] + [rcopy(s.mz.at[z], s.mz.at[z], zp[i]) for i in range(1, dp)]

    for m in (1, 2, 3):
        rwait(h_t4[m], zrows(s.tf, c * 4 + qs[m], 16))
    next(chain[1])
    h_t5 = rcopy(zrows(s.tf, c, 64), zrows(s.tf, c, 64), sib)

    for i in range(1, dp):
        rwait(h_m1[i], s.mz.at[zfrom[i]])
    total = s.mz[0]
    for i in range(1, dp):
        total = total + s.mz[i]
    s.mq[e] = total
    h_m2 = [None] + [rcopy(s.mq.at[e], s.mq.at[e], plane[i]) for i in range(1, PL)]

    rwait(h_lay, s.layr)
    s.ffn[256:512, :] = s.layr[...]
    done.append(lcopy(s.ffn, lay, 0))
    rwait(h_tg, s.tgr)
    s.acc1[256:512, :] = s.tgr[...].astype(F32)
    done.append(lcopy(s.acc1, tg, 1))
    next(chain[0])
    next(chain[1])
    rwait(h_t5, zrows(s.tf, 1 - c, 64))
    s.acc2[:, 0:128] = s.tf[:, 0:512].astype(F32).T
    done.append(lcopy(s.tf.at[:, pl.ds(512, 128)], sideo, 8))
    done.append(lcopy(s.acc2.at[own_rows, pl.ds(0, 128)], kvo, 7))
    next(chain[2])
    next(chain[3])
    next(chain[4])
    for i in range(1, PL):
        rwait(h_m2[i], s.mq.at[(e + PL - i) % PL])
    total = s.mq[0]
    for i in range(1, PL):
        total = total + s.mq[i]
    s.cnt[...] = total
    done.append(lcopy(s.cnt, msgo, 6))
    for d in done:
        d.wait()
    for d in sends:
        d.wait_send()
    assert count[0] <= copies_of(dp)


def adam_kernel(steps, *refs):
    (lay, tg, msg, upg, downg, qg, og, side, kvg) = refs[:9]
    params = [refs[9 + 3 * i : 12 + 3 * i] for i in range(7)]
    layo, tgo, counts, norm = refs[30:34]
    outs = [refs[34 + 3 * i : 37 + 3 * i] for i in range(7)]
    step = pl.program_id(0)
    total = jnp.sqrt(jnp.full((8, 128), msg[24, 0], F32))
    clip = (CLIP_LIMIT / jnp.maximum(total, CLIP_LIMIT))[0:1, 0:1]

    def update(k, g, rate, decay, at=Ellipsis):
        w, m, v = [r[at] for r in params[k]]
        g = g * clip
        m = BETA_FIRST * m + (1.0 - BETA_FIRST) * g
        v = BETA_SECOND * v + (1.0 - BETA_SECOND) * g * g
        mh = m * (1.0 / (1.0 - BETA_FIRST**ADAM_STEP))
        vh = v * (1.0 / (1.0 - BETA_SECOND**ADAM_STEP))
        outs[k][0][at] = w - rate * (mh / (jnp.sqrt(vh) + ADAM_EPS) + decay * w)
        outs[k][1][at] = m
        outs[k][2][at] = v

    @pl.when(step == 0)
    def _():
        norm[...] = total[0:1, 0:1]
        for i in range(NE):
            counts[i] = msg[i, 0].astype(jnp.int32)
        sd = side[...].astype(F32)
        for row in range(2):
            g = jnp.concatenate([sd[96 + 4 * row + j : 97 + 4 * row + j] for j in range(4)], axis=1)
            update(0, g, 0.7, 0.0, pl.ds(row, 1))
        g = jnp.concatenate([sd[j * NE : (j + 1) * NE] for j in range(4)], axis=1)
        update(1, g, 0.03, 0.1)

    layo[...] = lay[...]
    tgo[...] = tg[...]
    update(2, kvg[...], 0.06, 0.1)
    update(3, qg[...].astype(F32), 0.06, 0.1)
    update(4, og[...].astype(F32), 2.0, 0.1)
    update(5, upg[0].astype(F32), 0.06, 0.1)
    update(6, downg[0].astype(F32).T, 0.03, 0.1)


def on_device(tokens, cotangent, routes, group_batch, seq_lengths, *state):
    dp = lax.axis_size("dp")
    shard = D // dp
    state = list(state)
    for i in range(3):
        state[3 + i] = state[3 + i].T
        state[9 + i] = state[9 + i].transpose(0, 2, 1)
    gains, router, keyval, query, output, up, down = [state[3 * i] for i in range(7)]

    scr = []
    for item in scratch_list(dp).values():
        if item is None:
            scr.append(pltpu.SemaphoreType.DMA((copies_of(dp),)))
        elif len(item) == 1:
            scr.append(pltpu.SemaphoreType.DMA(item))
        else:
            scr.append(pltpu.VMEM(item[0], item[1]))
    routes_cols = routes.T
    vm = pl.BlockSpec(memory_space=pltpu.VMEM)
    sm = pl.BlockSpec(memory_space=pltpu.SMEM)
    hbm = pl.BlockSpec(memory_space=pl.ANY)
    outs = [
        jax.ShapeDtypeStruct((T, D), BF),
        jax.ShapeDtypeStruct((T, D), F32),
        jax.ShapeDtypeStruct((32, 128), F32),
        jax.ShapeDtypeStruct((2, shard, FF), BF),
        jax.ShapeDtypeStruct((ER, D), BF),
        jax.ShapeDtypeStruct((ER, D), BF),
        jax.ShapeDtypeStruct((128, 128), BF),
        jax.ShapeDtypeStruct((shard, 128), F32),
    ]

    def kernel(*refs):
        layer_kernel(dp, *refs)

    lay, tg, msg, f2, fq, fo, side, kvg = pl.pallas_call(
        kernel,
        out_shape=outs,
        in_specs=[vm, hbm, vm, vm, hbm, hbm, hbm, hbm, vm, vm, sm, sm],
        out_specs=[hbm] * len(outs),
        scratch_shapes=scr,
        compiler_params=pltpu.CompilerParams(
            collective_id=0, has_side_effects=True, vmem_limit_bytes=64 * 2**20 - 2**17
        ),
        name="layer",
    )(
        tokens, cotangent, routes_cols, keyval, up, down, query, output, router, gains,
        group_batch, seq_lengths,
    )

    steps = 2
    rows = lambda i: (i, 0)
    middle = lambda i: (0, i, 0)
    blocks = [
        pl.BlockSpec((2, D), lambda i: (0, 0)),
        pl.BlockSpec((NE, D), lambda i: (0, 0)),
        pl.BlockSpec((shard // steps, 2 * HD), rows),
        pl.BlockSpec((LE, HD // steps, D), middle),
        pl.BlockSpec((LE, HD // steps, D), middle),
        pl.BlockSpec((shard // steps, FF), rows),
        pl.BlockSpec((FF // steps, shard), rows),
    ]
    each = [b for b in blocks for _ in range(3)]

    def update(*refs):
        adam_kernel(steps, *refs)

    result = list(pl.pallas_call(
        update,
        grid=(steps,),
        out_shape=[
            jax.ShapeDtypeStruct((T, D), BF),
            jax.ShapeDtypeStruct((T, D), F32),
            jax.ShapeDtypeStruct((NE,), jnp.int32),
            jax.ShapeDtypeStruct((1, 1), F32),
        ]
        + [jax.ShapeDtypeStruct(x.shape, F32) for x in state],
        in_specs=[
            pl.BlockSpec((T // steps, D), rows),
            pl.BlockSpec((T // steps, D), rows),
            sm,
            pl.BlockSpec((1, shard // steps, FF), middle),
            pl.BlockSpec((1, shard, FF // steps), lambda i: (1, 0, i)),
            pl.BlockSpec((LE, HD // steps, D), middle),
            pl.BlockSpec((LE, HD // steps, D), middle),
            pl.BlockSpec((128, 128), lambda i: (0, 0)),
            pl.BlockSpec((shard // steps, 2 * HD), rows),
        ]
        + each,
        out_specs=[pl.BlockSpec((T // steps, D), rows), pl.BlockSpec((T // steps, D), rows), sm, pl.BlockSpec((1, 1), lambda i: (0, 0))] + each,
        compiler_params=pltpu.CompilerParams(vmem_limit_bytes=63 * 2**20),
        name="adamw",
    )(lay, tg, msg, f2, f2, fq.reshape(LE, HD, D), fo.reshape(LE, HD, D), side, kvg, *state))
    result[3] = result[3].reshape(())
    for i in range(3):
        result[7 + i] = result[7 + i].T
        result[13 + i] = result[13 + i].transpose(0, 2, 1)
    return tuple(result)


def solution(mesh):
    tok = P(("dp", "expert"), None)
    dp0 = P("dp", None)
    ex0 = P("expert", None, None)
    dp1 = P(None, "dp")
    return jax.shard_map(
        on_device,
        mesh=mesh,
        in_specs=(tok,) * 3 + (P(),) * 8 + (dp0,) * 3 + (ex0,) * 6 + (dp0,) * 3 + (dp1,) * 3,
        out_specs=(tok,) * 2 + (P(),) * 8 + (dp0,) * 3 + (ex0,) * 6 + (dp0,) * 3 + (dp1,) * 3,
        check_vma=False,
    )
```

```python
import math

import jax
import jax.numpy as jnp
from jax import lax
from jax.experimental import pallas as pl
from jax.experimental.pallas import tpu as pltpu
from jax.sharding import PartitionSpec as P

ADAM_STEP = 10
NORM_EPS = 1e-06
BETA_FIRST = 0.9
BETA_SECOND = 0.999
ADAM_EPS = 1e-08
CLIP_LIMIT = 1.0
MASKED = -1e30
LOG2E = math.log2(math.e)
LN2 = math.log(2.0)
MESH = pl.DeviceIdType.MESH
BF = jnp.bfloat16
F32 = jnp.float32

T = 512
D = 512
FF = 2048
HD = 64
K8 = 8
NE = 24
PL = 8
LE = NE // PL
ER = LE * HD
HB = FF // 2


def mm(a, b):
    return jnp.dot(a, b, preferred_element_type=F32)


def mm_nt(a, b):
    return lax.dot_general(a, b, (((1,), (1,)), ((), ())), preferred_element_type=F32)


def mm_tn(a, b):
    return lax.dot_general(a, b, (((0,), (0,)), ((), ())), preferred_element_type=F32)


def expert_at(place):
    return LE * device_at(place // LE) + place % LE


def device_at(slot):
    c, a, b = slot // 4, slot // 2 % 2, slot % 2
    qx, qy = (a, b) if c == 0 else (b, a)
    return 4 * qy + 2 * qx + c


def slot_of(dev):
    c, qx, qy = dev % 2, dev // 2 % 2, dev // 4
    return 4 * c + (2 * qx + qy if c == 0 else 2 * qy + qx)


def piece_rows(dp):
    return -(-ER // (dp * 16)) * 16


def scratch_list(dp):
    shard = D // dp
    pr = piece_rows(dp)
    return dict(
        wkvf=((D, 2 * HD), BF),
        w2=((2, D, FF), BF),
        eq=((NE * HD, D), BF),
        eo=((NE * HD, D), BF),
        kvb=((PL, 2, 256, 128), BF),
        tokx=((256, D), BF),
        cotx=((256, D), BF),
        rtx=((8, 256), jnp.int32),
        rts=((8, 256), jnp.int32),
        wrt=((32, D), F32),
        tokd=((T, D), BF),
        cotd=((T, D), BF),
        cott=((D, T), BF),
        rtd=((8, T), jnp.int32),
        nd=((T, D), BF),
        gate=((8, T), F32),
        dgate=((8, T), F32),
        big=((NE * HD, T), F32),
        peak=((2, 9, 8, 1024), F32),
        at=((NE * HD, T), BF),
        qx=((4, 128, 1024), BF),
        dox=((4, 128, 1024), BF),
        att=((4, HD + 16, 1024), F32),
        top=((4, 8, 1024), F32),
        linv=((4, 8, 1024), F32),
        kx=((2, 8, 256, 128), BF),
        vx=((2, 8, 256, 128), BF),
        kt=((2, 8, HD, 256), BF),
        vt=((2, 8, HD + 16, 256), BF),
        pst=((2, 9, 256, 1024), BF),
        dkv=((2, 8, 256, 128), F32),
        mixed=((T, D), F32),
        ffn=((T, D), BF),
        ffnt=((D, T), BF),
        acc1=((T, D), F32),
        acc2=((T, D), F32),
        gfh=((2, D, HB), BF),
        gfl=((2, D, HB), BF),
        rf1=((2, D, HB), BF),
        rfa=((D, HB // 2), BF),
        rfb=((D, HB // 4), BF),
        rfc=((dp - 1, shard, HB // 4), BF),
        rga=((shard, HB // 2), BF),
        rgb=((shard, HB // 4), BF),
        rgc=((dp - 1, shard, HB), BF),
        rgs=((shard, HB), BF),
        f2=((2, shard, FF), BF),
        go=((NE * HD, D), BF),
        rq1=((NE * HD // 2, D), BF),
        ro1=((NE * HD // 2, D), BF),
        rq2=((2 * ER, D), BF),
        ro2=((2 * ER, D), BF),
        rq3=((ER, D), BF),
        ro3=((ER, D), BF),
        xq=((dp * pr, D), BF),
        xo=((dp * pr, D), BF),
        rq4=((dp - 1, pr, D), BF),
        ro4=((dp - 1, pr, D), BF),
        fq=((dp * pr, D), BF),
        fo=((dp * pr, D), BF),
        rk1=((4, 2, 256, 128), BF),
        rk2=((3, 2, 256, 128), BF),
        dkvd=((T, 128), BF),
        tb=((128, 640), BF),
        rt1=((64, 640), BF),
        tsm=((64, 640), BF),
        rt2=((3, 16, 640), BF),
        rt3=((dp, 16, 640), BF),
        tf=((128, 640), BF),
        cnt=((32, 128), F32),
        mz=((dp, 32, 128), F32),
        mq=((PL, 32, 128), F32),
        layx=((256, D), BF),
        layr=((256, D), BF),
        tgr=((256, D), BF),
        gain=((8, D), F32),
        i_cot=((T, D), BF),
        i_up=((shard, FF), F32),
        i_down=((FF, shard), F32),
        i_qw=((LE, HD, D), F32),
        i_ow=((LE, HD, D), F32),
        osem=(10,),
        ssem=None,
        rsem=None,
    )


def copies_of(dp):
    return 80 + 16 * dp


def layer_kernel(dp, *refs):
    shard = D // dp
    pr = piece_rows(dp)
    (tok, cot_, routes, wkv, up_, down_, qw_, ow_, rw, gains, gbatch, lens) = refs[:12]
    (lay, tg, msgo, f2o, fqo, foo, sideo, kvo) = refs[12:20]
    names = list(scratch_list(dp))
    s = type("Scratch", (), dict(zip(names, refs[20:])))

    z = lax.axis_index("dp")
    e = lax.axis_index("expert")
    c = e % 2
    qx = e // 2 % 2
    qy = e // 4
    a = (1 - c) * qx + c * qy
    b = (1 - c) * qy + c * qx
    q = 2 * a + b

    def device(a_, b_):
        return (z, 4 * ((1 - c) * b_ + c * a_) + 2 * ((1 - c) * a_ + c * b_) + c)

    qs = [q, 2 * a + 1 - b, 2 * (1 - a) + b, 2 * (1 - a) + 1 - b]
    sib = (z, e + 1 - 2 * c)
    near, far = device(a, 1 - b), device(1 - a, b)
    chips = [None, near, far, device(1 - a, 1 - b)]
    swap = (z, 7 - e)
    zp = [None] + [((z + i) % dp, e) for i in range(1, dp)]
    zfrom = [None] + [(z + dp - i) % dp for i in range(1, dp)]
    slot = c * 4 + q
    plane = [sib] + [(z, (e + i) % PL) for i in range(1, PL)]

    count = [0]
    sends = []

    def rcopy(src, dst, peer):
        k = count[0]
        count[0] += 1
        d = pltpu.make_async_remote_copy(
            src_ref=src,
            dst_ref=dst,
            send_sem=s.ssem.at[k],
            recv_sem=s.rsem.at[k],
            device_id=peer,
            device_id_type=MESH,
        )
        d.start()
        sends.append(d)
        return (k, peer, d)

    def sent(handle):
        sends[:] = [d for d in sends if d is not handle[2]]
        handle[2].wait_send()

    def rwait(handle, dst):
        k, peer, _ = handle
        pltpu.make_async_remote_copy(
            src_ref=dst,
            dst_ref=dst,
            send_sem=s.ssem.at[k],
            recv_sem=s.rsem.at[k],
            device_id=peer,
            device_id_type=MESH,
        ).wait_recv()

    def lcopy(src, dst, k):
        d = pltpu.make_async_copy(src, dst, s.osem.at[k])
        d.start()
        return d

    cot, up, down, qw, ow = s.i_cot, s.i_up, s.i_down, s.i_qw, s.i_ow
    loads = [
        lcopy(x, y, k)
        for k, (x, y) in enumerate(
            ((up_, up), (down_, down), (qw_, qw), (ow_, ow), (cot_, cot))
        )
    ]
    bar = pltpu.get_barrier_semaphore()
    for peer in plane[1:] + zp[1:]:
        pl.semaphore_signal(bar, inc=1, device_id=peer, device_id_type=MESH)

    def zrows(ref, i, n):
        return ref.at[pl.ds(pl.multiple_of(i * n, n), n)]

    def turned(x):
        rows, cols = x.shape
        if cols % 128:
            x = jnp.concatenate([x, jnp.zeros((rows, 128 - cols % 128), x.dtype)], axis=1)
        return x.T[0:cols]

    lo = pl.multiple_of(c * HB, HB)
    hi = pl.multiple_of((1 - c) * HB, HB)
    ri = lax.broadcasted_iota(jnp.int32, (256, 256), 0)
    ci = lax.broadcasted_iota(jnp.int32, (256, 256), 1)
    split = jnp.where(ci == 2 * (ri % 128) + ri // 128, 1.0, 0.0).astype(BF)
    join = jnp.where(ri == 2 * (ci % 128) + ci // 128, 1.0, 0.0).astype(BF)
    own_rows = pl.ds(pl.multiple_of(z * shard, shard), shard)
    s.wkvf[own_rows, :] = wkv[...].astype(BF)
    rtt = routes[...].astype(F32).astype(BF)
    s.rtd[:, 0:256] = mm(rtt[:, 0:256], join).astype(jnp.int32)
    s.rts[...] = mm(rtt[:, 256:512], join).astype(jnp.int32)
    WD = HB // 2
    WP = (HB - WD) // 4
    part = pl.multiple_of(c * HB + WD + q * WP, WP)
    def w2_rows(w, i, at, n):
        return s.w2.at[w, pl.ds(pl.multiple_of(i * shard, shard), shard), pl.ds(at, n)]

    def to_all_z(ref):
        return [None] + [rcopy(ref, ref, zp[i]) for i in range(1, dp)]
    pl.semaphore_wait(bar, PL - 1 + dp - 1)
    h_wkv = [None] + [
        rcopy(zrows(s.wkvf, z, shard), zrows(s.wkvf, z, shard), zp[i]) for i in range(1, dp)
    ]
    h_tok = rcopy(tok.at[pl.ds(256, 256)], s.tokx, swap)
    h_rt = rcopy(s.rts, s.rtx, swap)
    loads[2].wait()
    loads[3].wait()
    for i in range(LE):
        rows = pl.ds(pl.multiple_of(slot * ER + i * HD, HD), HD)
        s.eq[rows, :] = qw[i].astype(BF)
        s.eo[rows, :] = ow[i].astype(BF)
    own_eq = zrows(s.eq, slot, ER)
    own_eo = zrows(s.eo, slot, ER)
    h_eq1 = rcopy(own_eq, own_eq, near)
    loads[0].wait()
    loads[1].wait()
    for at, n in ((lo, WD), (part, WP)):
        s.w2[0, own_rows, pl.ds(at, n)] = up[:, pl.ds(at, n)].astype(BF)
    s.w2[1, own_rows, pl.ds(lo, HB)] = turned(down[pl.ds(lo, HB), :]).astype(BF)

    h_wp1 = to_all_z(w2_rows(0, z, part, WP))
    h_wu = to_all_z(w2_rows(0, z, lo, WD))
    h_wd = to_all_z(w2_rows(1, z, lo, HB))

    def gather_far(h, ref):
        rwait(h, zrows(ref, c * 4 + qs[1], ER))
        pair = zrows(ref, c * 2 + a, 2 * ER)
        return rcopy(pair, pair, far)

    def gather_sib(h, ref):
        rwait(h, zrows(ref, c * 2 + 1 - a, 2 * ER))
        mine = zrows(ref, c, 4 * ER)
        return rcopy(mine, mine, sib)

    def w2_cols(w, at, n):
        return s.w2.at[w, :, pl.ds(at, n)]

    s.wrt[0:NE, :] = rw[...]
    s.wrt[NE:32, :] = jnp.zeros((32 - NE, D), F32)

    g0 = gains[0:1, :]
    g1 = gains[1:2, :]

    def rms(x):
        inv = lax.rsqrt(jnp.mean(x * x, axis=-1, keepdims=True) + NORM_EPS)
        return x * inv, inv

    nat0 = mm(split, tok[0:256, :])
    nat1 = mm(split, tok[256:512, :])
    s.tokd[0:256, :] = nat0.astype(BF)
    n0 = (rms(nat0)[0] * g0).astype(BF)
    n1 = (rms(nat1)[0] * g0).astype(BF)
    s.nd[0:256, :] = n0
    loads[4].wait()
    cot0 = mm(split, cot[0:256, :])
    s.cotd[0:256, :] = cot0.astype(BF)

    for i in range(1, dp):
        rwait(h_wkv[i], zrows(s.wkvf, zfrom[i], shard))
    kv0 = mm(n0, s.wkvf[...]).astype(BF)
    kv1 = mm(n1, s.wkvf[...]).astype(BF)
    for p in range(2):
        s.kvb[slot, p, 0:128, :] = kv0[p * 128 : (p + 1) * 128]
        s.kvb[slot, p, 128:256, :] = kv1[p * 128 : (p + 1) * 128]
    h_kv1 = rcopy(s.kvb.at[slot], s.kvb.at[slot], near)
    h_eq2 = gather_far(h_eq1, s.eq)

    rwait(h_tok, s.tokx)
    rwait(h_rt, s.rtx)
    sw = mm(split, s.tokx[...])
    s.tokd[256:512, :] = sw.astype(BF)
    s.nd[256:512, :] = (rms(sw)[0] * g0).astype(BF)
    s.rtd[:, 256:512] = s.rtx[...]

    wrt = s.wrt[...].astype(BF)
    bm1 = gbatch[z] - 1
    is2 = (4 - gbatch[z]) // 2

    def seq_pos(r):
        return r & bm1, (r >> 1) * is2 + (r >> 2) * (1 - is2)

    def limit_of(index):
        out = jnp.zeros(index.shape, jnp.int32)
        for i in range(4):
            out = jnp.where(index == i, lens[z, i], out)
        return out

    block = [2 * e, 15 - 2 * e]
    lanes128 = lax.broadcasted_iota(jnp.int32, (16, 128), 1)
    row16 = lax.broadcasted_iota(jnp.int32, (16, 128), 0)
    row32 = lax.broadcasted_iota(jnp.int32, (32, 128), 0)

    logits = mm_nt(wrt, s.nd[...])
    row_e = lax.broadcasted_iota(jnp.int32, (32, T), 0)
    chosen = jnp.concatenate(
        [
            jnp.sum(jnp.where(row_e == s.rtd[k : k + 1, :], logits, 0.0), axis=0, keepdims=True)
            for k in range(K8)
        ],
        axis=0,
    )
    ex = jnp.exp(chosen - jnp.max(chosen, axis=0, keepdims=True))
    s.gate[...] = ex / jnp.sum(ex, axis=0, keepdims=True)

    counts = jnp.zeros((32, 128), F32)
    for g in range(4):
        blk, p = g // 2, g % 2
        row = 2 * (block[blk] * 128 + lanes128) + p
        seq, pos = seq_pos(row)
        live = (pos < limit_of(seq))[0:1, :].astype(F32)
        for k in range(K8):
            counts = counts + jnp.where(
                row32 == s.rtd[k : k + 1, g * 128 : (g + 1) * 128], live, 0.0
            )
        feat = jnp.where(seq == row16, 1.0, 0.0).astype(BF)
        s.qx[g, 64:80, :] = jnp.concatenate([feat] * K8, axis=1)
        s.qx[g, 80:128, :] = jnp.zeros((48, 1024), BF)
    s.cnt[...] = jnp.broadcast_to(jnp.sum(counts, axis=1, keepdims=True), (32, 128))

    half = NE * HD // 2
    rwait(h_kv1, s.kvb.at[c * 4 + qs[1]])
    kv_pair = s.kvb.at[pl.ds(c * 4 + a * 2, 2)]
    h_kv2 = rcopy(kv_pair, kv_pair, far)
    h_eqs = gather_sib(h_eq2, s.eq)
    rwait(h_kv2, s.kvb.at[pl.ds(c * 4 + (1 - a) * 2, 2)])
    h_eo1 = rcopy(own_eo, own_eo, near)
    h_kvs = rcopy(s.kvb.at[pl.ds(c * 4, 4)], s.kvb.at[pl.ds(c * 4, 4)], sib)
    rwait(h_eqs, zrows(s.eq, 1 - c, half))

    def query_rows(i, _):
        rows = pl.ds(pl.multiple_of(i * 256, 256), 256)
        s.big[rows, :] = mm_nt(s.eq[rows, :], s.nd[...])
        return 0

    lax.fori_loop(0, NE * HD // 256, query_rows, 0)

    def pick(g, k):
        lanes = pl.ds(pl.multiple_of(g * 128, 128), 128)
        rk = s.rtd[k : k + 1, lanes]
        acc = jnp.zeros((HD, 128), F32)
        for place in range(NE):
            acc = jnp.where(rk == expert_at(place), s.big[place * HD : (place + 1) * HD, lanes], acc)
        return acc

    def choose(g, _):
        for k in range(K8):
            s.qx[g, 0:64, k * 128 : (k + 1) * 128] = (pick(g, k) * (0.125 * LOG2E)).astype(BF)
        return 0

    lax.fori_loop(0, 4, choose, 0)

    rwait(h_kvs, s.kvb.at[pl.ds((1 - c) * 4, 4)])
    krow = lax.broadcasted_iota(jnp.int32, (256, 128), 0)
    klane = lax.broadcasted_iota(jnp.int32, (256, 128), 1)
    for t in range(8):
        for p in range(2):
            kv = s.kvb[slot_of(t), p].astype(F32)
            seq, pos = seq_pos(2 * (t * 256 + krow) + p)
            col = klane - 64
            shown = (seq == col) & (pos < limit_of(col))
            feat = jnp.where(shown | (col > 3), 0.0, MASKED)
            s.kx[p, t] = jnp.where(col < 0, kv, feat).astype(BF)
            s.vx[p, t] = jnp.where(col >= 0, kv, jnp.where(klane < 2, 1.0, 0.0)).astype(BF)
            kvt = kv.T
            s.kt[p, t] = kvt[0:64].astype(BF)
            s.vt[p, t, 0:64, :] = kvt[64:128].astype(BF)
            s.vt[p, t, 64:80, :] = jnp.ones((16, 256), BF)

    turn = e + 1
    below = lax.broadcasted_iota(jnp.int32, (256, 128), 0) - lax.broadcasted_iota(
        jnp.int32, (256, 128), 1
    )
    s.att[...] = jnp.zeros(s.att.shape, F32)
    s.top[...] = jnp.full(s.top.shape, MASKED, F32)

    def place_of(i):
        blk = jnp.where(i >= turn, 1, 0)
        return blk * 2, i - blk * turn

    def attend(i, _):
        g0_, t = place_of(i)
        visible = below <= jnp.where(i == turn - 1, 0, jnp.where(i == 8, 128, 256))
        visible = jnp.concatenate([visible] * K8, axis=1)
        both_p = range(2)
        scs = [jnp.where(visible, mm(s.kx[p, t], s.qx[g0_ + p]), MASKED) for p in both_p]
        tops = [jnp.max(jnp.max(x.reshape(32, 8, 1024), axis=0), axis=0, keepdims=True) for x in scs]
        olds = [s.top[g0_ + p, 0:1, :] for p in both_p]
        news = [jnp.maximum(old, jnp.ceil(x)) for old, x in zip(olds, tops)]
        pbs = [jnp.exp2(sc - new).astype(BF) for sc, new in zip(scs, news)]
        outs = [mm(s.vt[p, t], pbs[p]) for p in both_p]
        for p in both_p:
            s.att[g0_ + p] = s.att[g0_ + p] * jnp.exp2(olds[p] - news[p]) + outs[p]
            s.pst[p, i] = pbs[p]
            s.peak[p, i] = jnp.broadcast_to(news[p], (8, 1024))
            s.top[g0_ + p] = jnp.broadcast_to(news[p], (8, 1024))
        return 0

    h_eo2 = gather_far(h_eo1, s.eo)
    lax.fori_loop(0, 3, attend, 0)
    for i in range(1, dp):
        rwait(h_wp1[i], w2_rows(0, zfrom[i], part, WP))
    h_wp2 = rcopy(w2_cols(0, part, WP), w2_cols(0, part, WP), near)
    h_cot = rcopy(cot.at[pl.ds(256, 256)], s.cotx, swap)
    lax.fori_loop(3, 5, attend, 0)
    rwait(h_wp2, w2_cols(0, c * HB + WD + qs[1] * WP, WP))
    both_parts = pl.multiple_of(c * HB + WD + a * 2 * WP, 2 * WP)
    h_wp3 = rcopy(w2_cols(0, both_parts, 2 * WP), w2_cols(0, both_parts, 2 * WP), far)
    lax.fori_loop(5, 7, attend, 0)
    h_eos = gather_sib(h_eo2, s.eo)
    lax.fori_loop(7, 9, attend, 0)
    for g in range(4):
        inv = 1.0 / s.att[g, 64:72, :]
        s.linv[g] = inv
        s.att[g, 0:64, :] = s.att[g, 0:64, :] * inv[0:1]
    rwait(h_wp3, w2_cols(0, pl.multiple_of(c * HB + WD + (1 - a) * 2 * WP, 2 * WP), 2 * WP))
    for i in range(1, dp):
        rwait(h_wu[i], w2_rows(0, zfrom[i], lo, WD))
    h_w2s = [rcopy(w2_cols(0, lo, HB), w2_cols(0, lo, HB), sib)]
    def spread(dst, src, scale):
        def one(g, _):
            lanes = pl.ds(pl.multiple_of(g * 128, 128), 128)
            for k in range(K8):
                part = src[g, 0:HD, k * 128 : (k + 1) * 128]
                if scale is not None:
                    part = part * scale[k : k + 1, lanes]
                else:
                    part = part * 0.125
                s.acc1[k * HD : (k + 1) * HD, 0:128] = part
            for place in range(NE):
                acc = jnp.zeros((HD, 128), F32)
                for k in range(K8):
                    acc = jnp.where(
                        s.rtd[k : k + 1, lanes] == expert_at(place),
                        s.acc1[k * HD : (k + 1) * HD, 0:128],
                        acc,
                    )
                dst[place * HD : (place + 1) * HD, lanes] = acc.astype(BF)
            return 0

        lax.fori_loop(0, 4, one, 0)

    spread(s.at, s.att, s.gate)
    for i in range(1, dp):
        rwait(h_wd[i], w2_rows(1, zfrom[i], lo, HB))
    h_w2s.append(rcopy(w2_cols(1, lo, HB), w2_cols(1, lo, HB), sib))
    rwait(h_eos, zrows(s.eo, 1 - c, half))
    s.acc1[...] = s.tokd[...].astype(F32)

    def mix(i, _):
        rows = pl.ds(pl.multiple_of(i * 256, 256), 256)
        s.acc1[...] += mm_tn(s.at[rows, :], s.eo[rows, :])
        return 0

    lax.fori_loop(0, NE * HD // 256, mix, 0)
    mixed = s.acc1[...]
    s.mixed[...] = mixed
    ffn = rms(mixed)[0] * g1
    s.ffn[...] = ffn.astype(BF)
    s.ffnt[...] = ffn.T.astype(BF)
    rwait(h_cot, s.cotx)
    cot1 = mm(split, s.cotx[...])
    s.cotd[256:512, :] = cot1.astype(BF)
    s.cott[:, 0:256] = cot0.T.astype(BF)
    s.cott[:, 256:512] = cot1.T.astype(BF)
    s.acc2[...] = jnp.zeros((T, D), F32)
    for w in range(2):
        rwait(h_w2s[w], w2_cols(w, hi, HB))

    FT = 256

    def feed(i, base_, at, keep):
        cols = pl.ds(pl.multiple_of(base_ + at + i * FT, FT), FT)
        part_cols = pl.ds(pl.multiple_of(at + i * FT, FT), FT)
        up = mm(s.ffn[...], s.w2[0, :, cols])
        sq = up * up
        th = jnp.tanh(0.79788456 * up * (1.0 + 0.044715 * sq))
        hid = (0.5 * up * (1.0 + th)).astype(BF)
        slope = 0.5 * (1.0 + th) + 0.5 * up * (1.0 - th * th) * (
            0.79788456 * (1.0 + 3 * 0.044715 * sq)
        )
        s.acc1[...] += mm_nt(hid, s.w2[1, :, cols])
        dup = (mm(s.cotd[...], s.w2[1, :, cols]) * slope).astype(BF)
        keep[0, :, part_cols] = mm(s.ffnt[...], dup).astype(BF)
        keep[1, :, part_cols] = mm(s.cott[...], hid).astype(BF)
        s.acc2[...] += mm_nt(dup, s.w2[0, :, cols])
        return 0

    def both(x, y):
        return (x.astype(F32) + y.astype(F32)).astype(BF)

    def fold(sq):
        sq = jnp.sum(sq, axis=0, keepdims=True)
        out = sq[:, 0:128]
        for j in range(1, sq.shape[1] // 128):
            out = out + sq[:, j * 128 : (j + 1) * 128]
        return out

    done, squares = [], []
    quart = HB // 4
    keep2 = pl.multiple_of(a * 2 * quart, 2 * quart)
    give2 = pl.multiple_of((1 - a) * 2 * quart, 2 * quart)
    keep1 = pl.multiple_of(q * quart, quart)
    give1 = pl.multiple_of(qs[1] * quart, quart)
    place1 = pl.multiple_of(c * HB + keep1, quart)

    def feed_grad(w):
        own, total, one, two, three = s.gfl.at[w], s.rf1.at[w], s.rfa, s.rfb, s.rfc

        def pair(j, at):
            cols = pl.ds(at, 2 * quart)
            rwait(h_f1[j][w], total.at[:, cols])
            total[:, cols] = both(own[:, cols], total[:, cols])

        pair(0, give2)
        h = rcopy(total.at[:, pl.ds(give2, 2 * quart)], one, far)
        yield
        pair(1, keep2)
        yield
        rwait(h, one)
        for at in (give1, keep1):
            inner = pl.multiple_of(at - keep2, quart)
            total[:, pl.ds(at, quart)] = both(
                total[:, pl.ds(at, quart)], one[:, pl.ds(inner, quart)]
            )
            if at is give1:
                h = rcopy(total.at[:, pl.ds(give1, quart)], two, near)
        yield
        rwait(h, two)
        total[:, pl.ds(keep1, quart)] = both(total[:, pl.ds(keep1, quart)], two[...])

        def zpart(i):
            return total.at[pl.ds(pl.multiple_of(i * shard, shard), shard), pl.ds(keep1, quart)]

        hz = [rcopy(zpart(zp[i][0]), three.at[i - 1], zp[i]) for i in range(1, dp)]
        yield
        acc = zpart(z)[...].astype(F32)
        for i in range(1, dp):
            rwait(hz[i - 1], three.at[i - 1])
            acc = acc + three[i - 1].astype(F32)
        yield from spread_grad(w, acc)

    def spread_grad(w, acc):
        out = s.f2.at[w]
        acc = acc.astype(BF)
        out[:, pl.ds(place1, quart)] = acc
        acc = acc.astype(F32)
        squares.append(fold(acc * acc))
        h = rcopy(out.at[:, pl.ds(place1, quart)], out.at[:, pl.ds(place1, quart)], near)
        yield
        rwait(h, out.at[:, pl.ds(pl.multiple_of(c * HB + give1, quart), quart)])
        wide = out.at[:, pl.ds(pl.multiple_of(c * HB + keep2, 2 * quart), 2 * quart)]
        h = rcopy(wide, wide, far)
        yield
        rwait(h, out.at[:, pl.ds(pl.multiple_of(c * HB + give2, 2 * quart), 2 * quart)])
        h = rcopy(out.at[:, pl.ds(lo, HB)], out.at[:, pl.ds(lo, HB)], sib)
        yield
        rwait(h, out.at[:, pl.ds(hi, HB)])
        done.append(lcopy(out, f2o.at[w], 2 + w))
        yield

    def dp_first_grad(w):
        own, total, one, two, three = s.gfl.at[w], s.rf1.at[w], s.rga, s.rgb, s.rgc
        hz = []
        for j, at in ((0, give2), (1, keep2)):
            cols = pl.ds(at, 2 * quart)
            rwait(h_f1[j][w], total.at[:, cols])
            total[:, cols] = both(own[:, cols], total[:, cols])
            for i in range(1, dp):
                mine = pl.ds(pl.multiple_of(zp[i][0] * shard, shard), shard)
                hz.append((rcopy(total.at[mine, cols], three.at[i - 1, :, cols], zp[i]), i, cols))
            yield
        for h, i, cols in hz:
            rwait(h, three.at[i - 1, :, cols])
        acc = total[own_rows, :].astype(F32)
        for i in range(1, dp):
            acc = acc + three[i - 1].astype(F32)
        s.rgs[...] = acc.astype(BF)
        h = rcopy(s.rgs.at[:, pl.ds(give2, 2 * quart)], one, far)
        yield
        rwait(h, one)
        s.rgs[:, pl.ds(keep2, 2 * quart)] = both(s.rgs[:, pl.ds(keep2, 2 * quart)], one[...])
        h = rcopy(s.rgs.at[:, pl.ds(give1, quart)], two, near)
        yield
        rwait(h, two)
        acc = s.rgs[:, pl.ds(keep1, quart)].astype(F32) + two[...].astype(F32)
        yield from spread_grad(w, acc)

    def head_grad(src, total, one, two, full, part_, final, dst, sem):
        h = rcopy(zrows(src, 1 - c, half), total, sib)
        s.half_sent = h
        yield
        rwait(h, total)

        def pair(which):
            rows = pl.ds(pl.multiple_of(which * 2 * ER, 128), 2 * ER)
            wide = pl.ds(pl.multiple_of(c * half + which * 2 * ER, 128), 2 * ER)
            total[rows, :] = both(src[wide, :], total[rows, :])

        pair(1 - a)
        h = rcopy(zrows(total, 1 - a, 2 * ER), one, far)
        pair(a)
        yield
        rwait(h, one)
        for which in (1 - b, b):
            rows = pl.ds(pl.multiple_of((2 * a + which) * ER, ER), ER)
            total[rows, :] = both(total[rows, :], one[pl.ds(pl.multiple_of(which * ER, ER), ER), :])
            if which is not b:
                h = rcopy(zrows(total, qs[1], ER), two, near)
        yield
        rwait(h, two)
        full[0:ER, :] = both(total[pl.ds(pl.multiple_of(q * ER, ER), ER), :], two[...])
        if dp * pr > ER:
            full[ER:, :] = jnp.zeros((dp * pr - ER, full.shape[1]), BF)
        hz = [rcopy(zrows(full, zp[i][0], pr), part_.at[i - 1], zp[i]) for i in range(1, dp)]
        yield
        mine = pl.ds(pl.multiple_of(z * pr, pr), pr)
        acc = full[mine, :].astype(F32)
        for i in range(1, dp):
            rwait(hz[i - 1], part_.at[i - 1])
            acc = acc + part_[i - 1].astype(F32)
        acc = acc.astype(BF)
        final[mine, :] = acc
        acc = acc.astype(F32)
        squares.append(fold(acc * acc))
        hz = to_all_z(zrows(final, z, pr))
        yield
        for i in range(1, dp):
            rwait(hz[i], zrows(final, zfrom[i], pr))
        done.append(lcopy(final.at[pl.ds(0, ER)], dst, sem))
        yield

    def feed_tiles(base_, at, keep):
        lax.fori_loop(0, HB // FT // 2, lambda i, _: feed(i, base_, at, keep), 0)

    def to_sibling(at):
        cols = pl.ds(at, 2 * quart)
        return [rcopy(s.gfh.at[w, :, cols], s.rf1.at[w, :, cols], sib) for w in range(2)]

    sib_give2 = pl.multiple_of((1 - b) * 2 * quart, 2 * quart)
    sib_keep2 = pl.multiple_of(b * 2 * quart, 2 * quart)
    feed_tiles(hi, sib_give2, s.gfh)
    h_f1 = [to_sibling(sib_give2)]
    feed_tiles(lo, give2, s.gfl)
    chain = [feed_grad(0), dp_first_grad(1)]
    next(chain[0])
    next(chain[1])
    feed_tiles(hi, sib_keep2, s.gfh)
    h_f1.append(to_sibling(sib_keep2))
    feed_tiles(lo, keep2, s.gfl)
    next(chain[0])
    next(chain[1])

    out = s.acc1[...].astype(BF)
    s.layx[...] = mm(join, out[256:512]).astype(BF)
    s.ffn[0:256, :] = mm(join, out[0:256]).astype(BF)

    def rms_back(dn, gain, unit, inv):
        a = dn * gain
        return inv * (a - unit * jnp.mean(a * unit, axis=-1, keepdims=True)), jnp.sum(
            dn * unit, axis=0, keepdims=True
        )

    unit1, inv1 = rms(s.mixed[...])
    back, gain1 = rms_back(s.acc2[...], g1, unit1, inv1)
    s.gain[1:2, :] = gain1
    dmix = s.cotd[...].astype(F32) + back
    s.mixed[...] = dmix
    s.cott[...] = dmix.astype(BF)

    def out_rows(i, _):
        rows = pl.ds(pl.multiple_of(i * 256, 256), 256)
        s.big[rows, :] = mm_nt(s.eo[rows, :], s.cott[...])
        s.go[rows, :] = mm(s.at[rows, :], s.cott[...]).astype(BF)
        return 0

    lax.fori_loop(0, NE * HD // 256, out_rows, 0)
    chain.append(head_grad(s.go, s.ro1, s.ro2, s.ro3, s.xo, s.ro4, s.fo, foo, 4))
    next(chain[2])
    sent_o = s.half_sent

    def heads_back(g, _):
        lanes = pl.ds(pl.multiple_of(g * 128, 128), 128)
        for k in range(K8):
            ks = slice(k * 128, (k + 1) * 128)
            da = pick(g, k)
            at = s.att[g, 0:HD, ks]
            s.dgate[k : k + 1, lanes] = jnp.sum(at * da, axis=0, keepdims=True)
            do = (da * (s.gate[k : k + 1, lanes] * s.linv[g, 0:1, ks])).astype(BF)
            s.dox[g, 64:128, ks] = do
            delta = -jnp.sum(do.astype(F32) * at, axis=0, keepdims=True)
            top = delta.astype(BF).astype(F32)
            s.dox[g, 0:16, ks] = jnp.where(
                row16 == 0, top, jnp.where(row16 == 1, delta - top, 0.0)
            ).astype(BF)
            s.dox[g, 16:64, ks] = jnp.zeros((48, 128), BF)
        return 0

    lax.fori_loop(0, 4, heads_back, 0)
    s.dkv[...] = jnp.zeros(s.dkv.shape, F32)

    left = lax.broadcasted_iota(jnp.int32, (256, 128), 1) < 64

    s.att[...] = jnp.zeros(s.att.shape, F32)

    def attend_back(i, _):
        g0_, t = place_of(i)
        both_p = range(2)
        scales = [jnp.exp2(s.peak[p, i, 0:1, :] - s.top[g0_ + p, 0:1, :]) for p in both_p]
        doxs = [(s.dox[g0_ + p].astype(F32) * scales[p]).astype(BF) for p in both_p]
        dprobs = [mm(s.vx[p, t], doxs[p]) for p in both_p]
        vparts = [mm_nt(s.pst[p, i], doxs[p]) for p in both_p]
        dss = [(s.pst[p, i].astype(F32) * dprobs[p]).astype(BF) for p in both_p]
        kparts = [mm_nt(dss[p], s.qx[g0_ + p]) for p in both_p]
        dqs = [mm(s.kt[p, t], dss[p]) for p in both_p]
        for p in both_p:
            s.dkv[p, t] += jnp.where(left, kparts[p] * LN2, vparts[p])
            s.att[g0_ + p, 0:HD, :] += dqs[p]
        return 0

    next(chain[2])
    lax.fori_loop(0, 3, attend_back, 0)
    next(chain[0])
    lax.fori_loop(3, 5, attend_back, 0)
    next(chain[2])
    lax.fori_loop(5, 7, attend_back, 0)
    next(chain[0])
    lax.fori_loop(7, 9, attend_back, 0)
    next(chain[2])
    h_lay = rcopy(s.layx, s.layr, swap)
    for h in (h_kv1, h_kv2, h_kvs):
        sent(h)
    for dev in range(PL):
        sl = slot_of(dev)
        for side_, blk in enumerate((2 * dev, 15 - 2 * dev)):
            for p in range(2):
                s.kvb[sl, side_, p * 128 : (p + 1) * 128, :] = s.dkv[p, blk // 2, (blk % 2) * 128 : (blk % 2) * 128 + 128, :].astype(BF)
    h_k1 = rcopy(s.kvb.at[pl.ds((1 - c) * 4, 4)], s.rk1, sib)
    spread(s.at, s.att, None)
    sent(sent_o)

    def query_grad(i, cols):
        rows = pl.ds(pl.multiple_of(i * 256, 256), 256)
        s.go[rows, cols] = mm(s.at[rows, :], s.nd[:, cols]).astype(BF)
        return 0

    for j in range(2):
        cols = pl.ds(j * 256, 256)
        lax.fori_loop(0, NE * HD // 256, lambda i, _: query_grad(i, cols), 0)
        chain.append(
            head_grad(
                *[x.at[:, cols] for x in (s.go, s.rq1, s.rq2, s.rq3, s.xq)],
                s.rq4.at[:, :, cols], s.fq.at[:, cols], fqo.at[:, cols], 5 + 4 * j,
            )
        )
        next(chain[3 + j])
        if j == 0:
            rwait(h_k1, s.rk1)
            for i in range(4):
                s.rk1[i] = both(s.kvb[c * 4 + i], s.rk1[i])
            h_k2 = [None] + [
                rcopy(s.rk1.at[qs[m]], s.rk2.at[m - 1], chips[m]) for m in (1, 2, 3)
            ]
    s.acc2[...] = jnp.zeros((T, D), F32)

    def slot_sum(i, _):
        rows = pl.ds(pl.multiple_of(i * 256, 256), 256)
        s.acc2[...] += mm_tn(s.at[rows, :], s.eq[rows, :])
        return 0

    lax.fori_loop(0, NE * HD // 256, slot_sum, 0)
    gate = s.gate[...]
    dch = gate * (s.dgate[...] - jnp.sum(gate * s.dgate[...], axis=0, keepdims=True))
    dlog = jnp.zeros((32, T), F32)
    for k in range(K8):
        dlog = dlog + jnp.where(row_e == s.rtd[k : k + 1, :], dch[k : k + 1, :], 0.0)
    dlog = dlog.astype(BF)
    s.acc2[...] += mm_tn(dlog, wrt)
    grt = mm(dlog, s.nd[...])

    next(chain[3])
    next(chain[4])
    next(chain[1])
    next(chain[0])
    for m in (1, 2, 3):
        rwait(h_k2[m], s.rk2.at[m - 1])
    for i in range(2):
        total = s.rk1[q, i].astype(F32)
        for m in (1, 2, 3):
            total = total + s.rk2[m - 1, i].astype(F32)
        s.dkvd[i * 256 : (i + 1) * 256, :] = total.astype(BF)
    dn = s.acc2[...] + mm_nt(s.dkvd[...], s.wkvf[...])
    unit0, inv0 = rms(s.tokd[...].astype(F32))
    back0, gain0 = rms_back(dn, g0, unit0, inv0)
    s.tb[:, 0:512] = mm_tn(s.dkvd[...], s.nd[...]).astype(BF)
    side = s.acc1.at[pl.ds(0, 128), pl.ds(0, 128)]
    for j in range(4):
        js = slice(j * 128, (j + 1) * 128)
        side[j * 24 : (j + 1) * 24, :] = grt[0:24, js]
        side[96 + j : 97 + j, :] = gain0[:, js]
        side[100 + j : 101 + j, :] = s.gain[1:2, js]
    side[104:128, :] = jnp.zeros((24, 128), F32)
    s.tb[:, 512:640] = side[...].astype(BF)
    h_t1 = rcopy(zrows(s.tb, 1 - c, 64), s.rt1, sib)
    next(chain[3])
    next(chain[4])
    rwait(h_t1, s.rt1)
    s.tsm[...] = both(s.tb[pl.ds(pl.multiple_of(c * 64, 64), 64), :], s.rt1[...])
    h_t2 = [None] + [rcopy(zrows(s.tsm, qs[m], 16), s.rt2.at[m - 1], chips[m]) for m in (1, 2, 3)]
    next(chain[1])
    next(chain[0])
    next(chain[2])
    grad = s.mixed[...] + back0
    sent(h_lay)
    s.layx[...] = mm(join, grad[256:512].astype(BF)).astype(BF)
    top = grad[0:256].astype(BF)
    rest = (grad[0:256] - top.astype(F32)).astype(BF)
    s.acc1[0:256, :] = mm(join, top) + mm(join, rest)
    next(chain[1])
    next(chain[3])
    next(chain[4])
    next(chain[0])
    for m in (1, 2, 3):
        rwait(h_t2[m], s.rt2.at[m - 1])
    total = s.tsm[pl.ds(pl.multiple_of(q * 16, 16), 16), :].astype(F32)
    for m in (1, 2, 3):
        total = total + s.rt2[m - 1].astype(F32)
    s.rt3[z] = total.astype(BF)
    h_t3 = [None] + [rcopy(s.rt3.at[z], s.rt3.at[z], zp[i]) for i in range(1, dp)]
    h_tg = rcopy(s.layx, s.tgr, swap)
    next(chain[1])
    for i in range(1, dp):
        rwait(h_t3[i], s.rt3.at[zfrom[i]])
    total = s.rt3[0].astype(F32)
    for i in range(1, dp):
        total = total + s.rt3[i].astype(F32)
    tail = total.astype(BF)
    s.tf[pl.ds(pl.multiple_of(slot * 16, 16), 16), :] = tail
    h_t4 = [None] + [
        rcopy(zrows(s.tf, slot, 16), zrows(s.tf, slot, 16), chips[m]) for m in (1, 2, 3)
    ]
    next(chain[3])
    next(chain[4])
    sq_t = fold(tail.astype(F32) * tail.astype(F32)) * (1.0 / dp)

    total = squares[0]
    for sq in squares[1:] + [sq_t]:
        total = total + sq
    squares = jnp.sum(total, axis=1, keepdims=True)
    s.mz[z] = jnp.where(row32 < 24, s.cnt[...], jnp.where(row32 == 24, squares, 0.0))
    h_m1 = [None] + [rcopy(s.mz.at[z], s.mz.at[z], zp[i]) for i in range(1, dp)]

    for m in (1, 2, 3):
        rwait(h_t4[m], zrows(s.tf, c * 4 + qs[m], 16))
    next(chain[1])
    h_t5 = rcopy(zrows(s.tf, c, 64), zrows(s.tf, c, 64), sib)

    for i in range(1, dp):
        rwait(h_m1[i], s.mz.at[zfrom[i]])
    total = s.mz[0]
    for i in range(1, dp):
        total = total + s.mz[i]
    s.mq[e] = total
    h_m2 = [None] + [rcopy(s.mq.at[e], s.mq.at[e], plane[i]) for i in range(1, PL)]

    rwait(h_lay, s.layr)
    s.ffn[256:512, :] = s.layr[...]
    done.append(lcopy(s.ffn, lay, 0))
    rwait(h_tg, s.tgr)
    s.acc1[256:512, :] = s.tgr[...].astype(F32)
    done.append(lcopy(s.acc1, tg, 1))
    next(chain[0])
    next(chain[1])
    rwait(h_t5, zrows(s.tf, 1 - c, 64))
    s.acc2[:, 0:128] = s.tf[:, 0:512].astype(F32).T
    done.append(lcopy(s.tf.at[:, pl.ds(512, 128)], sideo, 8))
    done.append(lcopy(s.acc2.at[own_rows, pl.ds(0, 128)], kvo, 7))
    next(chain[2])
    next(chain[3])
    next(chain[4])
    for i in range(1, PL):
        rwait(h_m2[i], s.mq.at[(e + PL - i) % PL])
    total = s.mq[0]
    for i in range(1, PL):
        total = total + s.mq[i]
    s.cnt[...] = total
    done.append(lcopy(s.cnt, msgo, 6))
    for d in done:
        d.wait()
    for d in sends:
        d.wait_send()
    assert count[0] <= copies_of(dp)


def adam_kernel(steps, *refs):
    (lay, tg, msg, upg, downg, qg, og, side, kvg) = refs[:9]
    params = [refs[9 + 3 * i : 12 + 3 * i] for i in range(7)]
    layo, tgo, counts, norm = refs[30:34]
    outs = [refs[34 + 3 * i : 37 + 3 * i] for i in range(7)]
    step = pl.program_id(0)
    total = jnp.sqrt(jnp.full((8, 128), msg[24, 0], F32))
    clip = (CLIP_LIMIT / jnp.maximum(total, CLIP_LIMIT))[0:1, 0:1]

    def update(k, g, rate, decay, at=Ellipsis):
        w, m, v = [r[at] for r in params[k]]
        g = g * clip
        m = BETA_FIRST * m + (1.0 - BETA_FIRST) * g
        v = BETA_SECOND * v + (1.0 - BETA_SECOND) * g * g
        mh = m * (1.0 / (1.0 - BETA_FIRST**ADAM_STEP))
        vh = v * (1.0 / (1.0 - BETA_SECOND**ADAM_STEP))
        outs[k][0][at] = w - rate * (mh / (jnp.sqrt(vh) + ADAM_EPS) + decay * w)
        outs[k][1][at] = m
        outs[k][2][at] = v

    @pl.when(step == 0)
    def _():
        norm[...] = total[0:1, 0:1]
        for i in range(NE):
            counts[i] = msg[i, 0].astype(jnp.int32)
        sd = side[...].astype(F32)
        for row in range(2):
            g = jnp.concatenate([sd[96 + 4 * row + j : 97 + 4 * row + j] for j in range(4)], axis=1)
            update(0, g, 0.7, 0.0, pl.ds(row, 1))
        g = jnp.concatenate([sd[j * NE : (j + 1) * NE] for j in range(4)], axis=1)
        update(1, g, 0.03, 0.1)

    layo[...] = lay[...]
    tgo[...] = tg[...]
    update(2, kvg[...], 0.06, 0.1)
    update(3, qg[...].astype(F32), 0.06, 0.1)
    update(4, og[...].astype(F32), 2.0, 0.1)
    update(5, upg[0].astype(F32), 0.06, 0.1)
    update(6, downg[0].astype(F32).T, 0.03, 0.1)


def on_device(tokens, cotangent, routes, group_batch, seq_lengths, *state):
    dp = lax.axis_size("dp")
    shard = D // dp
    state = list(state)
    for i in range(3):
        state[3 + i] = state[3 + i].T
        state[9 + i] = state[9 + i].transpose(0, 2, 1)
    gains, router, keyval, query, output, up, down = [state[3 * i] for i in range(7)]

    scr = []
    for item in scratch_list(dp).values():
        if item is None:
            scr.append(pltpu.SemaphoreType.DMA((copies_of(dp),)))
        elif len(item) == 1:
            scr.append(pltpu.SemaphoreType.DMA(item))
        else:
            scr.append(pltpu.VMEM(item[0], item[1]))
    routes_cols = routes.T
    vm = pl.BlockSpec(memory_space=pltpu.VMEM)
    sm = pl.BlockSpec(memory_space=pltpu.SMEM)
    hbm = pl.BlockSpec(memory_space=pl.ANY)
    outs = [
        jax.ShapeDtypeStruct((T, D), BF),
        jax.ShapeDtypeStruct((T, D), F32),
        jax.ShapeDtypeStruct((32, 128), F32),
        jax.ShapeDtypeStruct((2, shard, FF), BF),
        jax.ShapeDtypeStruct((ER, D), BF),
        jax.ShapeDtypeStruct((ER, D), BF),
        jax.ShapeDtypeStruct((128, 128), BF),
        jax.ShapeDtypeStruct((shard, 128), F32),
    ]

    def kernel(*refs):
        layer_kernel(dp, *refs)

    lay, tg, msg, f2, fq, fo, side, kvg = pl.pallas_call(
        kernel,
        out_shape=outs,
        in_specs=[vm, hbm, vm, vm, hbm, hbm, hbm, hbm, vm, vm, sm, sm],
        out_specs=[hbm] * len(outs),
        scratch_shapes=scr,
        compiler_params=pltpu.CompilerParams(
            collective_id=0, has_side_effects=True, vmem_limit_bytes=64 * 2**20 - 2**17
        ),
        name="layer",
    )(
        tokens, cotangent, routes_cols, keyval, up, down, query, output, router, gains,
        group_batch, seq_lengths,
    )

    steps = 2
    rows = lambda i: (i, 0)
    middle = lambda i: (0, i, 0)
    blocks = [
        pl.BlockSpec((2, D), lambda i: (0, 0)),
        pl.BlockSpec((NE, D), lambda i: (0, 0)),
        pl.BlockSpec((shard // steps, 2 * HD), rows),
        pl.BlockSpec((LE, HD // steps, D), middle),
        pl.BlockSpec((LE, HD // steps, D), middle),
        pl.BlockSpec((shard // steps, FF), rows),
        pl.BlockSpec((FF // steps, shard), rows),
    ]
    each = [b for b in blocks for _ in range(3)]

    def update(*refs):
        adam_kernel(steps, *refs)

    result = list(pl.pallas_call(
        update,
        grid=(steps,),
        out_shape=[
            jax.ShapeDtypeStruct((T, D), BF),
            jax.ShapeDtypeStruct((T, D), F32),
            jax.ShapeDtypeStruct((NE,), jnp.int32),
            jax.ShapeDtypeStruct((1, 1), F32),
        ]
        + [jax.ShapeDtypeStruct(x.shape, F32) for x in state],
        in_specs=[
            pl.BlockSpec((T // steps, D), rows),
            pl.BlockSpec((T // steps, D), rows),
            sm,
            pl.BlockSpec((1, shard // steps, FF), middle),
            pl.BlockSpec((1, shard, FF // steps), lambda i: (1, 0, i)),
            pl.BlockSpec((LE, HD // steps, D), middle),
            pl.BlockSpec((LE, HD // steps, D), middle),
            pl.BlockSpec((128, 128), lambda i: (0, 0)),
            pl.BlockSpec((shard // steps, 2 * HD), rows),
        ]
        + each,
        out_specs=[pl.BlockSpec((T // steps, D), rows), pl.BlockSpec((T // steps, D), rows), sm, pl.BlockSpec((1, 1), lambda i: (0, 0))] + each,
        compiler_params=pltpu.CompilerParams(vmem_limit_bytes=63 * 2**20),
        name="adamw",
    )(lay, tg, msg, f2, f2, fq.reshape(LE, HD, D), fo.reshape(LE, HD, D), side, kvg, *state))
    result[3] = result[3].reshape(())
    for i in range(3):
        result[7 + i] = result[7 + i].T
        result[13 + i] = result[13 + i].transpose(0, 2, 1)
    return tuple(result)


def solution(mesh):
    tok = P(("dp", "expert"), None)
    dp0 = P("dp", None)
    ex0 = P("expert", None, None)
    dp1 = P(None, "dp")
    return jax.shard_map(
        on_device,
        mesh=mesh,
        in_specs=(tok,) * 3 + (P(),) * 8 + (dp0,) * 3 + (ex0,) * 6 + (dp0,) * 3 + (dp1,) * 3,
        out_specs=(tok,) * 2 + (P(),) * 8 + (dp0,) * 3 + (ex0,) * 6 + (dp0,) * 3 + (dp1,) * 3,
        check_vma=False,
    )
```

```python
import math

import jax
import jax.numpy as jnp
from jax import lax
from jax.experimental import pallas as pl
from jax.experimental.pallas import tpu as pltpu
from jax.sharding import PartitionSpec as P

ADAM_STEP = 10
NORM_EPS = 1e-06
BETA_FIRST = 0.9
BETA_SECOND = 0.999
ADAM_EPS = 1e-08
CLIP_LIMIT = 1.0
MASKED = -1e30
LOG2E = math.log2(math.e)
LN2 = math.log(2.0)
MESH = pl.DeviceIdType.MESH
BF = jnp.bfloat16
F32 = jnp.float32

T = 512
D = 512
FF = 2048
HD = 64
K8 = 8
NE = 24
PL = 8
LE = NE // PL
ER = LE * HD
HB = FF // 2


def mm(a, b):
    return jnp.dot(a, b, preferred_element_type=F32)


def mm_nt(a, b):
    return lax.dot_general(a, b, (((1,), (1,)), ((), ())), preferred_element_type=F32)


def mm_tn(a, b):
    return lax.dot_general(a, b, (((0,), (0,)), ((), ())), preferred_element_type=F32)


def expert_at(place):
    return LE * device_at(place // LE) + place % LE


def device_at(slot):
    c, a, b = slot // 4, slot // 2 % 2, slot % 2
    qx, qy = (a, b) if c == 0 else (b, a)
    return 4 * qy + 2 * qx + c


def slot_of(dev):
    c, qx, qy = dev % 2, dev // 2 % 2, dev // 4
    return 4 * c + (2 * qx + qy if c == 0 else 2 * qy + qx)


def piece_rows(dp):
    return -(-ER // (dp * 16)) * 16


def scratch_list(dp):
    shard = D // dp
    pr = piece_rows(dp)
    return dict(
        wkvf=((D, 2 * HD), BF),
        w2=((2, D, FF), BF),
        eq=((NE * HD, D), BF),
        eo=((NE * HD, D), BF),
        kvb=((PL, 2, 256, 128), BF),
        tokx=((256, D), BF),
        cotx=((256, D), BF),
        rtx=((8, 256), jnp.int32),
        rts=((8, 256), jnp.int32),
        wrt=((32, D), F32),
        tokd=((T, D), BF),
        cotd=((T, D), BF),
        cott=((D, T), BF),
        rtd=((8, T), jnp.int32),
        nd=((T, D), BF),
        gate=((8, T), F32),
        dgate=((8, T), F32),
        big=((NE * HD, T), F32),
        peak=((2, 9, 8, 1024), F32),
        at=((NE * HD, T), BF),
        qx=((4, 128, 1024), BF),
        dox=((4, 128, 1024), BF),
        att=((4, HD + 16, 1024), F32),
        top=((4, 8, 1024), F32),
        linv=((4, 8, 1024), F32),
        kx=((2, 8, 256, 128), BF),
        vx=((2, 8, 256, 128), BF),
        kt=((2, 8, HD, 256), BF),
        vt=((2, 8, HD + 16, 256), BF),
        pst=((2, 9, 256, 1024), BF),
        dkv=((2, 8, 256, 128), F32),
        mixed=((T, D), F32),
        ffn=((T, D), BF),
        ffnt=((D, T), BF),
        acc1=((T, D), F32),
        acc2=((T, D), F32),
        gfh=((2, D, HB), BF),
        gfl=((2, D, HB), BF),
        rf1=((2, D, HB), BF),
        rfa=((D, HB // 2), BF),
        rfb=((D, HB // 4), BF),
        rfc=((dp - 1, shard, HB // 4), BF),
        rga=((shard, HB // 2), BF),
        rgb=((shard, HB // 4), BF),
        rgc=((dp - 1, shard, HB), BF),
        rgs=((shard, HB), BF),
        f2=((2, shard, FF), BF),
        go=((NE * HD, D), BF),
        rq1=((NE * HD // 2, D), BF),
        ro1=((NE * HD // 2, D), BF),
        rq2=((2 * ER, D), BF),
        ro2=((2 * ER, D), BF),
        rq3=((ER, D), BF),
        ro3=((ER, D), BF),
        xq=((dp * pr, D), BF),
        xo=((dp * pr, D), BF),
        rq4=((dp - 1, pr, D), BF),
        ro4=((dp - 1, pr, D), BF),
        fq=((dp * pr, D), BF),
        fo=((dp * pr, D), BF),
        rk1=((4, 2, 256, 128), BF),
        rk2=((3, 2, 256, 128), BF),
        dkvd=((T, 128), BF),
        tb=((128, 640), BF),
        rt1=((64, 640), BF),
        tsm=((64, 640), BF),
        rt2=((3, 16, 640), BF),
        rt3=((dp, 16, 640), BF),
        tf=((128, 640), BF),
        cnt=((32, 128), F32),
        mz=((dp, 32, 128), F32),
        mq=((PL, 32, 128), F32),
        layx=((256, D), BF),
        layr=((256, D), BF),
        tgr=((256, D), BF),
        gain=((8, D), F32),
        i_cot=((T, D), BF),
        i_up=((shard, FF), F32),
        i_down=((FF, shard), F32),
        i_qw=((LE, HD, D), F32),
        i_ow=((LE, HD, D), F32),
        osem=(10,),
        ssem=None,
        rsem=None,
    )


def copies_of(dp):
    return 80 + 16 * dp


def layer_kernel(dp, *refs):
    shard = D // dp
    pr = piece_rows(dp)
    (tok, cot_, routes, wkv, up_, down_, qw_, ow_, rw, gains, gbatch, lens) = refs[:12]
    (lay, tg, msgo, f2o, fqo, foo, sideo, kvo) = refs[12:20]
    names = list(scratch_list(dp))
    s = type("Scratch", (), dict(zip(names, refs[20:])))

    z = lax.axis_index("dp")
    e = lax.axis_index("expert")
    c = e % 2
    qx = e // 2 % 2
    qy = e // 4
    a = (1 - c) * qx + c * qy
    b = (1 - c) * qy + c * qx
    q = 2 * a + b

    def device(a_, b_):
        return (z, 4 * ((1 - c) * b_ + c * a_) + 2 * ((1 - c) * a_ + c * b_) + c)

    qs = [q, 2 * a + 1 - b, 2 * (1 - a) + b, 2 * (1 - a) + 1 - b]
    sib = (z, e + 1 - 2 * c)
    near, far = device(a, 1 - b), device(1 - a, b)
    chips = [None, near, far, device(1 - a, 1 - b)]
    swap = (z, 7 - e)
    zp = [None] + [((z + i) % dp, e) for i in range(1, dp)]
    zfrom = [None] + [(z + dp - i) % dp for i in range(1, dp)]
    slot = c * 4 + q
    plane = [sib] + [(z, (e + i) % PL) for i in range(1, PL)]

    count = [0]
    sends = []

    def rcopy(src, dst, peer):
        k = count[0]
        count[0] += 1
        d = pltpu.make_async_remote_copy(
            src_ref=src,
            dst_ref=dst,
            send_sem=s.ssem.at[k],
            recv_sem=s.rsem.at[k],
            device_id=peer,
            device_id_type=MESH,
        )
        d.start()
        sends.append(d)
        return (k, peer, d)

    def sent(handle):
        sends[:] = [d for d in sends if d is not handle[2]]
        handle[2].wait_send()

    def rwait(handle, dst):
        k, peer, _ = handle
        pltpu.make_async_remote_copy(
            src_ref=dst,
            dst_ref=dst,
            send_sem=s.ssem.at[k],
            recv_sem=s.rsem.at[k],
            device_id=peer,
            device_id_type=MESH,
        ).wait_recv()

    def lcopy(src, dst, k):
        d = pltpu.make_async_copy(src, dst, s.osem.at[k])
        d.start()
        return d

    cot, up, down, qw, ow = s.i_cot, s.i_up, s.i_down, s.i_qw, s.i_ow
    loads = [
        lcopy(x, y, k)
        for k, (x, y) in enumerate(
            ((up_, up), (down_, down), (qw_, qw), (ow_, ow), (cot_, cot))
        )
    ]
    bar = pltpu.get_barrier_semaphore()
    for peer in plane[1:] + zp[1:]:
        pl.semaphore_signal(bar, inc=1, device_id=peer, device_id_type=MESH)

    def zrows(ref, i, n):
        return ref.at[pl.ds(pl.multiple_of(i * n, n), n)]

    def turned(x):
        rows, cols = x.shape
        if cols % 128:
            x = jnp.concatenate([x, jnp.zeros((rows, 128 - cols % 128), x.dtype)], axis=1)
        return x.T[0:cols]

    lo = pl.multiple_of(c * HB, HB)
    hi = pl.multiple_of((1 - c) * HB, HB)
    ri = lax.broadcasted_iota(jnp.int32, (256, 256), 0)
    ci = lax.broadcasted_iota(jnp.int32, (256, 256), 1)
    split = jnp.where(ci == 2 * (ri % 128) + ri // 128, 1.0, 0.0).astype(BF)
    join = jnp.where(ri == 2 * (ci % 128) + ci // 128, 1.0, 0.0).astype(BF)
    own_rows = pl.ds(pl.multiple_of(z * shard, shard), shard)
    s.wkvf[own_rows, :] = wkv[...].astype(BF)
    rtt = routes[...].astype(F32).astype(BF)
    s.rtd[:, 0:256] = mm(rtt[:, 0:256], join).astype(jnp.int32)
    s.rts[...] = mm(rtt[:, 256:512], join).astype(jnp.int32)
    WD = HB // 2
    WP = (HB - WD) // 4
    part = pl.multiple_of(c * HB + WD + q * WP, WP)
    def w2_rows(w, i, at, n):
        return s.w2.at[w, pl.ds(pl.multiple_of(i * shard, shard), shard), pl.ds(at, n)]

    def to_all_z(ref):
        return [None] + [rcopy(ref, ref, zp[i]) for i in range(1, dp)]
    pl.semaphore_wait(bar, PL - 1 + dp - 1)
    h_wkv = [None] + [
        rcopy(zrows(s.wkvf, z, shard), zrows(s.wkvf, z, shard), zp[i]) for i in range(1, dp)
    ]
    h_tok = rcopy(tok.at[pl.ds(256, 256)], s.tokx, swap)
    h_rt = rcopy(s.rts, s.rtx, swap)
    loads[2].wait()
    loads[3].wait()
    for i in range(LE):
        rows = pl.ds(pl.multiple_of(slot * ER + i * HD, HD), HD)
        s.eq[rows, :] = qw[i].astype(BF)
        s.eo[rows, :] = ow[i].astype(BF)
    own_eq = zrows(s.eq, slot, ER)
    own_eo = zrows(s.eo, slot, ER)
    h_eq1 = rcopy(own_eq, own_eq, near)
    loads[0].wait()
    loads[1].wait()
    for at, n in ((lo, WD), (part, WP)):
        s.w2[0, own_rows, pl.ds(at, n)] = up[:, pl.ds(at, n)].astype(BF)
    s.w2[1, own_rows, pl.ds(lo, HB)] = turned(down[pl.ds(lo, HB), :]).astype(BF)

    h_wp1 = to_all_z(w2_rows(0, z, part, WP))
    h_wu = to_all_z(w2_rows(0, z, lo, WD))
    h_wd = to_all_z(w2_rows(1, z, lo, HB))

    def gather_far(h, ref):
        rwait(h, zrows(ref, c * 4 + qs[1], ER))
        pair = zrows(ref, c * 2 + a, 2 * ER)
        return rcopy(pair, pair, far)

    def gather_sib(h, ref):
        rwait(h, zrows(ref, c * 2 + 1 - a, 2 * ER))
        mine = zrows(ref, c, 4 * ER)
        return rcopy(mine, mine, sib)

    def w2_cols(w, at, n):
        return s.w2.at[w, :, pl.ds(at, n)]

    s.wrt[0:NE, :] = rw[...]
    s.wrt[NE:32, :] = jnp.zeros((32 - NE, D), F32)

    g0 = gains[0:1, :]
    g1 = gains[1:2, :]

    def rms(x):
        inv = lax.rsqrt(jnp.mean(x * x, axis=-1, keepdims=True) + NORM_EPS)
        return x * inv, inv

    nat0 = mm(split, tok[0:256, :])
    nat1 = mm(split, tok[256:512, :])
    s.tokd[0:256, :] = nat0.astype(BF)
    n0 = (rms(nat0)[0] * g0).astype(BF)
    n1 = (rms(nat1)[0] * g0).astype(BF)
    s.nd[0:256, :] = n0
    loads[4].wait()
    cot0 = mm(split, cot[0:256, :])
    s.cotd[0:256, :] = cot0.astype(BF)

    for i in range(1, dp):
        rwait(h_wkv[i], zrows(s.wkvf, zfrom[i], shard))
    kv0 = mm(n0, s.wkvf[...]).astype(BF)
    kv1 = mm(n1, s.wkvf[...]).astype(BF)
    for p in range(2):
        s.kvb[slot, p, 0:128, :] = kv0[p * 128 : (p + 1) * 128]
        s.kvb[slot, p, 128:256, :] = kv1[p * 128 : (p + 1) * 128]
    h_kv1 = rcopy(s.kvb.at[slot], s.kvb.at[slot], near)
    h_eq2 = gather_far(h_eq1, s.eq)

    rwait(h_tok, s.tokx)
    rwait(h_rt, s.rtx)
    sw = mm(split, s.tokx[...])
    s.tokd[256:512, :] = sw.astype(BF)
    s.nd[256:512, :] = (rms(sw)[0] * g0).astype(BF)
    s.rtd[:, 256:512] = s.rtx[...]

    wrt = s.wrt[...].astype(BF)
    bm1 = gbatch[z] - 1
    is2 = (4 - gbatch[z]) // 2

    def seq_pos(r):
        return r & bm1, (r >> 1) * is2 + (r >> 2) * (1 - is2)

    def limit_of(index):
        out = jnp.zeros(index.shape, jnp.int32)
        for i in range(4):
            out = jnp.where(index == i, lens[z, i], out)
        return out

    block = [2 * e, 15 - 2 * e]
    lanes128 = lax.broadcasted_iota(jnp.int32, (16, 128), 1)
    row16 = lax.broadcasted_iota(jnp.int32, (16, 128), 0)
    row32 = lax.broadcasted_iota(jnp.int32, (32, 128), 0)

    logits = mm_nt(wrt, s.nd[...])
    row_e = lax.broadcasted_iota(jnp.int32, (32, T), 0)
    chosen = jnp.concatenate(
        [
            jnp.sum(jnp.where(row_e == s.rtd[k : k + 1, :], logits, 0.0), axis=0, keepdims=True)
            for k in range(K8)
        ],
        axis=0,
    )
    ex = jnp.exp(chosen - jnp.max(chosen, axis=0, keepdims=True))
    s.gate[...] = ex / jnp.sum(ex, axis=0, keepdims=True)

    counts = jnp.zeros((32, 128), F32)
    for g in range(4):
        blk, p = g // 2, g % 2
        row = 2 * (block[blk] * 128 + lanes128) + p
        seq, pos = seq_pos(row)
        live = (pos < limit_of(seq))[0:1, :].astype(F32)
        for k in range(K8):
            counts = counts + jnp.where(
                row32 == s.rtd[k : k + 1, g * 128 : (g + 1) * 128], live, 0.0
            )
        feat = jnp.where(seq == row16, 1.0, 0.0).astype(BF)
        s.qx[g, 64:80, :] = jnp.concatenate([feat] * K8, axis=1)
        s.qx[g, 80:128, :] = jnp.zeros((48, 1024), BF)
    s.cnt[...] = jnp.broadcast_to(jnp.sum(counts, axis=1, keepdims=True), (32, 128))

    half = NE * HD // 2
    rwait(h_kv1, s.kvb.at[c * 4 + qs[1]])
    kv_pair = s.kvb.at[pl.ds(c * 4 + a * 2, 2)]
    h_kv2 = rcopy(kv_pair, kv_pair, far)
    h_eqs = gather_sib(h_eq2, s.eq)
    rwait(h_kv2, s.kvb.at[pl.ds(c * 4 + (1 - a) * 2, 2)])
    h_eo1 = rcopy(own_eo, own_eo, near)
    h_kvs = rcopy(s.kvb.at[pl.ds(c * 4, 4)], s.kvb.at[pl.ds(c * 4, 4)], sib)
    rwait(h_eqs, zrows(s.eq, 1 - c, half))

    def query_rows(i, _):
        rows = pl.ds(pl.multiple_of(i * 256, 256), 256)
        s.big[rows, :] = mm_nt(s.eq[rows, :], s.nd[...])
        return 0

    lax.fori_loop(0, NE * HD // 256, query_rows, 0)

    def pick(g, k):
        lanes = pl.ds(pl.multiple_of(g * 128, 128), 128)
        rk = s.rtd[k : k + 1, lanes]
        acc = jnp.zeros((HD, 128), F32)
        for place in range(NE):
            acc = jnp.where(rk == expert_at(place), s.big[place * HD : (place + 1) * HD, lanes], acc)
        return acc

    def choose(g, _):
        for k in range(K8):
            s.qx[g, 0:64, k * 128 : (k + 1) * 128] = (pick(g, k) * (0.125 * LOG2E)).astype(BF)
        return 0

    lax.fori_loop(0, 4, choose, 0)

    rwait(h_kvs, s.kvb.at[pl.ds((1 - c) * 4, 4)])
    krow = lax.broadcasted_iota(jnp.int32, (256, 128), 0)
    klane = lax.broadcasted_iota(jnp.int32, (256, 128), 1)
    for t in range(8):
        for p in range(2):
            kv = s.kvb[slot_of(t), p].astype(F32)
            seq, pos = seq_pos(2 * (t * 256 + krow) + p)
            col = klane - 64
            shown = (seq == col) & (pos < limit_of(col))
            feat = jnp.where(shown | (col > 3), 0.0, MASKED)
            s.kx[p, t] = jnp.where(col < 0, kv, feat).astype(BF)
            s.vx[p, t] = jnp.where(col >= 0, kv, jnp.where(klane < 2, 1.0, 0.0)).astype(BF)
            kvt = kv.T
            s.kt[p, t] = kvt[0:64].astype(BF)
            s.vt[p, t, 0:64, :] = kvt[64:128].astype(BF)
            s.vt[p, t, 64:80, :] = jnp.ones((16, 256), BF)

    turn = e + 1
    below = lax.broadcasted_iota(jnp.int32, (256, 128), 0) - lax.broadcasted_iota(
        jnp.int32, (256, 128), 1
    )
    s.att[...] = jnp.zeros(s.att.shape, F32)
    s.top[...] = jnp.full(s.top.shape, MASKED, F32)

    def place_of(i):
        blk = jnp.where(i >= turn, 1, 0)
        return blk * 2, i - blk * turn

    def attend(i, _):
        g0_, t = place_of(i)
        visible = below <= jnp.where(i == turn - 1, 0, jnp.where(i == 8, 128, 256))
        visible = jnp.concatenate([visible] * K8, axis=1)
        both_p = range(2)
        scs = [jnp.where(visible, mm(s.kx[p, t], s.qx[g0_ + p]), MASKED) for p in both_p]
        tops = [jnp.max(jnp.max(x.reshape(32, 8, 1024), axis=0), axis=0, keepdims=True) for x in scs]
        olds = [s.top[g0_ + p, 0:1, :] for p in both_p]
        news = [jnp.maximum(old, jnp.ceil(x)) for old, x in zip(olds, tops)]
        pbs = [jnp.exp2(sc - new).astype(BF) for sc, new in zip(scs, news)]
        outs = [mm(s.vt[p, t], pbs[p]) for p in both_p]
        for p in both_p:
            s.att[g0_ + p] = s.att[g0_ + p] * jnp.exp2(olds[p] - news[p]) + outs[p]
            s.pst[p, i] = pbs[p]
            s.peak[p, i] = jnp.broadcast_to(news[p], (8, 1024))
            s.top[g0_ + p] = jnp.broadcast_to(news[p], (8, 1024))
        return 0

    h_eo2 = gather_far(h_eo1, s.eo)
    lax.fori_loop(0, 3, attend, 0)
    for i in range(1, dp):
        rwait(h_wp1[i], w2_rows(0, zfrom[i], part, WP))
    h_wp2 = rcopy(w2_cols(0, part, WP), w2_cols(0, part, WP), near)
    h_cot = rcopy(cot.at[pl.ds(256, 256)], s.cotx, swap)
    lax.fori_loop(3, 5, attend, 0)
    rwait(h_wp2, w2_cols(0, c * HB + WD + qs[1] * WP, WP))
    both_parts = pl.multiple_of(c * HB + WD + a * 2 * WP, 2 * WP)
    h_wp3 = rcopy(w2_cols(0, both_parts, 2 * WP), w2_cols(0, both_parts, 2 * WP), far)
    lax.fori_loop(5, 7, attend, 0)
    h_eos = gather_sib(h_eo2, s.eo)
    lax.fori_loop(7, 9, attend, 0)
    for g in range(4):
        inv = 1.0 / s.att[g, 64:72, :]
        s.linv[g] = inv
        s.att[g, 0:64, :] = s.att[g, 0:64, :] * inv[0:1]
    rwait(h_wp3, w2_cols(0, pl.multiple_of(c * HB + WD + (1 - a) * 2 * WP, 2 * WP), 2 * WP))
    for i in range(1, dp):
        rwait(h_wu[i], w2_rows(0, zfrom[i], lo, WD))
    h_w2s = [rcopy(w2_cols(0, lo, HB), w2_cols(0, lo, HB), sib)]
    def spread(dst, src, scale):
        def one(g, _):
            lanes = pl.ds(pl.multiple_of(g * 128, 128), 128)
            for k in range(K8):
                part = src[g, 0:HD, k * 128 : (k + 1) * 128]
                if scale is not None:
                    part = part * scale[k : k + 1, lanes]
                else:
                    part = part * 0.125
                s.acc1[k * HD : (k + 1) * HD, 0:128] = part
            for place in range(NE):
                acc = jnp.zeros((HD, 128), F32)
                for k in range(K8):
                    acc = jnp.where(
                        s.rtd[k : k + 1, lanes] == expert_at(place),
                        s.acc1[k * HD : (k + 1) * HD, 0:128],
                        acc,
                    )
                dst[place * HD : (place + 1) * HD, lanes] = acc.astype(BF)
            return 0

        lax.fori_loop(0, 4, one, 0)

    spread(s.at, s.att, s.gate)
    rwait(h_eos, zrows(s.eo, 1 - c, half))
    s.acc1[...] = s.tokd[...].astype(F32)

    def mix(i, _):
        rows = pl.ds(pl.multiple_of(i * 256, 256), 256)
        s.acc1[...] += mm_tn(s.at[rows, :], s.eo[rows, :])
        return 0

    lax.fori_loop(0, NE * HD // 256, mix, 0)
    for i in range(1, dp):
        rwait(h_wd[i], w2_rows(1, zfrom[i], lo, HB))
    h_w2s.append(rcopy(w2_cols(1, lo, HB), w2_cols(1, lo, HB), sib))
    mixed = s.acc1[...]
    s.mixed[...] = mixed
    ffn = rms(mixed)[0] * g1
    s.ffn[...] = ffn.astype(BF)
    s.ffnt[...] = ffn.T.astype(BF)
    rwait(h_cot, s.cotx)
    cot1 = mm(split, s.cotx[...])
    s.cotd[256:512, :] = cot1.astype(BF)
    s.cott[:, 0:256] = cot0.T.astype(BF)
    s.cott[:, 256:512] = cot1.T.astype(BF)
    s.acc2[...] = jnp.zeros((T, D), F32)
    for w in range(2):
        rwait(h_w2s[w], w2_cols(w, hi, HB))

    FT = 256

    def feed(i, base_, at, keep):
        cols = pl.ds(pl.multiple_of(base_ + at + i * FT, FT), FT)
        part_cols = pl.ds(pl.multiple_of(at + i * FT, FT), FT)
        up = mm(s.ffn[...], s.w2[0, :, cols])
        sq = up * up
        th = jnp.tanh(0.79788456 * up * (1.0 + 0.044715 * sq))
        hid = (0.5 * up * (1.0 + th)).astype(BF)
        slope = 0.5 * (1.0 + th) + 0.5 * up * (1.0 - th * th) * (
            0.79788456 * (1.0 + 3 * 0.044715 * sq)
        )
        s.acc1[...] += mm_nt(hid, s.w2[1, :, cols])
        dup = (mm(s.cotd[...], s.w2[1, :, cols]) * slope).astype(BF)
        keep[0, :, part_cols] = mm(s.ffnt[...], dup).astype(BF)
        keep[1, :, part_cols] = mm(s.cott[...], hid).astype(BF)
        s.acc2[...] += mm_nt(dup, s.w2[0, :, cols])
        return 0

    def both(x, y):
        return (x.astype(F32) + y.astype(F32)).astype(BF)

    def fold(sq):
        sq = jnp.sum(sq, axis=0, keepdims=True)
        out = sq[:, 0:128]
        for j in range(1, sq.shape[1] // 128):
            out = out + sq[:, j * 128 : (j + 1) * 128]
        return out

    done, squares = [], []
    quart = HB // 4
    keep2 = pl.multiple_of(a * 2 * quart, 2 * quart)
    give2 = pl.multiple_of((1 - a) * 2 * quart, 2 * quart)
    keep1 = pl.multiple_of(q * quart, quart)
    give1 = pl.multiple_of(qs[1] * quart, quart)
    place1 = pl.multiple_of(c * HB + keep1, quart)

    def feed_grad(w):
        own, total, one, two, three = s.gfl.at[w], s.rf1.at[w], s.rfa, s.rfb, s.rfc

        def pair(j, at):
            cols = pl.ds(at, 2 * quart)
            rwait(h_f1[j][w], total.at[:, cols])
            total[:, cols] = both(own[:, cols], total[:, cols])

        pair(0, give2)
        h = rcopy(total.at[:, pl.ds(give2, 2 * quart)], one, far)
        yield
        pair(1, keep2)
        yield
        rwait(h, one)
        for at in (give1, keep1):
            inner = pl.multiple_of(at - keep2, quart)
            total[:, pl.ds(at, quart)] = both(
                total[:, pl.ds(at, quart)], one[:, pl.ds(inner, quart)]
            )
            if at is give1:
                h = rcopy(total.at[:, pl.ds(give1, quart)], two, near)
        yield
        rwait(h, two)
        total[:, pl.ds(keep1, quart)] = both(total[:, pl.ds(keep1, quart)], two[...])

        def zpart(i):
            return total.at[pl.ds(pl.multiple_of(i * shard, shard), shard), pl.ds(keep1, quart)]

        hz = [rcopy(zpart(zp[i][0]), three.at[i - 1], zp[i]) for i in range(1, dp)]
        yield
        acc = zpart(z)[...].astype(F32)
        for i in range(1, dp):
            rwait(hz[i - 1], three.at[i - 1])
            acc = acc + three[i - 1].astype(F32)
        yield from spread_grad(w, acc)

    def spread_grad(w, acc):
        out = s.f2.at[w]
        acc = acc.astype(BF)
        out[:, pl.ds(place1, quart)] = acc
        acc = acc.astype(F32)
        squares.append(fold(acc * acc))
        h = rcopy(out.at[:, pl.ds(place1, quart)], out.at[:, pl.ds(place1, quart)], near)
        yield
        rwait(h, out.at[:, pl.ds(pl.multiple_of(c * HB + give1, quart), quart)])
        wide = out.at[:, pl.ds(pl.multiple_of(c * HB + keep2, 2 * quart), 2 * quart)]
        h = rcopy(wide, wide, far)
        yield
        rwait(h, out.at[:, pl.ds(pl.multiple_of(c * HB + give2, 2 * quart), 2 * quart)])
        h = rcopy(out.at[:, pl.ds(lo, HB)], out.at[:, pl.ds(lo, HB)], sib)
        yield
        rwait(h, out.at[:, pl.ds(hi, HB)])
        done.append(lcopy(out, f2o.at[w], 2 + w))
        yield

    def dp_first_grad(w):
        own, total, one, two, three = s.gfl.at[w], s.rf1.at[w], s.rga, s.rgb, s.rgc
        hz = []
        for j, at in ((0, give2), (1, keep2)):
            cols = pl.ds(at, 2 * quart)
            rwait(h_f1[j][w], total.at[:, cols])
            total[:, cols] = both(own[:, cols], total[:, cols])
            for i in range(1, dp):
                mine = pl.ds(pl.multiple_of(zp[i][0] * shard, shard), shard)
                hz.append((rcopy(total.at[mine, cols], three.at[i - 1, :, cols], zp[i]), i, cols))
            yield
        for h, i, cols in hz:
            rwait(h, three.at[i - 1, :, cols])
        acc = total[own_rows, :].astype(F32)
        for i in range(1, dp):
            acc = acc + three[i - 1].astype(F32)
        s.rgs[...] = acc.astype(BF)
        h = rcopy(s.rgs.at[:, pl.ds(give2, 2 * quart)], one, far)
        yield
        rwait(h, one)
        s.rgs[:, pl.ds(keep2, 2 * quart)] = both(s.rgs[:, pl.ds(keep2, 2 * quart)], one[...])
        h = rcopy(s.rgs.at[:, pl.ds(give1, quart)], two, near)
        yield
        rwait(h, two)
        acc = s.rgs[:, pl.ds(keep1, quart)].astype(F32) + two[...].astype(F32)
        yield from spread_grad(w, acc)

    def head_grad(src, total, one, two, full, part_, final, dst, sem):
        h = rcopy(zrows(src, 1 - c, half), total, sib)
        s.half_sent = h
        yield
        rwait(h, total)

        def pair(which):
            rows = pl.ds(pl.multiple_of(which * 2 * ER, 128), 2 * ER)
            wide = pl.ds(pl.multiple_of(c * half + which * 2 * ER, 128), 2 * ER)
            total[rows, :] = both(src[wide, :], total[rows, :])

        pair(1 - a)
        h = rcopy(zrows(total, 1 - a, 2 * ER), one, far)
        pair(a)
        yield
        rwait(h, one)
        for which in (1 - b, b):
            rows = pl.ds(pl.multiple_of((2 * a + which) * ER, ER), ER)
            total[rows, :] = both(total[rows, :], one[pl.ds(pl.multiple_of(which * ER, ER), ER), :])
            if which is not b:
                h = rcopy(zrows(total, qs[1], ER), two, near)
        yield
        rwait(h, two)
        full[0:ER, :] = both(total[pl.ds(pl.multiple_of(q * ER, ER), ER), :], two[...])
        if dp * pr > ER:
            full[ER:, :] = jnp.zeros((dp * pr - ER, full.shape[1]), BF)
        hz = [rcopy(zrows(full, zp[i][0], pr), part_.at[i - 1], zp[i]) for i in range(1, dp)]
        yield
        mine = pl.ds(pl.multiple_of(z * pr, pr), pr)
        acc = full[mine, :].astype(F32)
        for i in range(1, dp):
            rwait(hz[i - 1], part_.at[i - 1])
            acc = acc + part_[i - 1].astype(F32)
        acc = acc.astype(BF)
        final[mine, :] = acc
        acc = acc.astype(F32)
        squares.append(fold(acc * acc))
        hz = to_all_z(zrows(final, z, pr))
        yield
        for i in range(1, dp):
            rwait(hz[i], zrows(final, zfrom[i], pr))
        done.append(lcopy(final.at[pl.ds(0, ER)], dst, sem))
        yield

    def feed_tiles(base_, at, keep):
        lax.fori_loop(0, HB // FT // 2, lambda i, _: feed(i, base_, at, keep), 0)

    def to_sibling(at):
        cols = pl.ds(at, 2 * quart)
        return [rcopy(s.gfh.at[w, :, cols], s.rf1.at[w, :, cols], sib) for w in range(2)]

    sib_give2 = pl.multiple_of((1 - b) * 2 * quart, 2 * quart)
    sib_keep2 = pl.multiple_of(b * 2 * quart, 2 * quart)
    feed_tiles(hi, sib_give2, s.gfh)
    h_f1 = [to_sibling(sib_give2)]
    feed_tiles(lo, give2, s.gfl)
    chain = [feed_grad(0), dp_first_grad(1)]
    next(chain[0])
    next(chain[1])
    feed_tiles(hi, sib_keep2, s.gfh)
    h_f1.append(to_sibling(sib_keep2))
    feed_tiles(lo, keep2, s.gfl)
    next(chain[0])
    next(chain[1])

    out = s.acc1[...].astype(BF)
    s.layx[...] = mm(join, out[256:512]).astype(BF)
    s.ffn[0:256, :] = mm(join, out[0:256]).astype(BF)

    def rms_back(dn, gain, unit, inv):
        a = dn * gain
        return inv * (a - unit * jnp.mean(a * unit, axis=-1, keepdims=True)), jnp.sum(
            dn * unit, axis=0, keepdims=True
        )

    unit1, inv1 = rms(s.mixed[...])
    back, gain1 = rms_back(s.acc2[...], g1, unit1, inv1)
    s.gain[1:2, :] = gain1
    dmix = s.cotd[...].astype(F32) + back
    s.mixed[...] = dmix
    s.cott[...] = dmix.astype(BF)

    def out_rows(i, _):
        rows = pl.ds(pl.multiple_of(i * 256, 256), 256)
        s.big[rows, :] = mm_nt(s.eo[rows, :], s.cott[...])
        s.go[rows, :] = mm(s.at[rows, :], s.cott[...]).astype(BF)
        return 0

    lax.fori_loop(0, NE * HD // 256, out_rows, 0)
    chain.append(head_grad(s.go, s.ro1, s.ro2, s.ro3, s.xo, s.ro4, s.fo, foo, 4))
    next(chain[2])
    sent_o = s.half_sent

    def heads_back(g, _):
        lanes = pl.ds(pl.multiple_of(g * 128, 128), 128)
        for k in range(K8):
            ks = slice(k * 128, (k + 1) * 128)
            da = pick(g, k)
            at = s.att[g, 0:HD, ks]
            s.dgate[k : k + 1, lanes] = jnp.sum(at * da, axis=0, keepdims=True)
            do = (da * (s.gate[k : k + 1, lanes] * s.linv[g, 0:1, ks])).astype(BF)
            s.dox[g, 64:128, ks] = do
            delta = -jnp.sum(do.astype(F32) * at, axis=0, keepdims=True)
            top = delta.astype(BF).astype(F32)
            s.dox[g, 0:16, ks] = jnp.where(
                row16 == 0, top, jnp.where(row16 == 1, delta - top, 0.0)
            ).astype(BF)
            s.dox[g, 16:64, ks] = jnp.zeros((48, 128), BF)
        return 0

    lax.fori_loop(0, 4, heads_back, 0)
    s.dkv[...] = jnp.zeros(s.dkv.shape, F32)

    left = lax.broadcasted_iota(jnp.int32, (256, 128), 1) < 64

    s.att[...] = jnp.zeros(s.att.shape, F32)

    def attend_back(i, _):
        g0_, t = place_of(i)
        both_p = range(2)
        scales = [jnp.exp2(s.peak[p, i, 0:1, :] - s.top[g0_ + p, 0:1, :]) for p in both_p]
        doxs = [(s.dox[g0_ + p].astype(F32) * scales[p]).astype(BF) for p in both_p]
        dprobs = [mm(s.vx[p, t], doxs[p]) for p in both_p]
        vparts = [mm_nt(s.pst[p, i], doxs[p]) for p in both_p]
        dss = [(s.pst[p, i].astype(F32) * dprobs[p]).astype(BF) for p in both_p]
        kparts = [mm_nt(dss[p], s.qx[g0_ + p]) for p in both_p]
        dqs = [mm(s.kt[p, t], dss[p]) for p in both_p]
        for p in both_p:
            s.dkv[p, t] += jnp.where(left, kparts[p] * LN2, vparts[p])
            s.att[g0_ + p, 0:HD, :] += dqs[p]
        return 0

    next(chain[2])
    lax.fori_loop(0, 3, attend_back, 0)
    next(chain[0])
    lax.fori_loop(3, 5, attend_back, 0)
    next(chain[2])
    lax.fori_loop(5, 7, attend_back, 0)
    next(chain[0])
    lax.fori_loop(7, 9, attend_back, 0)
    next(chain[2])
    h_lay = rcopy(s.layx, s.layr, swap)
    for h in (h_kv1, h_kv2, h_kvs):
        sent(h)
    for dev in range(PL):
        sl = slot_of(dev)
        for side_, blk in enumerate((2 * dev, 15 - 2 * dev)):
            for p in range(2):
                s.kvb[sl, side_, p * 128 : (p + 1) * 128, :] = s.dkv[p, blk // 2, (blk % 2) * 128 : (blk % 2) * 128 + 128, :].astype(BF)
    h_k1 = rcopy(s.kvb.at[pl.ds((1 - c) * 4, 4)], s.rk1, sib)
    spread(s.at, s.att, None)
    sent(sent_o)

    def query_grad(i, cols):
        rows = pl.ds(pl.multiple_of(i * 256, 256), 256)
        s.go[rows, cols] = mm(s.at[rows, :], s.nd[:, cols]).astype(BF)
        return 0

    for j in range(2):
        cols = pl.ds(j * 256, 256)
        lax.fori_loop(0, NE * HD // 256, lambda i, _: query_grad(i, cols), 0)
        chain.append(
            head_grad(
                *[x.at[:, cols] for x in (s.go, s.rq1, s.rq2, s.rq3, s.xq)],
                s.rq4.at[:, :, cols], s.fq.at[:, cols], fqo.at[:, cols], 5 + 4 * j,
            )
        )
        next(chain[3 + j])
        if j == 0:
            rwait(h_k1, s.rk1)
            for i in range(4):
                s.rk1[i] = both(s.kvb[c * 4 + i], s.rk1[i])
            h_k2 = [None] + [
                rcopy(s.rk1.at[qs[m]], s.rk2.at[m - 1], chips[m]) for m in (1, 2, 3)
            ]
    s.acc2[...] = jnp.zeros((T, D), F32)

    def slot_sum(i, _):
        rows = pl.ds(pl.multiple_of(i * 256, 256), 256)
        s.acc2[...] += mm_tn(s.at[rows, :], s.eq[rows, :])
        return 0

    lax.fori_loop(0, NE * HD // 256, slot_sum, 0)
    gate = s.gate[...]
    dch = gate * (s.dgate[...] - jnp.sum(gate * s.dgate[...], axis=0, keepdims=True))
    dlog = jnp.zeros((32, T), F32)
    for k in range(K8):
        dlog = dlog + jnp.where(row_e == s.rtd[k : k + 1, :], dch[k : k + 1, :], 0.0)
    dlog = dlog.astype(BF)
    s.acc2[...] += mm_tn(dlog, wrt)
    grt = mm(dlog, s.nd[...])

    next(chain[3])
    next(chain[4])
    next(chain[1])
    next(chain[0])
    for m in (1, 2, 3):
        rwait(h_k2[m], s.rk2.at[m - 1])
    for i in range(2):
        total = s.rk1[q, i].astype(F32)
        for m in (1, 2, 3):
            total = total + s.rk2[m - 1, i].astype(F32)
        s.dkvd[i * 256 : (i + 1) * 256, :] = total.astype(BF)
    dn = s.acc2[...] + mm_nt(s.dkvd[...], s.wkvf[...])
    unit0, inv0 = rms(s.tokd[...].astype(F32))
    back0, gain0 = rms_back(dn, g0, unit0, inv0)
    s.tb[:, 0:512] = mm_tn(s.dkvd[...], s.nd[...]).astype(BF)
    side = s.acc1.at[pl.ds(0, 128), pl.ds(0, 128)]
    for j in range(4):
        js = slice(j * 128, (j + 1) * 128)
        side[j * 24 : (j + 1) * 24, :] = grt[0:24, js]
        side[96 + j : 97 + j, :] = gain0[:, js]
        side[100 + j : 101 + j, :] = s.gain[1:2, js]
    side[104:128, :] = jnp.zeros((24, 128), F32)
    s.tb[:, 512:640] = side[...].astype(BF)
    h_t1 = rcopy(zrows(s.tb, 1 - c, 64), s.rt1, sib)
    next(chain[1])
    next(chain[0])
    next(chain[2])
    next(chain[3])
    next(chain[4])
    rwait(h_t1, s.rt1)
    s.tsm[...] = both(s.tb[pl.ds(pl.multiple_of(c * 64, 64), 64), :], s.rt1[...])
    h_t2 = [None] + [rcopy(zrows(s.tsm, qs[m], 16), s.rt2.at[m - 1], chips[m]) for m in (1, 2, 3)]
    grad = s.mixed[...] + back0
    sent(h_lay)
    s.layx[...] = mm(join, grad[256:512].astype(BF)).astype(BF)
    top = grad[0:256].astype(BF)
    rest = (grad[0:256] - top.astype(F32)).astype(BF)
    s.acc1[0:256, :] = mm(join, top) + mm(join, rest)
    next(chain[1])
    next(chain[3])
    next(chain[4])
    next(chain[0])
    for m in (1, 2, 3):
        rwait(h_t2[m], s.rt2.at[m - 1])
    total = s.tsm[pl.ds(pl.multiple_of(q * 16, 16), 16), :].astype(F32)
    for m in (1, 2, 3):
        total = total + s.rt2[m - 1].astype(F32)
    s.rt3[z] = total.astype(BF)
    h_t3 = [None] + [rcopy(s.rt3.at[z], s.rt3.at[z], zp[i]) for i in range(1, dp)]
    h_tg = rcopy(s.layx, s.tgr, swap)
    next(chain[1])
    for i in range(1, dp):
        rwait(h_t3[i], s.rt3.at[zfrom[i]])
    total = s.rt3[0].astype(F32)
    for i in range(1, dp):
        total = total + s.rt3[i].astype(F32)
    tail = total.astype(BF)
    s.tf[pl.ds(pl.multiple_of(slot * 16, 16), 16), :] = tail
    h_t4 = [None] + [
        rcopy(zrows(s.tf, slot, 16), zrows(s.tf, slot, 16), chips[m]) for m in (1, 2, 3)
    ]
    next(chain[3])
    next(chain[4])
    sq_t = fold(tail.astype(F32) * tail.astype(F32)) * (1.0 / dp)

    total = squares[0]
    for sq in squares[1:] + [sq_t]:
        total = total + sq
    squares = jnp.sum(total, axis=1, keepdims=True)
    s.mz[z] = jnp.where(row32 < 24, s.cnt[...], jnp.where(row32 == 24, squares, 0.0))
    h_m1 = [None] + [rcopy(s.mz.at[z], s.mz.at[z], zp[i]) for i in range(1, dp)]

    for m in (1, 2, 3):
        rwait(h_t4[m], zrows(s.tf, c * 4 + qs[m], 16))
    next(chain[1])
    h_t5 = rcopy(zrows(s.tf, c, 64), zrows(s.tf, c, 64), sib)

    for i in range(1, dp):
        rwait(h_m1[i], s.mz.at[zfrom[i]])
    total = s.mz[0]
    for i in range(1, dp):
        total = total + s.mz[i]
    s.mq[e] = total
    h_m2 = [None] + [rcopy(s.mq.at[e], s.mq.at[e], plane[i]) for i in range(1, PL)]

    rwait(h_lay, s.layr)
    s.ffn[256:512, :] = s.layr[...]
    done.append(lcopy(s.ffn, lay, 0))
    rwait(h_tg, s.tgr)
    s.acc1[256:512, :] = s.tgr[...].astype(F32)
    done.append(lcopy(s.acc1, tg, 1))
    next(chain[0])
    next(chain[1])
    rwait(h_t5, zrows(s.tf, 1 - c, 64))
    s.acc2[:, 0:128] = s.tf[:, 0:512].astype(F32).T
    done.append(lcopy(s.tf.at[:, pl.ds(512, 128)], sideo, 8))
    done.append(lcopy(s.acc2.at[own_rows, pl.ds(0, 128)], kvo, 7))
    next(chain[2])
    next(chain[3])
    next(chain[4])
    for i in range(1, PL):
        rwait(h_m2[i], s.mq.at[(e + PL - i) % PL])
    total = s.mq[0]
    for i in range(1, PL):
        total = total + s.mq[i]
    s.cnt[...] = total
    done.append(lcopy(s.cnt, msgo, 6))
    for d in done:
        d.wait()
    for d in sends:
        d.wait_send()
    assert count[0] <= copies_of(dp)


def adam_kernel(steps, *refs):
    (lay, tg, msg, upg, downg, qg, og, side, kvg) = refs[:9]
    params = [refs[9 + 3 * i : 12 + 3 * i] for i in range(7)]
    layo, tgo, counts, norm = refs[30:34]
    outs = [refs[34 + 3 * i : 37 + 3 * i] for i in range(7)]
    step = pl.program_id(0)
    total = jnp.sqrt(jnp.full((8, 128), msg[24, 0], F32))
    clip = (CLIP_LIMIT / jnp.maximum(total, CLIP_LIMIT))[0:1, 0:1]

    def update(k, g, rate, decay, at=Ellipsis):
        w, m, v = [r[at] for r in params[k]]
        g = g * clip
        m = BETA_FIRST * m + (1.0 - BETA_FIRST) * g
        v = BETA_SECOND * v + (1.0 - BETA_SECOND) * g * g
        mh = m * (1.0 / (1.0 - BETA_FIRST**ADAM_STEP))
        vh = v * (1.0 / (1.0 - BETA_SECOND**ADAM_STEP))
        outs[k][0][at] = w - rate * (mh / (jnp.sqrt(vh) + ADAM_EPS) + decay * w)
        outs[k][1][at] = m
        outs[k][2][at] = v

    @pl.when(step == 0)
    def _():
        norm[...] = total[0:1, 0:1]
        for i in range(NE):
            counts[i] = msg[i, 0].astype(jnp.int32)
        sd = side[...].astype(F32)
        for row in range(2):
            g = jnp.concatenate([sd[96 + 4 * row + j : 97 + 4 * row + j] for j in range(4)], axis=1)
            update(0, g, 0.7, 0.0, pl.ds(row, 1))
        g = jnp.concatenate([sd[j * NE : (j + 1) * NE] for j in range(4)], axis=1)
        update(1, g, 0.03, 0.1)

    layo[...] = lay[...]
    tgo[...] = tg[...]
    update(2, kvg[...], 0.06, 0.1)
    update(3, qg[...].astype(F32), 0.06, 0.1)
    update(4, og[...].astype(F32), 2.0, 0.1)
    update(5, upg[0].astype(F32), 0.06, 0.1)
    update(6, downg[0].astype(F32).T, 0.03, 0.1)


def on_device(tokens, cotangent, routes, group_batch, seq_lengths, *state):
    dp = lax.axis_size("dp")
    shard = D // dp
    state = list(state)
    for i in range(3):
        state[3 + i] = state[3 + i].T
        state[9 + i] = state[9 + i].transpose(0, 2, 1)
    gains, router, keyval, query, output, up, down = [state[3 * i] for i in range(7)]

    scr = []
    for item in scratch_list(dp).values():
        if item is None:
            scr.append(pltpu.SemaphoreType.DMA((copies_of(dp),)))
        elif len(item) == 1:
            scr.append(pltpu.SemaphoreType.DMA(item))
        else:
            scr.append(pltpu.VMEM(item[0], item[1]))
    routes_cols = routes.T
    vm = pl.BlockSpec(memory_space=pltpu.VMEM)
    sm = pl.BlockSpec(memory_space=pltpu.SMEM)
    hbm = pl.BlockSpec(memory_space=pl.ANY)
    outs = [
        jax.ShapeDtypeStruct((T, D), BF),
        jax.ShapeDtypeStruct((T, D), F32),
        jax.ShapeDtypeStruct((32, 128), F32),
        jax.ShapeDtypeStruct((2, shard, FF), BF),
        jax.ShapeDtypeStruct((ER, D), BF),
        jax.ShapeDtypeStruct((ER, D), BF),
        jax.ShapeDtypeStruct((128, 128), BF),
        jax.ShapeDtypeStruct((shard, 128), F32),
    ]

    def kernel(*refs):
        layer_kernel(dp, *refs)

    lay, tg, msg, f2, fq, fo, side, kvg = pl.pallas_call(
        kernel,
        out_shape=outs,
        in_specs=[vm, hbm, vm, vm, hbm, hbm, hbm, hbm, vm, vm, sm, sm],
        out_specs=[hbm] * len(outs),
        scratch_shapes=scr,
        compiler_params=pltpu.CompilerParams(
            collective_id=0, has_side_effects=True, vmem_limit_bytes=64 * 2**20 - 2**17
        ),
        name="layer",
    )(
        tokens, cotangent, routes_cols, keyval, up, down, query, output, router, gains,
        group_batch, seq_lengths,
    )

    steps = 2
    rows = lambda i: (i, 0)
    middle = lambda i: (0, i, 0)
    blocks = [
        pl.BlockSpec((2, D), lambda i: (0, 0)),
        pl.BlockSpec((NE, D), lambda i: (0, 0)),
        pl.BlockSpec((shard // steps, 2 * HD), rows),
        pl.BlockSpec((LE, HD // steps, D), middle),
        pl.BlockSpec((LE, HD // steps, D), middle),
        pl.BlockSpec((shard // steps, FF), rows),
        pl.BlockSpec((FF // steps, shard), rows),
    ]
    each = [b for b in blocks for _ in range(3)]

    def update(*refs):
        adam_kernel(steps, *refs)

    result = list(pl.pallas_call(
        update,
        grid=(steps,),
        out_shape=[
            jax.ShapeDtypeStruct((T, D), BF),
            jax.ShapeDtypeStruct((T, D), F32),
            jax.ShapeDtypeStruct((NE,), jnp.int32),
            jax.ShapeDtypeStruct((1, 1), F32),
        ]
        + [jax.ShapeDtypeStruct(x.shape, F32) for x in state],
        in_specs=[
            pl.BlockSpec((T // steps, D), rows),
            pl.BlockSpec((T // steps, D), rows),
            sm,
            pl.BlockSpec((1, shard // steps, FF), middle),
            pl.BlockSpec((1, shard, FF // steps), lambda i: (1, 0, i)),
            pl.BlockSpec((LE, HD // steps, D), middle),
            pl.BlockSpec((LE, HD // steps, D), middle),
            pl.BlockSpec((128, 128), lambda i: (0, 0)),
            pl.BlockSpec((shard // steps, 2 * HD), rows),
        ]
        + each,
        out_specs=[pl.BlockSpec((T // steps, D), rows), pl.BlockSpec((T // steps, D), rows), sm, pl.BlockSpec((1, 1), lambda i: (0, 0))] + each,
        compiler_params=pltpu.CompilerParams(vmem_limit_bytes=63 * 2**20),
        name="adamw",
    )(lay, tg, msg, f2, f2, fq.reshape(LE, HD, D), fo.reshape(LE, HD, D), side, kvg, *state))
    result[3] = result[3].reshape(())
    for i in range(3):
        result[7 + i] = result[7 + i].T
        result[13 + i] = result[13 + i].transpose(0, 2, 1)
    return tuple(result)


def solution(mesh):
    tok = P(("dp", "expert"), None)
    dp0 = P("dp", None)
    ex0 = P("expert", None, None)
    dp1 = P(None, "dp")
    return jax.shard_map(
        on_device,
        mesh=mesh,
        in_specs=(tok,) * 3 + (P(),) * 8 + (dp0,) * 3 + (ex0,) * 6 + (dp0,) * 3 + (dp1,) * 3,
        out_specs=(tok,) * 2 + (P(),) * 8 + (dp0,) * 3 + (ex0,) * 6 + (dp0,) * 3 + (dp1,) * 3,
        check_vma=False,
    )
```
